128 devices in a mesh: slab: 32 (over x, y, core), wsh: 4 (over z).
Axes of the slice: x: 4, y: 4, z: 4, core: 2. Of those that a mesh axis runs over, the one named last changes fastest.
Arguments:
- node_feat: bfloat16 [524288, 128], P(('slab', 'wsh')), may hold values from -6 to 6
- cotangent: bfloat16 [524288, 128], P(('slab', 'wsh')), may hold values from -6 to 6
- w_msg: bfloat16 [128, 128], P('wsh'), may hold values from -0.5 to 0.5
- w_in: bfloat16 [256, 128], P('wsh'), may hold values from -0.375 to 0.375
- w_out: bfloat16 [128, 128], P('wsh'), may hold values from -0.5 to 0.5
- ln_gain: bfloat16 [128], P('wsh'), may hold values from 0.25 to 1.75
- tile_values: bfloat16 [16384, 4, 128], P(('slab', 'wsh')), may hold values from -2 to 2
- tile_cols: int32 [16384, 4, 128], P(('slab', 'wsh')), may hold values from 0 to 127
- tile_dst: int32 [16384], P(('slab', 'wsh')), may hold values from 0 to 31
- tile_src: int32 [16384], P(('slab', 'wsh')), may hold values from 0 to 191
- tile_count: int32 [128], P(('slab', 'wsh')), may hold values from 16 to 128, as said below
- halo_rows: int32 [128, 2, 1024], P(('slab', 'wsh')), may hold values from 0 to 4095, as said below
- halo_count: int32 [128, 2], P(('slab', 'wsh')), may hold values from 512 to 1024, as said below
Outputs:
- node_out: bfloat16 [524288, 128], P(('slab', 'wsh'))
- d_node: bfloat16 [524288, 128], P(('slab', 'wsh'))
- d_w_msg: float32 [128, 128], P('wsh')
- d_w_in: float32 [256, 128], P('wsh')
- d_w_out: float32 [128, 128], P('wsh')
- d_gain: float32 [128], P('wsh')
The draws below stay inside these ranges and needn't reach their ends.
Inputs may be any that keep to these rules, and one draw needn't show every extreme that they name: In every slab one device uses all 128 slots; the used slots are the first tile_count ones. `halo_rows`: each list holds distinct rows of the sending device. `halo_count`: some device uses all 1024 slots of both lists.
All inputs are finite; a program needn't handle non-finite values.
Results may differ from the reference program's by a relative error of at most 0.019.
Values may be sent and summed in bfloat16 or wider, within the bound.
No kernel may reach another device: no remote copies, remote signals or barrier semaphores. Data moves between devices by JAX's collectives and lax.ppermute only.
A program may use at most 128 MiB of HBM per device.

```python
import jax
import jax.numpy as jnp
from jax import lax

D = 128
BLOCK = 128
EDGE_ROW = 4
NODE_DEV = 4096
HALO = 1024
NBLK = 32
TILES = 128
SRC_BLOCKS = 192
NODES = 524288
N_SLAB = 32
N_WSH = 4


def draw_tile_count(key, part):
    key = jax.random.fold_in(key, 11)
    first_key, second_key = jax.random.split(key)
    busiest = jax.random.randint(first_key, (N_SLAB, 1), 0, N_WSH)
    lighter = jax.random.randint(second_key, (N_SLAB, N_WSH), TILES // 8, TILES // 2 + 1)
    counts = jnp.where(jnp.arange(N_WSH)[None, :] == busiest, TILES, lighter)
    return counts.reshape(N_SLAB * N_WSH).astype(jnp.int32)


def draw_halo_rows(key, part):
    key = jax.random.fold_in(key, 12)
    key_list = jax.random.split(key, N_SLAB * N_WSH * 2)
    picked = jax.vmap(lambda single: jax.random.permutation(single, 2 * HALO - 1)[:HALO - 1] + 1)(key_list)
    listed = jnp.concatenate([jnp.zeros((N_SLAB * N_WSH * 2, 1), jnp.int32), picked.astype(jnp.int32)], axis=1)
    listed = listed.reshape(N_SLAB * N_WSH, 2, HALO)
    direction = jnp.arange(2).reshape(1, 2, 1)
    return jnp.where(direction == 0, listed, NODE_DEV - 1 - listed).astype(jnp.int32)


def draw_halo_count(key, part):
    key = jax.random.fold_in(key, 13)
    counts = jax.random.randint(key, (N_SLAB * N_WSH, 2), HALO // 2, HALO + 1)
    return counts.at[0].set(HALO).astype(jnp.int32)


def place_ends(drawn, own_key, smallest, high):
    shape = drawn.shape
    index_at = [jax.random.randint(jax.random.fold_in(own_key, axis), (), 0, shape[axis]) for axis in range(len(shape))]
    drawn = drawn.at[tuple(index_at)].set(smallest)
    longest = shape.index(max(shape))
    index_at[longest] = (index_at[longest] + 1) % shape[longest]
    return drawn.at[tuple(index_at)].set(high)


def block_levels(stream_key, extent, cuts, least, top_value):
    level, own = 1.0, jax.random.fold_in(stream_key, 6)
    for axis_at, shards_of in cuts:
        heights = jnp.exp(jax.random.uniform(jax.random.fold_in(own, axis_at), (shards_of,), jnp.float32, least / len(cuts), top_value / len(cuts)))
        level = level * jnp.repeat(heights, extent[axis_at] // shards_of).reshape([-1 if axis == axis_at else 1 for axis in range(len(extent))])
    return level


def centred(rng, shape, scale, reach, pieces=(), held_as=jnp.bfloat16):
    factor_of = block_levels(rng, shape, pieces, -0.22, 0.18) if pieces else 1.0
    result = jax.random.normal(rng, shape, jnp.float32) * scale * factor_of
    return jnp.minimum(jnp.maximum(result, -reach), reach).astype(held_as)


def setup_inputs(seed: int = 0) -> dict:
    seeds = jax.random.split(jax.random.key(seed), 14)
    return {
        "node_feat": centred(seeds[0], (NODES, D), 1.0, 6.0, ((0, 128),)),
        "cotangent": centred(seeds[1], (NODES, D), 1.0, 6.0, ((0, 128),)),
        "w_msg": centred(seeds[2], (D, D), D ** -0.5, 0.5, ((0, 4),)),
        "w_in": centred(seeds[3], (2 * D, D), (2 * D) ** -0.5, 0.375, ((0, 4),)),
        "w_out": centred(seeds[4], (D, D), D ** -0.5, 0.5, ((0, 4),)),
        "ln_gain": jnp.clip(1.0 + 0.15 * jax.random.normal(seeds[5], (D,), jnp.float32), 0.25, 1.75).astype(jnp.bfloat16),
        "tile_values": centred(seeds[6], (N_SLAB * N_WSH * TILES, EDGE_ROW, BLOCK), (2 * EDGE_ROW) ** -0.5, 2.0, ((0, 128),)),
        "tile_cols": place_ends(jax.random.randint(seeds[7], (N_SLAB * N_WSH * TILES, EDGE_ROW, BLOCK), 0, BLOCK), jax.random.fold_in(seeds[7], 1), 0, BLOCK - 1).astype(jnp.int32),
        "tile_dst": place_ends(jax.random.randint(seeds[8], (N_SLAB * N_WSH * TILES,), 0, NBLK), jax.random.fold_in(seeds[8], 1), 0, NBLK - 1).astype(jnp.int32),
        "tile_src": place_ends(jax.random.randint(seeds[9], (N_SLAB * N_WSH * TILES,), 0, SRC_BLOCKS), jax.random.fold_in(seeds[9], 1), 0, SRC_BLOCKS - 1).astype(jnp.int32),
        "tile_count": draw_tile_count(jax.random.fold_in(seeds[13], 71), 0),
        "halo_rows": draw_halo_rows(jax.random.fold_in(seeds[13], 71), 0),
        "halo_count": draw_halo_count(jax.random.fold_in(seeds[13], 71), 0),
    }


def silu_slope(argument):
    logistic = jax.nn.sigmoid(argument)
    return logistic * (1.0 + argument * (1.0 - logistic))

def contract_rows(left, right):
    return lax.dot_general(left, right, (((0,), (0,)), ((), ())), preferred_element_type=jnp.float32)

def contract_cols(left, right):
    return lax.dot_general(left, right, (((1,), (1,)), ((), ())), preferred_element_type=jnp.float32)

def reference(node_feat, cotangent, w_msg, w_in, w_out, ln_gain, tile_values, tile_cols, tile_dst, tile_src, tile_count, halo_rows, halo_count):
    devices = N_SLAB * N_WSH
    block_count = NODE_DEV // BLOCK
    local_rows = NODE_DEV + 2 * HALO
    pre_act = jnp.dot(node_feat, w_msg, preferred_element_type=jnp.float32)
    message = jax.nn.silu(pre_act).astype(jnp.bfloat16)
    by_device = message.reshape(devices, NODE_DEV, D)
    listed = halo_rows.reshape(devices, 2 * HALO)
    kept_slot = (jnp.arange(HALO)[None, None, :] < halo_count[:, :, None]).reshape(devices, 2 * HALO)
    outgoing = jax.vmap(lambda slab_rows, row_index: slab_rows[row_index])(by_device, listed)
    outgoing = jnp.where(kept_slot[:, :, None], outgoing, jnp.zeros_like(outgoing))
    outgoing = outgoing.reshape(N_SLAB, N_WSH, 2, HALO, D)
    zero_rim = jnp.zeros((1, N_WSH, HALO, D), jnp.bfloat16)
    from_lower = jnp.concatenate([zero_rim, outgoing[:-1, :, 1]], axis=0)
    from_upper = jnp.concatenate([outgoing[1:, :, 0], zero_rim], axis=0)
    sources = jnp.concatenate([by_device.reshape(N_SLAB, N_WSH, NODE_DEV, D), from_lower, from_upper], axis=2)
    sources = sources.reshape(N_SLAB, N_WSH * local_rows, D)
    tile_set = tile_values.reshape(N_SLAB, N_WSH * TILES, EDGE_ROW, BLOCK)
    col_set = tile_cols.reshape(N_SLAB, N_WSH * TILES, EDGE_ROW, BLOCK)
    offsets = (jnp.arange(N_WSH, dtype=jnp.int32) * block_count)[:, None]
    targets = (tile_dst.reshape(N_SLAB, N_WSH, TILES) + offsets[None]).reshape(N_SLAB, N_WSH * TILES)
    anchors = tile_src.reshape(N_SLAB, N_WSH * TILES)
    active = (jnp.arange(TILES)[None, :] < tile_count[:, None]).reshape(N_SLAB, N_WSH * TILES)

    def gather_slab(inputs):
        tile_part, cols, target, anchor, in_use, source = inputs
        rows = (anchor[:, None, None] * BLOCK + cols).astype(jnp.int32)
        picked = source[rows].astype(jnp.float32)
        product = lax.optimization_barrier(jnp.sum(tile_part.astype(jnp.float32)[..., None] * picked, axis=1))
        product = jnp.where(in_use[:, None, None], product, jnp.zeros_like(product))
        return jnp.zeros((N_WSH * block_count, BLOCK, D), jnp.float32).at[target].add(product)
    aggregate = lax.map(gather_slab, (tile_set, col_set, targets, anchors, active, sources)).reshape(-1, D)
    agg_rounded = aggregate.astype(jnp.bfloat16)
    hidden_pre = jnp.dot(node_feat, w_in[:D], preferred_element_type=jnp.float32) + jnp.dot(agg_rounded, w_in[D:], preferred_element_type=jnp.float32)
    hidden = jax.nn.silu(hidden_pre).astype(jnp.bfloat16)
    update = jnp.dot(hidden, w_out, preferred_element_type=jnp.float32)
    centre = update - lax.optimization_barrier(jnp.mean(update, axis=-1, keepdims=True))
    inverse = lax.rsqrt(lax.optimization_barrier(jnp.mean(centre * centre, axis=-1, keepdims=True)) + 1e-05)
    normed = centre * inverse
    gain = ln_gain.astype(jnp.float32)
    node_out = (node_feat.astype(jnp.float32) + gain * normed).astype(jnp.bfloat16)
    upstream = cotangent.astype(jnp.float32)
    d_normed = upstream * gain
    d_gain = lax.optimization_barrier(jnp.sum(upstream * normed, axis=0))
    d_update = ((d_normed - lax.optimization_barrier(jnp.mean(d_normed, axis=-1, keepdims=True)) - normed * lax.optimization_barrier(jnp.mean(d_normed * normed, axis=-1, keepdims=True))) * inverse).astype(jnp.bfloat16)
    d_w_out = contract_rows(hidden, d_update)
    d_hidden_pre = (contract_cols(d_update, w_out) * silu_slope(hidden_pre)).astype(jnp.bfloat16)
    d_w_in = jnp.concatenate([contract_rows(node_feat, d_hidden_pre), contract_rows(agg_rounded, d_hidden_pre)], axis=0)
    d_direct = contract_cols(d_hidden_pre, w_in[:D])
    d_agg = contract_cols(d_hidden_pre, w_in[D:]).astype(jnp.bfloat16).reshape(N_SLAB, N_WSH * block_count, BLOCK, D)

    def scatter_slab(inputs):
        tile_part, cols, target, anchor, in_use, upstream_blocks = inputs
        rows = (anchor[:, None, None] * BLOCK + cols).astype(jnp.int32)
        picked = upstream_blocks[target].astype(jnp.float32)
        terms = tile_part.astype(jnp.float32)[..., None] * picked[:, None]
        terms = jnp.where(in_use[:, None, None, None], terms, jnp.zeros_like(terms))
        return jnp.zeros((N_WSH * local_rows, D), jnp.float32).at[rows.reshape(-1)].add(terms.reshape(-1, D))
    d_sources = lax.map(scatter_slab, (tile_set, col_set, targets, anchors, active, d_agg)).reshape(N_SLAB, N_WSH, local_rows, D)
    d_own = d_sources[:, :, :NODE_DEV].reshape(devices, NODE_DEV, D)
    lower_grads = d_sources[:, :, NODE_DEV:NODE_DEV + HALO].astype(jnp.bfloat16)
    upper_grads = d_sources[:, :, NODE_DEV + HALO:].astype(jnp.bfloat16)
    zero_grads = jnp.zeros((1, N_WSH, HALO, D), jnp.bfloat16)
    back_lower = jnp.concatenate([zero_grads, upper_grads[:-1]], axis=0)
    back_upper = jnp.concatenate([lower_grads[1:], zero_grads], axis=0)
    returned = jnp.stack([back_lower, back_upper], axis=2).reshape(devices, 2 * HALO, D).astype(jnp.float32)
    returned = jnp.where(kept_slot[:, :, None], returned, jnp.zeros_like(returned))
    d_message = jax.vmap(lambda own_rows, row_index, extra: own_rows.at[row_index].add(extra))(d_own, listed, returned).reshape(-1, D)
    d_pre = (d_message * silu_slope(pre_act)).astype(jnp.bfloat16)
    d_w_msg = contract_rows(node_feat, d_pre)
    d_node = (upstream + d_direct + contract_cols(d_pre, w_msg)).astype(jnp.bfloat16)
    return (node_out, d_node, d_w_msg, d_w_in, d_w_out, d_gain)
```

```python
import functools

import jax
import jax.numpy as jnp
from jax import lax
from jax.experimental import pallas as pl
from jax.experimental.pallas import tpu as pltpu
from jax.sharding import PartitionSpec as P

F32 = jnp.float32
BF16 = jnp.bfloat16
SIDE = 128
UNROLL = 4
PARAMS = pltpu.CompilerParams(vmem_limit_bytes=48 * 2**20)
VMEM = pl.BlockSpec(memory_space=pltpu.VMEM)
SMEM = pl.BlockSpec(memory_space=pltpu.SMEM)


def dot(left, right, dims):
    return lax.dot_general(left, right, (dims, ((), ())), preferred_element_type=F32)


def rows_by_cols(left, right):
    return dot(left, right, ((1,), (0,)))


def contract_rows(left, right):
    return dot(left, right, ((0,), (0,)))


def contract_cols(left, right):
    return dot(left, right, ((1,), (1,)))


def sigmoid(v):
    return 1.0 / (1.0 + jnp.exp(-v))


def silu_slope(v):
    g = sigmoid(v)
    return g * (1.0 + v * (1.0 - g))


def pick_kernel(rows_ref, count_ref, feat_ref, out_ref, wide, picked):
    halo = rows_ref.shape[1]
    wide[...] = feat_ref[...].astype(F32)
    group = 16
    for k in range(2):
        count = count_ref[k]

        def body(step, carry):
            for u in range(group):
                slot = step * group + u
                row = rows_ref[k, slot]
                picked[pl.ds(slot, 1), :] = wide[pl.ds(row, 1), :]
            return carry

        lax.fori_loop(0, (count + group - 1) // group, body, 0)
        slots = lax.broadcasted_iota(jnp.int32, (halo, SIDE), 0)
        kept = jnp.where(slots < count, picked[...], 0.0)
        out_ref[pl.ds(k * halo, halo), :] = kept.astype(BF16)


def pick_rows(halo_rows, halo_count, node_feat):
    halo = halo_rows.shape[1]
    return pl.pallas_call(
        pick_kernel,
        out_shape=jax.ShapeDtypeStruct((2 * halo, SIDE), BF16),
        in_specs=[SMEM, SMEM, VMEM],
        out_specs=VMEM,
        scratch_shapes=[pltpu.VMEM(node_feat.shape, F32), pltpu.VMEM((halo, SIDE), F32)],
        compiler_params=PARAMS,
        name="pick_rows",
    )(halo_rows, halo_count, node_feat)


def list_kernel(parties, own_blocks, here_blocks, pos_ref, dst_ref, src_ref, count_ref, list_ref, total_ref):
    slots = dst_ref.shape[1]
    me = pos_ref[0]
    group = 8
    for k in range(parties):
        device = lax.rem(me + k, parties)
        count = count_ref[k]

        def body(step, carry):
            own, rim = carry
            for u in range(group):
                slot = step * group + u
                block = src_ref[k, slot] - me * here_blocks
                used = (slot < count) & (block >= 0) & (block < here_blocks)
                is_own = block < own_blocks
                base = device * slots + slot + (dst_ref[k, slot] << 16)
                list_ref[2 * k, own] = base + (block << 10)
                list_ref[2 * k + 1, rim] = base + ((block - own_blocks) << 10)
                own = own + jnp.where(used & is_own, 1, 0)
                rim = rim + jnp.where(used & jnp.logical_not(is_own), 1, 0)
            return (own, rim)

        own, rim = lax.fori_loop(0, slots // group, body, (jnp.int32(0), jnp.int32(0)))
        total_ref[2 * k] = own
        total_ref[2 * k + 1] = rim


def build_lists(position, dst, src, count, own_blocks, here_blocks):
    parties, slots = dst.shape
    return pl.pallas_call(
        functools.partial(list_kernel, parties, own_blocks, here_blocks),
        out_shape=(
            jax.ShapeDtypeStruct((2 * parties, slots + 16), jnp.int32),
            jax.ShapeDtypeStruct((2 * parties,), jnp.int32),
        ),
        in_specs=[SMEM] * 4,
        out_specs=(SMEM, SMEM),
        name="tile_lists",
    )(position, dst, src, count)


def dense_tile(tile, keep):
    column = lax.broadcasted_iota(jnp.int32, (SIDE, SIDE), 0).astype(F32)
    entries = tile.shape[0] // 2
    total = None
    for e in range(entries):
        weight = tile[e : e + 1, :] * keep
        term = jnp.where(column == tile[entries + e : entries + e + 1, :], weight, 0.0)
        total = term if total is None else total + term
    return total.astype(BF16)


def walk_list(list_ref, total_ref, which, tiles_ref, product, acc):
    count = total_ref[which]

    def body(step, carry):
        found = []
        for u in range(UNROLL):
            index = step * UNROLL + u
            used = index < count
            entry = jnp.where(used, list_ref[which, index], 0)
            dense = dense_tile(tiles_ref[entry & 1023], jnp.where(used, 1.0, 0.0))
            found.append(product(dense, (entry >> 10) & 63, entry >> 16))
        for target, value in found:
            acc[target] += value
        return carry

    lax.fori_loop(0, (count + UNROLL - 1) // UNROLL, body, 0)


def forward_kernel(ks, list_ref, total_ref, tiles_ref, own_ref, lower_ref, upper_ref, *rest):
    outs, (acc, rims) = rest[: len(ks)], rest[len(ks) :]
    half = lower_ref.shape[0]
    rims[pl.ds(0, half)] = lower_ref[...]
    rims[pl.ds(half, half)] = upper_ref[...]
    for k, out_ref in zip(ks, outs):
        acc[...] = jnp.zeros_like(acc)
        for part, ref in enumerate((own_ref, rims)):

            def product(dense, block, target, ref=ref):
                return (target, contract_rows(dense, ref[block]))

            walk_list(list_ref, total_ref, 2 * k + part, tiles_ref, product, acc)
        out_ref[...] = acc[...].astype(out_ref.dtype)


def forward_tiles(ks, lists, totals, tiles, own, lower, upper, kinds):
    return pl.pallas_call(
        functools.partial(forward_kernel, ks),
        out_shape=tuple(jax.ShapeDtypeStruct(own.shape, kind) for kind in kinds),
        in_specs=[SMEM, SMEM] + [VMEM] * 4,
        out_specs=tuple(VMEM for _ in ks),
        scratch_shapes=[
            pltpu.VMEM(own.shape, F32),
            pltpu.VMEM((2 * lower.shape[0],) + lower.shape[1:], BF16),
        ],
        compiler_params=PARAMS,
        cost_estimate=pl.CostEstimate(
            flops=60_000_000 * len(ks), bytes_accessed=4_000_000 * len(ks), transcendentals=0
        ),
        name="forward_tiles",
    )(lists, totals, tiles, own, lower, upper)


def node_kernel(
    feat_ref, cot_ref, a0_ref, a1_ref, a2_ref, a3_ref, in_ref, out_w_ref, gain_ref,
    node_ref, dagg_ref, dhid_ref, dwin_ref, dwout_ref, dgain_ref,
):
    @pl.when(pl.program_id(0) == 0)
    def _():
        dwin_ref[...] = jnp.zeros_like(dwin_ref)
        dwout_ref[...] = jnp.zeros_like(dwout_ref)
        dgain_ref[...] = jnp.zeros_like(dgain_ref)

    feat = feat_ref[...]
    agg = a0_ref[...] + a1_ref[...].astype(F32) + a2_ref[...].astype(F32) + a3_ref[...].astype(F32)
    agg = agg.astype(BF16)
    w_feat, w_agg, w_out = in_ref[:SIDE, :], in_ref[SIDE:, :], out_w_ref[...]
    gain = gain_ref[...].astype(F32)
    pre = rows_by_cols(feat, w_feat) + rows_by_cols(agg, w_agg)
    logistic = sigmoid(pre)
    hidden = (pre * logistic).astype(BF16)
    slope = logistic * (1.0 + pre * (1.0 - logistic))
    update = rows_by_cols(hidden, w_out)
    centre = update - jnp.mean(update, axis=-1, keepdims=True)
    inverse = lax.rsqrt(jnp.mean(centre * centre, axis=-1, keepdims=True) + 1e-05)
    normed = centre * inverse
    node_ref[...] = (feat.astype(F32) + gain * normed).astype(BF16)
    upstream = cot_ref[...].astype(F32)
    d_normed = upstream * gain
    dgain_ref[...] += jnp.sum(upstream * normed, axis=0, keepdims=True)
    d_update = (
        d_normed
        - jnp.mean(d_normed, axis=-1, keepdims=True)
        - normed * jnp.mean(d_normed * normed, axis=-1, keepdims=True)
    ) * inverse
    d_update = d_update.astype(BF16)
    d_hidden = (contract_cols(d_update, w_out) * slope).astype(BF16)
    dhid_ref[...] = d_hidden
    dagg_ref[...] = contract_cols(d_hidden, w_agg).astype(BF16)
    dwout_ref[...] += contract_rows(hidden, d_update)
    dwin_ref[:SIDE, :] += contract_rows(feat, d_hidden)
    dwin_ref[SIDE:, :] += contract_rows(agg, d_hidden)


def node_update(node_feat, cotangent, parts, w_in, w_out, gain):
    rows = node_feat.shape[0]
    steps = 8
    tall = pl.BlockSpec((rows // steps, SIDE), lambda i: (i, 0))

    def whole(shape):
        return pl.BlockSpec(shape, lambda i: (0, 0))

    wide = jax.ShapeDtypeStruct((rows, SIDE), BF16)
    return pl.pallas_call(
        node_kernel,
        grid=(steps,),
        out_shape=(
            wide,
            wide,
            wide,
            jax.ShapeDtypeStruct((2 * SIDE, SIDE), F32),
            jax.ShapeDtypeStruct((SIDE, SIDE), F32),
            jax.ShapeDtypeStruct((1, SIDE), F32),
        ),
        in_specs=[tall] * 6 + [whole((2 * SIDE, SIDE)), whole((SIDE, SIDE)), whole((1, SIDE))],
        out_specs=(tall, tall, tall, whole((2 * SIDE, SIDE)), whole((SIDE, SIDE)), whole((1, SIDE))),
        compiler_params=PARAMS,
        name="node_update",
    )(node_feat, cotangent, *parts, w_in, w_out, gain)


def backward_kernel(part, list_ref, total_ref, tiles_ref, g0_ref, g1_ref, g2_ref, g3_ref, out_ref, acc):
    acc[...] = jnp.zeros_like(acc)
    for k, ref in enumerate((g0_ref, g1_ref, g2_ref, g3_ref)):

        def product(dense, block, target, ref=ref):
            return (block, rows_by_cols(dense, ref[target]))

        walk_list(list_ref, total_ref, 2 * k + part, tiles_ref, product, acc)
    out_ref[...] = acc[...].astype(out_ref.dtype)


def backward_tiles(part, blocks, kind, lists, totals, tiles, grads):
    shape = (blocks, SIDE, SIDE)
    return pl.pallas_call(
        functools.partial(backward_kernel, part),
        out_shape=jax.ShapeDtypeStruct(shape, kind),
        in_specs=[SMEM, SMEM] + [VMEM] * 5,
        out_specs=VMEM,
        scratch_shapes=[pltpu.VMEM(shape, F32)],
        compiler_params=PARAMS,
        cost_estimate=pl.CostEstimate(flops=100_000_000, bytes_accessed=8_000_000, transcendentals=0),
        name="backward_tiles",
    )(lists, totals, tiles, *grads)


def last_kernel(
    pos_ref, rows_ref, count_ref, feat_ref, cot_ref, dhid_ref, own_ref, lower_ref, upper_ref, msg_ref, in_ref,
    dwin_ref, dwout_ref, dgain_ref,
    dnode_ref, r0_ref, r1_ref, r2_ref, r3_ref, acc, back, dw,
):
    halo = rows_ref.shape[1]
    acc[...] = own_ref[...]
    group = 8
    for k, ref in enumerate((lower_ref, upper_ref)):
        count = count_ref[k]
        slots = lax.broadcasted_iota(jnp.int32, (halo, SIDE), 0)
        back[...] = jnp.where(slots < count, ref[...].astype(F32), 0.0)

        def body(step, carry):
            rows = [rows_ref[k, step * group + u] for u in range(group)]
            added = [
                acc[pl.ds(row, 1), :] + back[pl.ds(step * group + u, 1), :] for u, row in enumerate(rows)
            ]
            for row, value in zip(rows, added):
                acc[pl.ds(row, 1), :] = value
            return carry

        lax.fori_loop(0, (count + group - 1) // group, body, 0)
    w_msg, w_feat = msg_ref[...], in_ref[:SIDE, :]
    dw[...] = jnp.zeros_like(dw)
    chunk = 512

    def step_rows(step, carry):
        at = pl.ds(pl.multiple_of(step * chunk, chunk), chunk)
        feat = feat_ref[at, :]
        d_pre = (acc[at, :] * silu_slope(rows_by_cols(feat, w_msg))).astype(BF16)
        dw[...] += contract_rows(feat, d_pre)
        total = cot_ref[at, :].astype(F32) + contract_cols(dhid_ref[at, :], w_feat)
        dnode_ref[at, :] = (total + contract_cols(d_pre, w_msg)).astype(BF16)
        return carry

    lax.fori_loop(0, acc.shape[0] // chunk, step_rows, 0)
    outs = (r0_ref, r1_ref, r2_ref, r3_ref)
    share = SIDE // len(outs)
    for k, out in enumerate(outs):
        device = lax.rem(pos_ref[0] + k, len(outs))
        start = pl.multiple_of(device * share, share)
        out[pl.ds(0, share), :] = dw[pl.ds(start, share), :]
        out[pl.ds(share, 2 * share), :] = dwin_ref[pl.ds(2 * start, 2 * share), :]
        out[pl.ds(3 * share, share), :] = dwout_ref[pl.ds(start, share), :]
        out[pl.ds(4 * share, 8), :] = jnp.broadcast_to(dgain_ref[...], (8, SIDE))


def last_products(position, halo_rows, halo_count, feat, cot, dhid, own, lower, upper, w_msg, w_in, dwin, dwout, dgain):
    rows = feat.shape[0]
    piece = jax.ShapeDtypeStruct((SIDE + 8, SIDE), F32)
    return pl.pallas_call(
        last_kernel,
        out_shape=(jax.ShapeDtypeStruct((rows, SIDE), BF16), piece, piece, piece, piece),
        in_specs=[SMEM] * 3 + [VMEM] * 11,
        out_specs=(VMEM,) * 5,
        scratch_shapes=[
            pltpu.VMEM((rows, SIDE), F32),
            pltpu.VMEM((halo_rows.shape[1], SIDE), F32),
            pltpu.VMEM((SIDE, SIDE), F32),
        ],
        compiler_params=PARAMS,
        name="last_products",
    )(position, halo_rows, halo_count, feat, cot, dhid, own, lower, upper, w_msg, w_in, dwin, dwout, dgain)


def shift_wsh(value, step):
    parties = lax.axis_size("wsh")
    return lax.ppermute(value, "wsh", [(i, (i + step) % parties) for i in range(parties)])


def shift_slab(value, step):
    count = lax.axis_size("slab")
    pairs = [(i, i + step) for i in range(count) if 0 <= i + step < count]
    return lax.ppermute(value, "slab", pairs)


def sum_slab(value):
    count = lax.axis_size("slab")
    for stride, size in ((8, 4), (2, 4), (1, 2)):
        total = value
        for k in range(1, size):
            span = stride * size
            pairs = [(i, (i // span) * span + (i + stride * k) % span) for i in range(count)]
            total = total + lax.ppermute(value, "slab", pairs)
        value = total
    return value


def on_device(
    node_feat, cotangent, w_msg, w_in, w_out, ln_gain,
    tile_values, tile_cols, tile_dst, tile_src, tile_count, halo_rows, halo_count,
):
    node_rows = node_feat.shape[0]
    slots, entries, side = tile_values.shape
    halo = halo_rows.shape[2]
    parties = lax.axis_size("wsh")
    me = lax.axis_index("wsh").astype(jnp.int32)
    position = me.reshape(1)
    share = w_msg.shape[0]
    own_blocks = node_rows // side
    rim_blocks = 2 * halo // side

    packed_tiles = jnp.concatenate([tile_values, tile_cols.astype(BF16)], axis=1)
    all_tiles = lax.all_gather(packed_tiles, "wsh", axis=0, tiled=True)

    gain_row = jnp.pad(ln_gain.reshape(1, share), ((0, 0), (0, side - share)))
    extras = jnp.concatenate(
        [
            gain_row,
            tile_dst.astype(BF16).reshape(1, side),
            tile_src.astype(BF16).reshape(1, side),
            jnp.broadcast_to(tile_count.astype(BF16).reshape(1, 1), (1, side)),
            jnp.zeros((12, side), BF16),
        ],
        axis=0,
    )
    small = jnp.concatenate([w_msg, w_in, w_out, extras], axis=0)
    arrived = [small] + [shift_wsh(small, -k) for k in range(1, parties)]
    relative = jnp.stack(arrived)
    absolute = lax.dynamic_slice_in_dim(
        jnp.concatenate([relative, relative], axis=0), lax.rem(parties - me, parties), parties, 0
    )
    full_msg = absolute[:, :share].reshape(4 * share, side)
    full_in = absolute[:, share : 3 * share].reshape(8 * share, side)
    full_out = absolute[:, 3 * share : 4 * share].reshape(4 * share, side)
    full_gain = absolute[:, 4 * share, :share].reshape(1, side)
    meta = relative[:, 4 * share + 1 : 4 * share + 4].astype(jnp.int32)
    dst, src, count = meta[:, 0], meta[:, 1], meta[:, 2, 0]

    rows = halo_rows.reshape(2, halo)
    counts = halo_count.reshape(2)
    picked = pick_rows(rows, counts, node_feat)
    outgoing = jax.nn.silu(rows_by_cols(picked, full_msg)).astype(BF16)
    lower = shift_slab(outgoing[halo:], 1)
    upper = shift_slab(outgoing[:halo], -1)
    message = jax.nn.silu(rows_by_cols(node_feat, full_msg)).astype(BF16)
    lists, totals = build_lists(position, dst, src, count, own_blocks, own_blocks + rim_blocks)
    tiles = all_tiles.astype(F32)

    blocks = message.reshape(own_blocks, side, side)
    lower = lower.reshape(rim_blocks // 2, side, side)
    upper = upper.reshape(rim_blocks // 2, side, side)
    (p2,) = forward_tiles((2,), lists, totals, tiles, blocks, lower, upper, (BF16,))
    a2 = shift_wsh(p2, 2)
    p1, p3 = forward_tiles((1, 3), lists, totals, tiles, blocks, lower, upper, (BF16, BF16))
    a1 = shift_wsh(p1, 1)
    a3 = shift_wsh(p3, 3)
    (p0,) = forward_tiles((0,), lists, totals, tiles, blocks, lower, upper, (F32,))
    parts = [part.reshape(node_rows, side) for part in (p0, a1, a2, a3)]

    node_out, d_agg, d_hidden, d_w_in, d_w_out, d_gain = node_update(
        node_feat, cotangent, parts, full_in, full_out, full_gain
    )
    grads = [d_agg] + [shift_wsh(d_agg, -k) for k in range(1, parties)]
    grads = [grad.reshape(own_blocks, side, side) for grad in grads]
    d_rims = backward_tiles(1, rim_blocks, BF16, lists, totals, tiles, grads).reshape(2 * halo, side)
    back_upper = shift_slab(d_rims[:halo], -1)
    back_lower = shift_slab(d_rims[halo:], 1)
    d_own = backward_tiles(0, own_blocks, F32, lists, totals, tiles, grads).reshape(node_rows, side)
    d_node, *pieces = last_products(
        position, rows, counts, node_feat, cotangent, d_hidden, d_own, back_lower, back_upper, full_msg, full_in,
        d_w_in, d_w_out, d_gain,
    )
    total = pieces[0]
    for k in range(1, parties):
        total = total + shift_wsh(pieces[k], k)
    total = sum_slab(total)
    gain_share = lax.dynamic_slice_in_dim(total[4 * share], me * share, share, 0)
    return (
        node_out, d_node, total[:share], total[share : 3 * share], total[3 * share : 4 * share], gain_share,
    )


def solution(mesh):
    both = ("slab", "wsh")
    tall, split, line = P(both, None), P("wsh", None), P(both)
    cube = P(both, None, None)
    return jax.shard_map(
        on_device,
        mesh=mesh,
        in_specs=(
            tall, tall, split, split, split, P("wsh"), cube, cube, line, line, line, cube, tall,
        ),
        out_specs=(tall, tall, split, split, split, P("wsh")),
        check_vma=False,
    )
```

```python
import functools

import jax
import jax.numpy as jnp
from jax import lax
from jax.experimental import pallas as pl
from jax.experimental.pallas import tpu as pltpu
from jax.sharding import PartitionSpec as P

F32 = jnp.float32
BF16 = jnp.bfloat16
SIDE = 128
UNROLL = 4
PARAMS = pltpu.CompilerParams(vmem_limit_bytes=48 * 2**20)
VMEM = pl.BlockSpec(memory_space=pltpu.VMEM)
SMEM = pl.BlockSpec(memory_space=pltpu.SMEM)


def dot(left, right, dims):
    return lax.dot_general(left, right, (dims, ((), ())), preferred_element_type=F32)


def rows_by_cols(left, right):
    return dot(left, right, ((1,), (0,)))


def contract_rows(left, right):
    return dot(left, right, ((0,), (0,)))


def contract_cols(left, right):
    return dot(left, right, ((1,), (1,)))


def sigmoid(v):
    return 1.0 / (1.0 + jnp.exp(-v))


def silu_slope(v):
    g = sigmoid(v)
    return g * (1.0 + v * (1.0 - g))


def pick_kernel(rows_ref, count_ref, feat_ref, out_ref, wide, picked):
    halo = rows_ref.shape[1]
    wide[...] = feat_ref[...].astype(F32)
    group = 16
    for k in range(2):
        count = count_ref[k]

        def body(step, carry):
            for u in range(group):
                slot = step * group + u
                row = rows_ref[k, slot]
                picked[pl.ds(slot, 1), :] = wide[pl.ds(row, 1), :]
            return carry

        lax.fori_loop(0, (count + group - 1) // group, body, 0)
        slots = lax.broadcasted_iota(jnp.int32, (halo, SIDE), 0)
        kept = jnp.where(slots < count, picked[...], 0.0)
        out_ref[pl.ds(k * halo, halo), :] = kept.astype(BF16)


def pick_rows(halo_rows, halo_count, node_feat):
    halo = halo_rows.shape[1]
    return pl.pallas_call(
        pick_kernel,
        out_shape=jax.ShapeDtypeStruct((2 * halo, SIDE), BF16),
        in_specs=[SMEM, SMEM, VMEM],
        out_specs=VMEM,
        scratch_shapes=[pltpu.VMEM(node_feat.shape, F32), pltpu.VMEM((halo, SIDE), F32)],
        compiler_params=PARAMS,
        name="pick_rows",
    )(halo_rows, halo_count, node_feat)


def pack_kernel(count_ref, msg_ref, in_ref, out_w_ref, gain_ref, dst_ref, src_ref, pack_ref, lines):
    share = msg_ref.shape[0]
    pack_ref[pl.ds(0, share), :] = msg_ref[...]
    pack_ref[pl.ds(share, 2 * share), :] = in_ref[...]
    pack_ref[pl.ds(3 * share, share), :] = out_w_ref[...]
    lines[...] = jnp.zeros_like(lines)
    gain = gain_ref[...].astype(F32)
    for j in range(SIDE // share):
        lines[0:1, j * share : (j + 1) * share] = gain
    lines[1:2, :] = dst_ref[...].astype(F32)
    lines[2:3, :] = src_ref[...].astype(F32)
    lines[3:4, :] = jnp.full((1, SIDE), count_ref[0]).astype(F32)
    pack_ref[pl.ds(4 * share, 16), :] = lines[...].astype(BF16)


def pack_small(tile_count, w_msg, w_in, w_out, ln_gain, tile_dst, tile_src):
    share = w_msg.shape[0]
    return pl.pallas_call(
        pack_kernel,
        out_shape=jax.ShapeDtypeStruct((4 * share + 16, SIDE), BF16),
        in_specs=[SMEM] + [VMEM] * 6,
        out_specs=VMEM,
        scratch_shapes=[pltpu.VMEM((16, SIDE), F32)],
        name="pack_small",
    )(tile_count, w_msg, w_in, w_out, ln_gain.reshape(1, share), tile_dst.reshape(1, SIDE), tile_src.reshape(1, SIDE))


def prepare_kernel(
    own_blocks, here_blocks, pos_ref, s0_ref, s1_ref, s2_ref, s3_ref, picked_ref,
    low_ref, high_ref, msg_ref, in_ref, out_w_ref, gain_ref, code_ref,
):
    me = pos_ref[0]
    smalls = (s0_ref, s1_ref, s2_ref, s3_ref)
    parties = len(smalls)
    share = SIDE // parties
    lane = lax.broadcasted_iota(jnp.int32, (1, SIDE), 1)
    gain = jnp.zeros((1, SIDE), F32)
    for k, ref in enumerate(smalls):
        device = lax.rem(me + k, parties)
        at = pl.multiple_of(device * share, share)
        msg_ref[pl.ds(at, share), :] = ref[pl.ds(0, share), :]
        in_ref[pl.ds(pl.multiple_of(2 * at, 2 * share), 2 * share), :] = ref[pl.ds(share, 2 * share), :]
        out_w_ref[pl.ds(at, share), :] = ref[pl.ds(3 * share, share), :]
        lines = ref[pl.ds(4 * share, 16), :].astype(F32)
        gain = jnp.where((lane >= at) & (lane < at + share), lines[0:1, :], gain)
        dst, src, count = (lines[i : i + 1, :].astype(jnp.int32) for i in (1, 2, 3))
        block = src - me * here_blocks
        used = (lane < count) & (block >= 0) & (block < here_blocks)
        is_rim = block >= own_blocks
        place = jnp.where(is_rim, block - own_blocks, block)
        code = lane + (place << 7) + (dst << 13) + jnp.where(is_rim, 2 << 20, 1 << 20)
        code_ref[k : k + 1, :] = jnp.where(used, code, 0)
        code_ref[parties + k : parties + k + 1, :] = count
    gain_ref[...] = gain
    half = low_ref.shape[0]
    w_msg = msg_ref[...]
    for k, ref in enumerate((low_ref, high_ref)):
        pre = rows_by_cols(picked_ref[pl.ds(k * half, half), :], w_msg)
        ref[...] = (pre * sigmoid(pre)).astype(BF16)


def prepare(position, smalls, picked, own_blocks, here_blocks):
    half = picked.shape[0] // 2
    return pl.pallas_call(
        functools.partial(prepare_kernel, own_blocks, here_blocks),
        out_shape=(
            jax.ShapeDtypeStruct((half, SIDE), BF16),
            jax.ShapeDtypeStruct((half, SIDE), BF16),
            jax.ShapeDtypeStruct((SIDE, SIDE), BF16),
            jax.ShapeDtypeStruct((2 * SIDE, SIDE), BF16),
            jax.ShapeDtypeStruct((SIDE, SIDE), BF16),
            jax.ShapeDtypeStruct((1, SIDE), F32),
            jax.ShapeDtypeStruct((8, SIDE), jnp.int32),
        ),
        in_specs=[SMEM] + [VMEM] * 5,
        out_specs=(VMEM,) * 7,
        compiler_params=PARAMS,
        name="prepare",
    )(position, *smalls, picked)


def list_kernel(code_ref, list_ref, total_ref):
    parties = code_ref.shape[0] // 2
    group = 8
    for k in range(parties):

        def body(step, carry):
            own, rim = carry
            for u in range(group):
                code = code_ref[k, step * group + u]
                list_ref[2 * k, own] = code
                list_ref[2 * k + 1, rim] = code
                own = own + ((code >> 20) & 1)
                rim = rim + (code >> 21)
            return (own, rim)

        steps = (code_ref[parties + k, 0] + group - 1) // group
        own, rim = lax.fori_loop(0, steps, body, (jnp.int32(0), jnp.int32(0)))
        total_ref[2 * k] = own
        total_ref[2 * k + 1] = rim


def build_lists(codes):
    parties, slots = codes.shape[0] // 2, codes.shape[1]
    return pl.pallas_call(
        list_kernel,
        out_shape=(
            jax.ShapeDtypeStruct((2 * parties, slots + 16), jnp.int32),
            jax.ShapeDtypeStruct((2 * parties,), jnp.int32),
        ),
        in_specs=[SMEM],
        out_specs=(SMEM, SMEM),
        name="tile_lists",
    )(codes)


def dense_tile(tile, keep):
    column = lax.broadcasted_iota(jnp.int32, (SIDE, SIDE), 0).astype(F32)
    entries = tile.shape[0] // 2
    total = None
    for e in range(entries):
        weight = tile[e : e + 1, :] * keep
        term = jnp.where(column == tile[entries + e : entries + e + 1, :], weight, 0.0)
        total = term if total is None else total + term
    return total.astype(BF16)


def walk_list(list_ref, total_ref, which, tiles_ref, product, acc):
    count = total_ref[which]

    def body(step, carry):
        found = []
        for u in range(UNROLL):
            index = step * UNROLL + u
            used = index < count
            entry = jnp.where(used, list_ref[which, index], 0)
            rows = pl.ds(pl.multiple_of((entry & 127) * 8, 8), 8)
            dense = dense_tile(tiles_ref[rows, :], jnp.where(used, 1.0, 0.0))
            found.append(product(dense, (entry >> 7) & 63, (entry >> 13) & 31))
        for target, value in found:
            acc[target] += value
        return carry

    lax.fori_loop(0, (count + UNROLL - 1) // UNROLL, body, 0)


def forward_kernel(ks, list_ref, total_ref, own_ref, lower_ref, upper_ref, *rest):
    tile_refs, rest = rest[: len(ks)], rest[len(ks) :]
    outs, (acc, rims, tiles) = rest[: 4 * len(ks)], rest[4 * len(ks) :]
    half = lower_ref.shape[0]
    rims[pl.ds(0, half)] = lower_ref[...]
    rims[pl.ds(half, half)] = upper_ref[...]
    for at, (k, tile_ref) in enumerate(zip(ks, tile_refs)):
        acc[...] = jnp.zeros_like(acc)
        tiles[...] = tile_ref[...].astype(F32)
        for part, ref in enumerate((own_ref, rims)):

            def product(dense, block, target, ref=ref):
                return (target, contract_rows(dense, ref[block]))

            walk_list(list_ref, total_ref, 2 * k + part, tiles, product, acc)
        for q in range(4):
            out_ref = outs[4 * at + q]
            span = out_ref.shape[0]
            out_ref[...] = acc[pl.ds(q * span, span)].astype(out_ref.dtype)


def forward_tiles(ks, lists, totals, own, lower, upper, tiles, kind):
    quarter = jax.ShapeDtypeStruct((own.shape[0] // 4,) + own.shape[1:], kind)
    return pl.pallas_call(
        functools.partial(forward_kernel, ks),
        out_shape=(quarter,) * (4 * len(ks)),
        in_specs=[SMEM, SMEM] + [VMEM] * (3 + len(ks)),
        out_specs=(VMEM,) * (4 * len(ks)),
        scratch_shapes=[
            pltpu.VMEM(own.shape, F32),
            pltpu.VMEM((2 * lower.shape[0],) + lower.shape[1:], BF16),
            pltpu.VMEM(tiles[0].shape, F32),
        ],
        compiler_params=PARAMS,
        cost_estimate=pl.CostEstimate(
            flops=1_000_000_000 * len(ks), bytes_accessed=4_000_000 * len(ks), transcendentals=0
        ),
        name="forward_tiles",
    )(lists, totals, own, lower, upper, *[tiles[k] for k in ks])


def node_kernel(
    feat_ref, cot_ref, own_ref, la_ref, ra_ref, lb_ref, rb_ref, in_ref, out_w_ref, gain_ref, *rest,
):
    node_ref, dhid_ref, dagg_ref, dwin_ref, dwout_ref, dgain_ref = rest[-6:]
    before = rest[:-6]
    sums = (dwin_ref, dwout_ref, dgain_ref)
    step = pl.program_id(0)

    @pl.when(step == 0)
    def _():
        for at, ref in enumerate(sums):
            ref[...] = before[2 + at][...] if before else jnp.zeros_like(ref)

    feat = feat_ref[...]
    first = step < pl.num_programs(0) // 2
    left = jnp.where(first, la_ref[...].astype(F32), lb_ref[...].astype(F32))
    right = jnp.where(first, ra_ref[...].astype(F32), rb_ref[...].astype(F32))
    agg = (own_ref[...] + (left + right)).astype(BF16)
    w_feat, w_agg, w_out = in_ref[:SIDE, :], in_ref[SIDE:, :], out_w_ref[...]
    gain = gain_ref[...]
    pre = rows_by_cols(feat, w_feat) + rows_by_cols(agg, w_agg)
    logistic = sigmoid(pre)
    hidden = (pre * logistic).astype(BF16)
    slope = logistic * (1.0 + pre * (1.0 - logistic))
    update = rows_by_cols(hidden, w_out)
    centre = update - jnp.mean(update, axis=-1, keepdims=True)
    inverse = lax.rsqrt(jnp.mean(centre * centre, axis=-1, keepdims=True) + 1e-05)
    normed = centre * inverse
    node_ref[...] = (feat.astype(F32) + gain * normed).astype(BF16)
    upstream = cot_ref[...].astype(F32)
    d_normed = upstream * gain
    dgain_ref[...] += jnp.sum(upstream * normed, axis=0, keepdims=True)
    d_update = (
        d_normed
        - jnp.mean(d_normed, axis=-1, keepdims=True)
        - normed * jnp.mean(d_normed * normed, axis=-1, keepdims=True)
    ) * inverse
    d_update = d_update.astype(BF16)
    d_hidden = (contract_cols(d_update, w_out) * slope).astype(BF16)
    dhid_ref[...] = d_hidden
    dagg_ref[...] = contract_cols(d_hidden, w_agg).astype(BF16)
    dwout_ref[...] += contract_rows(hidden, d_update)
    dwin_ref[:SIDE, :] += contract_rows(feat, d_hidden)
    dwin_ref[SIDE:, :] += contract_rows(agg, d_hidden)


def node_update(half, node_feat, cotangent, own, left_a, right_a, left_b, right_b, w_in, w_out, gain, before):
    rows = node_feat.shape[0]
    chunk = 512
    per = rows // 4 // chunk
    steps = 2 * per

    def whole(shape):
        return pl.BlockSpec(shape, lambda i: (0, 0))

    tall = pl.BlockSpec((chunk, SIDE), lambda i: (half * per + i + per * (i // per), 0))
    part_a = pl.BlockSpec((chunk, SIDE), lambda i: (jnp.minimum(i, per - 1), 0))
    part_b = pl.BlockSpec((chunk, SIDE), lambda i: (jnp.maximum(i - per, 0), 0))
    wide = jax.ShapeDtypeStruct((rows, SIDE), BF16)
    anywhere = pl.BlockSpec(memory_space=pl.ANY)
    sums = [(2 * SIDE, SIDE), (SIDE, SIDE), (1, SIDE)]
    return pl.pallas_call(
        node_kernel,
        grid=(steps,),
        out_shape=(
            wide,
            wide,
            jax.ShapeDtypeStruct((rows // 2, SIDE), BF16),
        ) + tuple(jax.ShapeDtypeStruct(shape, F32) for shape in sums),
        in_specs=[tall, tall, pl.BlockSpec((chunk, SIDE), lambda i: (i, 0)), part_a, part_a, part_b, part_b]
        + [whole((2 * SIDE, SIDE)), whole((SIDE, SIDE)), whole((1, SIDE))]
        + ([anywhere, anywhere] + [whole(shape) for shape in sums] if before else []),
        out_specs=(tall, tall, pl.BlockSpec((chunk, SIDE), lambda i: (i, 0)))
        + tuple(whole(shape) for shape in sums),
        input_output_aliases={10: 0, 11: 1} if before else {},
        compiler_params=PARAMS,
        cost_estimate=pl.CostEstimate(flops=5_000_000_000, bytes_accessed=10_000_000, transcendentals=0),
        name="node_update",
    )(node_feat, cotangent, own, left_a, right_a, left_b, right_b, w_in, w_out, gain, *before)


def share_kernel(pos_ref, dwin_ref, dwout_ref, dgain_ref, *outs):
    share = SIDE // len(outs)
    for k, out in enumerate(outs):
        device = lax.rem(pos_ref[0] + k, len(outs))
        start = pl.multiple_of(device * share, share)
        out[pl.ds(0, 2 * share), :] = dwin_ref[pl.ds(2 * start, 2 * share), :]
        out[pl.ds(2 * share, share), :] = dwout_ref[pl.ds(start, share), :]
        out[pl.ds(3 * share, 8), :] = jnp.broadcast_to(dgain_ref[...], (8, SIDE))


def split_shares(position, dwin, dwout, dgain):
    piece = jax.ShapeDtypeStruct((3 * SIDE // 4 + 8, SIDE), F32)
    return pl.pallas_call(
        share_kernel,
        out_shape=(piece,) * 4,
        in_specs=[SMEM] + [VMEM] * 3,
        out_specs=(VMEM,) * 4,
        name="split_shares",
    )(position, dwin, dwout, dgain)


def ahead_kernel(feat_ref, cot_ref, dhid_ref, msg_ref, in_ref, slope_ref, base_ref):
    slope_ref[...] = silu_slope(rows_by_cols(feat_ref[...], msg_ref[...]))
    base_ref[...] = cot_ref[...].astype(F32) + contract_cols(dhid_ref[...], in_ref[:SIDE, :])


def ahead(feat, cot, dhid, w_msg, w_in):
    rows = feat.shape[0]
    steps = 4
    tall = pl.BlockSpec((rows // steps, SIDE), lambda i: (i, 0))
    wide = jax.ShapeDtypeStruct((rows, SIDE), F32)
    return pl.pallas_call(
        ahead_kernel,
        grid=(steps,),
        out_shape=(wide, wide),
        in_specs=[tall] * 3 + [pl.BlockSpec(w.shape, lambda i: (0, 0)) for w in (w_msg, w_in)],
        out_specs=(tall, tall),
        compiler_params=PARAMS,
        cost_estimate=pl.CostEstimate(flops=3_000_000_000, bytes_accessed=7_000_000, transcendentals=0),
        name="ahead",
    )(feat, cot, dhid, w_msg, w_in)


def backward_kernel(part, list_ref, total_ref, *rest):
    tile_refs, quarters, (out_ref, acc, tiles, grads) = rest[:4], rest[4:-4], rest[-4:]
    acc[...] = jnp.zeros_like(acc)
    span = grads.shape[0] // 4
    for k, tile_ref in enumerate(tile_refs):
        tiles[...] = tile_ref[...].astype(F32)
        if k == 2:
            for q in range(4):
                grads[pl.ds(q * span, span)] = quarters[4 + q][...]
        else:
            for h in range(2):
                ref = quarters[{0: 0, 1: 2, 3: 8}[k] + h]
                grads[pl.ds(h * span, span)] = ref[pl.ds(0, span)]
                grads[pl.ds((2 + h) * span, span)] = ref[pl.ds(span, span)]

        def product(dense, block, target):
            return (block, rows_by_cols(dense, grads[target]))

        walk_list(list_ref, total_ref, 2 * k + part, tiles, product, acc)
    out_ref[...] = acc[...].astype(out_ref.dtype)


def backward_tiles(part, blocks, kind, lists, totals, tiles, grads):
    shape = (blocks, SIDE, SIDE)
    cubes = [grad.reshape(-1, SIDE, SIDE) for grad in grads]
    return pl.pallas_call(
        functools.partial(backward_kernel, part),
        out_shape=jax.ShapeDtypeStruct(shape, kind),
        in_specs=[SMEM, SMEM] + [VMEM] * (len(tiles) + len(cubes)),
        out_specs=VMEM,
        scratch_shapes=[
            pltpu.VMEM(shape, F32),
            pltpu.VMEM(tiles[0].shape, F32),
            pltpu.VMEM((2 * cubes[0].shape[0], SIDE, SIDE), BF16),
        ],
        compiler_params=PARAMS,
        cost_estimate=pl.CostEstimate(flops=3_000_000_000, bytes_accessed=8_000_000, transcendentals=0),
        name="backward_tiles",
    )(lists, totals, *tiles, *cubes)


def last_kernel(
    pos_ref, rows_ref, count_ref, own_ref, lower_ref, upper_ref, msg_ref, feat_any, slope_any, base_any,
    dnode_ref, r0_ref, r1_ref, r2_ref, r3_ref, back, dw, feat_ref, slope_ref, base_ref, acc, sems,
):
    copies = [
        pltpu.make_async_copy(source, target, sems.at[i])
        for i, (source, target) in enumerate(
            ((feat_any, feat_ref), (slope_any, slope_ref), (base_any, base_ref))
        )
    ]
    for copy in copies:
        copy.start()
    halo = rows_ref.shape[1]
    acc[...] = own_ref[...]
    group = 16
    for k, ref in enumerate((lower_ref, upper_ref)):
        count = count_ref[k]
        slots = lax.broadcasted_iota(jnp.int32, (halo, SIDE), 0)
        back[...] = jnp.where(slots < count, ref[...].astype(F32), 0.0)

        def body(step, carry):
            rows = [rows_ref[k, step * group + u] for u in range(group)]
            added = [
                acc[pl.ds(row, 1), :] + back[pl.ds(step * group + u, 1), :] for u, row in enumerate(rows)
            ]
            for row, value in zip(rows, added):
                acc[pl.ds(row, 1), :] = value
            return carry

        lax.fori_loop(0, (count + group - 1) // group, body, 0)
    for copy in copies:
        copy.wait()
    w_msg = msg_ref[...]
    dw[...] = jnp.zeros_like(dw)
    chunk = 512

    def step_rows(step, carry):
        at = pl.ds(pl.multiple_of(step * chunk, chunk), chunk)
        d_pre = (acc[at, :] * slope_ref[at, :]).astype(BF16)
        dw[...] += contract_rows(feat_ref[at, :], d_pre)
        dnode_ref[at, :] = (base_ref[at, :] + contract_cols(d_pre, w_msg)).astype(BF16)
        return carry

    lax.fori_loop(0, acc.shape[0] // chunk, step_rows, 0)
    outs = (r0_ref, r1_ref, r2_ref, r3_ref)
    share = SIDE // len(outs)
    for k, out in enumerate(outs):
        device = lax.rem(pos_ref[0] + k, len(outs))
        out[...] = dw[pl.ds(pl.multiple_of(device * share, share), share), :]


def last_products(position, halo_rows, halo_count, own, lower, upper, w_msg, feat, slope, base):
    rows = feat.shape[0]
    piece = jax.ShapeDtypeStruct((SIDE // 4, SIDE), F32)
    return pl.pallas_call(
        last_kernel,
        out_shape=(jax.ShapeDtypeStruct((rows, SIDE), BF16), piece, piece, piece, piece),
        in_specs=[SMEM] * 3 + [VMEM] * 4 + [pl.BlockSpec(memory_space=pl.ANY)] * 3,
        out_specs=(VMEM,) * 5,
        scratch_shapes=[
            pltpu.VMEM((halo_rows.shape[1], SIDE), F32),
            pltpu.VMEM((SIDE, SIDE), F32),
            pltpu.VMEM((rows, SIDE), BF16),
            pltpu.VMEM((rows, SIDE), F32),
            pltpu.VMEM((rows, SIDE), F32),
            pltpu.VMEM((rows, SIDE), F32),
            pltpu.SemaphoreType.DMA((3,)),
        ],
        compiler_params=PARAMS,
        name="last_products",
    )(position, halo_rows, halo_count, own, lower, upper, w_msg, feat, slope, base)


def shift_wsh(value, step):
    parties = lax.axis_size("wsh")
    return lax.ppermute(value, "wsh", [(i, (i + step) % parties) for i in range(parties)])


def shift_slab(value, step):
    count = lax.axis_size("slab")
    pairs = [(i, i + step) for i in range(count) if 0 <= i + step < count]
    return lax.ppermute(value, "slab", pairs)


def sum_slab(value):
    count = lax.axis_size("slab")
    for stride, size in ((8, 4), (2, 4), (1, 2)):
        total = value
        for k in range(1, size):
            span = stride * size
            pairs = [(i, (i // span) * span + (i + stride * k) % span) for i in range(count)]
            total = total + lax.ppermute(value, "slab", pairs)
        value = total
    return value


def sum_wsh(pieces):
    total = pieces[0]
    for k in range(1, len(pieces)):
        total = total + shift_wsh(pieces[k], k)
    return total


def add_parts(mine, theirs):
    return (mine.astype(F32) + theirs.astype(F32)).astype(BF16)


def on_device(
    node_feat, cotangent, w_msg, w_in, w_out, ln_gain,
    tile_values, tile_cols, tile_dst, tile_src, tile_count, halo_rows, halo_count,
):
    node_rows = node_feat.shape[0]
    slots, entries, side = tile_values.shape
    halo = halo_rows.shape[2]
    parties = lax.axis_size("wsh")
    me = lax.axis_index("wsh").astype(jnp.int32)
    position = me.reshape(1)
    share = w_msg.shape[0]
    own_blocks = node_rows // side
    rim_blocks = 2 * halo // side
    quarter = node_rows // 4

    small = pack_small(tile_count, w_msg, w_in, w_out, ln_gain, tile_dst, tile_src)
    smalls = [small] + [shift_wsh(small, -k) for k in range(1, parties)]
    own_tiles = jnp.concatenate([tile_values, tile_cols.astype(BF16)], axis=1).reshape(2 * entries * slots, side)
    tiles = [own_tiles] + [shift_wsh(own_tiles, -k) for k in range(1, parties)]

    rows = halo_rows.reshape(2, halo)
    counts = halo_count.reshape(2)
    picked = pick_rows(rows, counts, node_feat)
    low, high, full_msg, full_in, full_out, gain, codes = prepare(
        position, smalls, picked, own_blocks, own_blocks + rim_blocks
    )
    lower = shift_slab(high, 1).reshape(rim_blocks // 2, side, side)
    upper = shift_slab(low, -1).reshape(rim_blocks // 2, side, side)
    lists, totals = build_lists(codes)
    message = jax.nn.silu(rows_by_cols(node_feat, full_msg)).astype(BF16)
    sources = (message.reshape(own_blocks, side, side), lower, upper)

    far = forward_tiles((2,), lists, totals, *sources, tiles, BF16)
    from_right = [shift_wsh(far[q], -1) for q in (0, 1)]
    from_left = [shift_wsh(far[2 + q], 1) for q in (0, 1)]
    near = forward_tiles((1, 3), lists, totals, *sources, tiles, BF16)
    after, prior = near[:4], near[4:]
    left_a = [shift_wsh(after[q], 1) for q in (0, 1)]
    right_b = [shift_wsh(prior[2 + q], -1) for q in (0, 1)]
    left_b = [shift_wsh(add_parts(after[2 + q], from_left[q]), 1) for q in (0, 1)]
    right_a = [shift_wsh(add_parts(prior[q], from_right[q]), -1) for q in (0, 1)]
    mine = forward_tiles((0,), lists, totals, *sources, tiles, F32)

    before = ()
    halves = []
    for h in (0, 1):
        own = jnp.concatenate([mine[h], mine[2 + h]], axis=0).reshape(2 * quarter, side)
        pieces = [part.reshape(quarter, side) for part in (left_a[h], right_a[h], left_b[h], right_b[h])]
        node_out, d_hidden, half, *sums = node_update(
            h, node_feat, cotangent, own, *pieces, full_in, full_out, gain, before
        )
        before = (node_out, d_hidden, *sums)
        halves.append(half)
    after = [shift_wsh(half, -1) for half in halves]
    prior = [shift_wsh(half, 1) for half in halves]
    far_a = [shift_wsh(half[:quarter], 1) for half in prior]
    far_b = [shift_wsh(half[quarter:], -1) for half in after]
    grads = halves + after + far_a + far_b + prior

    early = sum_slab(sum_wsh(split_shares(position, *sums)))
    slope, base = ahead(node_feat, cotangent, d_hidden, full_msg, full_in)

    d_rims = backward_tiles(1, rim_blocks, BF16, lists, totals, tiles, grads).reshape(2 * halo, side)
    back_upper = shift_slab(d_rims[:halo], -1)
    back_lower = shift_slab(d_rims[halo:], 1)
    d_own = backward_tiles(0, own_blocks, F32, lists, totals, tiles, grads).reshape(node_rows, side)
    d_node, *pieces = last_products(
        position, rows, counts, d_own, back_lower, back_upper, full_msg, node_feat, slope, base
    )
    d_w_msg = sum_slab(sum_wsh(pieces))
    gain_share = lax.dynamic_slice_in_dim(early[3 * share], me * share, share, 0)
    return (node_out, d_node, d_w_msg, early[: 2 * share], early[2 * share : 3 * share], gain_share)


def solution(mesh):
    both = ("slab", "wsh")
    tall, split, line = P(both, None), P("wsh", None), P(both)
    cube = P(both, None, None)
    return jax.shard_map(
        on_device,
        mesh=mesh,
        in_specs=(
            tall, tall, split, split, split, P("wsh"), cube, cube, line, line, line, cube, tall,
        ),
        out_specs=(tall, tall, split, split, split, P("wsh")),
        check_vma=False,
    )
```

```python
import functools

import jax
import jax.numpy as jnp
from jax import lax
from jax.experimental import pallas as pl
from jax.experimental.pallas import tpu as pltpu
from jax.sharding import PartitionSpec as P

F32 = jnp.float32
BF16 = jnp.bfloat16
SIDE = 128
UNROLL = 4
PARAMS = pltpu.CompilerParams(vmem_limit_bytes=20 * 2**20)
ROOMY = pltpu.CompilerParams(vmem_limit_bytes=60 * 2**20)
VMEM = pl.BlockSpec(memory_space=pltpu.VMEM)
SMEM = pl.BlockSpec(memory_space=pltpu.SMEM)
ANY = pl.BlockSpec(memory_space=pl.ANY)


def cost(flops, size):
    return pl.CostEstimate(flops=flops, bytes_accessed=size, transcendentals=0)


def dot(left, right, dims):
    return lax.dot_general(left, right, (dims, ((), ())), preferred_element_type=F32)


def rows_by_cols(left, right):
    return dot(left, right, ((1,), (0,)))


def contract_rows(left, right):
    return dot(left, right, ((0,), (0,)))


def contract_cols(left, right):
    return dot(left, right, ((1,), (1,)))


def sigmoid(v):
    return 1.0 / (1.0 + jnp.exp(-v))


def silu_slope(v):
    g = sigmoid(v)
    return g * (1.0 + v * (1.0 - g))


def pick_kernel(rows_ref, count_ref, feat_ref, out_ref, wide, picked):
    halo = rows_ref.shape[1]
    wide[...] = feat_ref[...].astype(F32)
    group = 16
    for k in range(2):
        count = count_ref[k]

        def body(step, carry):
            for u in range(group):
                slot = step * group + u
                row = rows_ref[k, slot]
                picked[pl.ds(slot, 1), :] = wide[pl.ds(row, 1), :]
            return carry

        lax.fori_loop(0, (count + group - 1) // group, body, 0)
        slots = lax.broadcasted_iota(jnp.int32, (halo, SIDE), 0)
        kept = jnp.where(slots < count, picked[...], 0.0)
        out_ref[pl.ds(k * halo, halo), :] = kept.astype(BF16)


def pick_rows(halo_rows, halo_count, node_feat):
    halo = halo_rows.shape[1]
    return pl.pallas_call(
        pick_kernel,
        out_shape=jax.ShapeDtypeStruct((2 * halo, SIDE), BF16),
        in_specs=[SMEM, SMEM, VMEM],
        out_specs=VMEM,
        scratch_shapes=[pltpu.VMEM(node_feat.shape, F32), pltpu.VMEM((halo, SIDE), F32)],
        compiler_params=ROOMY,
        name="pick_rows",
    )(halo_rows, halo_count, node_feat)


def pack_kernel(
    count_ref, values_ref, cols_ref, msg_ref, in_ref, out_w_ref, gain_ref, dst_ref, src_ref, pack_ref, lines
):
    share, edges = msg_ref.shape[0], values_ref.shape[0]
    pack_ref[pl.ds(0, edges), :] = values_ref[...]
    pack_ref[pl.ds(edges, edges), :] = cols_ref[...].astype(F32).astype(BF16)
    small = 2 * edges
    pack_ref[pl.ds(small, share), :] = msg_ref[...]
    pack_ref[pl.ds(small + share, 2 * share), :] = in_ref[...]
    pack_ref[pl.ds(small + 3 * share, share), :] = out_w_ref[...]
    lines[...] = jnp.zeros_like(lines)
    gain = gain_ref[...].astype(F32)
    for j in range(SIDE // share):
        lines[0:1, j * share : (j + 1) * share] = gain
    lines[1:2, :] = dst_ref[...].astype(F32)
    lines[2:3, :] = src_ref[...].astype(F32)
    lines[3:4, :] = jnp.full((1, SIDE), count_ref[0]).astype(F32)
    pack_ref[pl.ds(small + 4 * share, 16), :] = lines[...].astype(BF16)


def pack_shares(tile_count, tile_values, tile_cols, w_msg, w_in, w_out, ln_gain, tile_dst, tile_src):
    share = w_msg.shape[0]
    values, cols = (array.reshape(-1, SIDE) for array in (tile_values, tile_cols))
    return pl.pallas_call(
        pack_kernel,
        out_shape=jax.ShapeDtypeStruct((2 * values.shape[0] + 4 * share + 16, SIDE), BF16),
        in_specs=[SMEM] + [VMEM] * 8,
        out_specs=VMEM,
        scratch_shapes=[pltpu.VMEM((16, SIDE), F32)],
        compiler_params=ROOMY,
        name="pack_shares",
    )(
        tile_count, values, cols, w_msg, w_in, w_out, ln_gain.reshape(1, share), tile_dst.reshape(1, SIDE),
        tile_src.reshape(1, SIDE),
    )


def prepare_kernel(
    own_blocks, here_blocks, pos_ref, s0_ref, s1_ref, s2_ref, s3_ref, picked_ref,
    low_ref, high_ref, msg_ref, in_ref, out_w_ref, gain_ref, code_ref,
):
    me = pos_ref[0]
    smalls = (s0_ref, s1_ref, s2_ref, s3_ref)
    parties = len(smalls)
    share = SIDE // parties
    small = s0_ref.shape[0] - SIDE - 16
    lane = lax.broadcasted_iota(jnp.int32, (1, SIDE), 1)
    gain = jnp.zeros((1, SIDE), F32)
    for k, ref in enumerate(smalls):
        device = lax.rem(me + k, parties)
        at = pl.multiple_of(device * share, share)
        msg_ref[pl.ds(at, share), :] = ref[pl.ds(small, share), :]
        in_ref[pl.ds(pl.multiple_of(2 * at, 2 * share), 2 * share), :] = ref[pl.ds(small + share, 2 * share), :]
        out_w_ref[pl.ds(at, share), :] = ref[pl.ds(small + 3 * share, share), :]
        lines = ref[pl.ds(small + 4 * share, 16), :].astype(F32)
        gain = jnp.where((lane >= at) & (lane < at + share), lines[0:1, :], gain)
        dst, src, count = (lines[i : i + 1, :].astype(jnp.int32) for i in (1, 2, 3))
        block = src - me * here_blocks
        used = (lane < count) & (block >= 0) & (block < here_blocks)
        is_rim = block >= own_blocks
        place = jnp.where(is_rim, block - own_blocks, block)
        code = lane + (place << 7) + (dst << 13) + jnp.where(is_rim, 2 << 20, 1 << 20)
        code_ref[k : k + 1, :] = jnp.where(used, code, 0)
        code_ref[parties + k : parties + k + 1, :] = count
    gain_ref[...] = gain
    half = low_ref.shape[0]
    w_msg = msg_ref[...]
    for k, ref in enumerate((low_ref, high_ref)):
        pre = rows_by_cols(picked_ref[pl.ds(k * half, half), :], w_msg)
        ref[...] = (pre * sigmoid(pre)).astype(BF16)


def prepare(position, smalls, picked, own_blocks, here_blocks):
    half = picked.shape[0] // 2
    return pl.pallas_call(
        functools.partial(prepare_kernel, own_blocks, here_blocks),
        out_shape=(
            jax.ShapeDtypeStruct((half, SIDE), BF16),
            jax.ShapeDtypeStruct((half, SIDE), BF16),
            jax.ShapeDtypeStruct((SIDE, SIDE), BF16),
            jax.ShapeDtypeStruct((2 * SIDE, SIDE), BF16),
            jax.ShapeDtypeStruct((SIDE, SIDE), BF16),
            jax.ShapeDtypeStruct((1, SIDE), F32),
            jax.ShapeDtypeStruct((8, SIDE), jnp.int32),
        ),
        in_specs=[SMEM] + [VMEM] * 5,
        out_specs=(VMEM,) * 7,
        compiler_params=PARAMS,
        name="prepare",
    )(position, *smalls, picked)


def message_kernel(feat_ref, msg_ref, out_ref):
    pre = rows_by_cols(feat_ref[...], msg_ref[...])
    out_ref[...] = (pre * sigmoid(pre)).astype(BF16)


def messages(feat, w_msg):
    rows = feat.shape[0]
    steps = 2
    tall = pl.BlockSpec((rows // steps, SIDE), lambda i: (i, 0))
    return pl.pallas_call(
        message_kernel,
        grid=(steps,),
        out_shape=jax.ShapeDtypeStruct((rows, SIDE), BF16),
        in_specs=[tall, pl.BlockSpec(w_msg.shape, lambda i: (0, 0))],
        out_specs=tall,
        compiler_params=PARAMS,
        name="messages",
    )(feat, w_msg)


def list_kernel(code_ref, list_ref, total_ref):
    parties = code_ref.shape[0] // 2
    group = 8
    for k in range(parties):

        def body(step, carry):
            own, rim = carry
            for u in range(group):
                code = code_ref[k, step * group + u]
                list_ref[2 * k, own] = code
                list_ref[2 * k + 1, rim] = code
                own = own + ((code >> 20) & 1)
                rim = rim + (code >> 21)
            return (own, rim)

        steps = (code_ref[parties + k, 0] + group - 1) // group
        own, rim = lax.fori_loop(0, steps, body, (jnp.int32(0), jnp.int32(0)))
        total_ref[2 * k] = own
        total_ref[2 * k + 1] = rim


def build_lists(codes):
    parties, slots = codes.shape[0] // 2, codes.shape[1]
    return pl.pallas_call(
        list_kernel,
        out_shape=(
            jax.ShapeDtypeStruct((2 * parties, slots + 16), jnp.int32),
            jax.ShapeDtypeStruct((2 * parties,), jnp.int32),
        ),
        in_specs=[SMEM],
        out_specs=(SMEM, SMEM),
        name="tile_lists",
    )(codes)


def dense_tile(tiles_ref, slot, keep):
    column = lax.broadcasted_iota(jnp.int32, (SIDE, SIDE), 0).astype(F32)
    edges = tiles_ref.shape[0] // 2
    entries = edges // SIDE
    total = None
    for e in range(entries):
        at = slot * entries + e
        weight = tiles_ref[pl.ds(at, 1), :] * keep
        term = jnp.where(column == tiles_ref[pl.ds(edges + at, 1), :], weight, 0.0)
        total = term if total is None else total + term
    return total.astype(BF16)


def walk_list(list_ref, total_ref, which, tiles_ref, product, acc):
    count = total_ref[which]

    def body(step, carry):
        found = []
        for u in range(UNROLL):
            index = step * UNROLL + u
            used = index < count
            entry = jnp.where(used, list_ref[which, index], 0)
            dense = dense_tile(tiles_ref, entry & 127, jnp.where(used, 1.0, 0.0))
            found.append(product(dense, (entry >> 7) & 63, (entry >> 13) & 31))
        for target, value in found:
            acc[target] += value
        return carry

    lax.fori_loop(0, (count + UNROLL - 1) // UNROLL, body, 0)


def forward_kernel(ks, list_ref, total_ref, own_ref, lower_ref, upper_ref, *rest):
    slot_refs, rest = rest[: len(ks)], rest[len(ks) :]
    outs, (acc, rims, tiles) = rest[: 2 * len(ks)], rest[2 * len(ks) :]
    half = lower_ref.shape[0]
    rims[pl.ds(0, half)] = lower_ref[...]
    rims[pl.ds(half, half)] = upper_ref[...]
    for at, (k, slot_ref) in enumerate(zip(ks, slot_refs)):
        acc[...] = jnp.zeros_like(acc)
        tiles[...] = slot_ref[pl.ds(0, tiles.shape[0]), :].astype(F32)
        for part, ref in enumerate((own_ref, rims)):

            def product(dense, block, target, ref=ref):
                return (target, contract_rows(dense, ref[block]))

            walk_list(list_ref, total_ref, 2 * k + part, tiles, product, acc)
        for h in range(2):
            out_ref = outs[2 * at + h]
            span = out_ref.shape[0]
            out_ref[...] = acc[pl.ds(h * span, span)].astype(out_ref.dtype)


def forward_tiles(ks, lists, totals, own, lower, upper, tiles, kind):
    blocks = own.shape[0]
    half = jax.ShapeDtypeStruct((blocks // 2,) + own.shape[1:], kind)
    return pl.pallas_call(
        functools.partial(forward_kernel, ks),
        out_shape=(half,) * (2 * len(ks)),
        in_specs=[SMEM, SMEM] + [VMEM] * (3 + len(ks)),
        out_specs=(VMEM,) * (2 * len(ks)),
        scratch_shapes=[
            pltpu.VMEM(own.shape, F32),
            pltpu.VMEM((2 * lower.shape[0],) + lower.shape[1:], BF16),
            pltpu.VMEM((tiles[0].shape[0] - SIDE - 16, SIDE), F32),
        ],
        compiler_params=PARAMS,
        cost_estimate=cost(1_000_000_000 * len(ks), 4_000_000 * len(ks)),
        name="forward_tiles",
    )(lists, totals, own, lower, upper, *[tiles[k] for k in ks])


def join_kernel(after_ref, left_ref, prior_ref, right_ref, *outs):
    for mine, theirs, out_ref in ((after_ref, left_ref, outs[0]), (prior_ref, right_ref, outs[1])):
        out_ref[...] = (mine[...].astype(F32) + theirs[...].astype(F32)).astype(BF16)


def join(after, from_left, prior, from_right):
    kind = jax.ShapeDtypeStruct(after.shape, BF16)
    return pl.pallas_call(
        join_kernel,
        out_shape=(kind, kind),
        in_specs=[VMEM] * 4,
        out_specs=(VMEM, VMEM),
        compiler_params=PARAMS,
        name="join",
    )(after, from_left, prior, from_right)


def node_kernel(
    feat_ref, cot_ref, own_a_ref, own_b_ref, la_ref, ra_ref, lb_ref, rb_ref, in_ref, out_w_ref, gain_ref,
    node_ref, dhid_ref, dagg_ref, dwin_ref, dwout_ref, dgain_ref,
):
    step = pl.program_id(0)

    @pl.when(step == 0)
    def _():
        for ref in (dwin_ref, dwout_ref, dgain_ref):
            ref[...] = jnp.zeros_like(ref)

    feat = feat_ref[...]
    first = step < pl.num_programs(0) // 2
    left = jnp.where(first, la_ref[...].astype(F32), lb_ref[...].astype(F32))
    right = jnp.where(first, ra_ref[...].astype(F32), rb_ref[...].astype(F32))
    own = jnp.where(first, own_a_ref[...], own_b_ref[...])
    agg = (own + (left + right)).astype(BF16)
    w_feat, w_agg, w_out = in_ref[:SIDE, :], in_ref[SIDE:, :], out_w_ref[...]
    gain = gain_ref[...]
    pre = rows_by_cols(feat, w_feat) + rows_by_cols(agg, w_agg)
    logistic = sigmoid(pre)
    hidden = (pre * logistic).astype(BF16)
    slope = logistic * (1.0 + pre * (1.0 - logistic))
    update = rows_by_cols(hidden, w_out)
    centre = update - jnp.mean(update, axis=-1, keepdims=True)
    inverse = lax.rsqrt(jnp.mean(centre * centre, axis=-1, keepdims=True) + 1e-05)
    normed = centre * inverse
    node_ref[...] = (feat.astype(F32) + gain * normed).astype(BF16)
    upstream = cot_ref[...].astype(F32)
    d_normed = upstream * gain
    dgain_ref[...] += jnp.sum(upstream * normed, axis=0, keepdims=True)
    d_update = (
        d_normed
        - jnp.mean(d_normed, axis=-1, keepdims=True)
        - normed * jnp.mean(d_normed * normed, axis=-1, keepdims=True)
    ) * inverse
    d_update = d_update.astype(BF16)
    d_hidden = (contract_cols(d_update, w_out) * slope).astype(BF16)
    dhid_ref[...] = d_hidden
    dagg_ref[...] = contract_cols(d_hidden, w_agg).astype(BF16)
    dwout_ref[...] += contract_rows(hidden, d_update)
    dwin_ref[:SIDE, :] += contract_rows(feat, d_hidden)
    dwin_ref[SIDE:, :] += contract_rows(agg, d_hidden)


def node_update(node_feat, cotangent, parts, w_in, w_out, gain):
    rows = node_feat.shape[0]
    chunk = 512
    steps = rows // chunk
    per = steps // 2

    def whole(shape):
        return pl.BlockSpec(shape, lambda i: (0, 0))

    tall = pl.BlockSpec((chunk, SIDE), lambda i: (i, 0))
    part_a = pl.BlockSpec((chunk, SIDE), lambda i: (jnp.minimum(i, per - 1), 0))
    part_b = pl.BlockSpec((chunk, SIDE), lambda i: (jnp.maximum(i - per, 0), 0))
    wide = jax.ShapeDtypeStruct((rows, SIDE), BF16)
    sums = [(2 * SIDE, SIDE), (SIDE, SIDE), (1, SIDE)]
    return pl.pallas_call(
        node_kernel,
        grid=(steps,),
        out_shape=(wide, wide, wide) + tuple(jax.ShapeDtypeStruct(shape, F32) for shape in sums),
        in_specs=[tall, tall, part_a, part_b, part_a, part_a, part_b, part_b]
        + [whole((2 * SIDE, SIDE)), whole((SIDE, SIDE)), whole((1, SIDE))],
        out_specs=(tall, tall, tall) + tuple(whole(shape) for shape in sums),
        compiler_params=PARAMS,
        cost_estimate=cost(10_000_000_000, 20_000_000),
        name="node_update",
    )(node_feat, cotangent, *parts, w_in, w_out, gain)


def ahead_kernel(feat_ref, cot_ref, dhid_ref, msg_ref, in_ref, slope_ref, base_ref):
    slope_ref[...] = silu_slope(rows_by_cols(feat_ref[...], msg_ref[...]))
    base_ref[...] = cot_ref[...].astype(F32) + contract_cols(dhid_ref[...], in_ref[:SIDE, :])


def ahead(feat, cot, dhid, w_msg, w_in):
    rows = feat.shape[0]
    steps = 4
    tall = pl.BlockSpec((rows // steps, SIDE), lambda i: (i, 0))
    wide = jax.ShapeDtypeStruct((rows, SIDE), F32)
    return pl.pallas_call(
        ahead_kernel,
        grid=(steps,),
        out_shape=(wide, wide),
        in_specs=[tall] * 3 + [pl.BlockSpec(w.shape, lambda i: (0, 0)) for w in (w_msg, w_in)],
        out_specs=(tall, tall),
        compiler_params=PARAMS,
        cost_estimate=cost(3_000_000_000, 7_000_000),
        name="ahead",
    )(feat, cot, dhid, w_msg, w_in)


def backward_kernel(ks, cuts, parts, started, list_ref, total_ref, *rest):
    slot_refs, rest = rest[: len(ks)], rest[len(ks) :]
    tiles, grads, accs = rest[-2 - len(parts)], rest[-1 - len(parts)], rest[-len(parts) :]
    arrays, rest = rest[: cuts * len(ks)], rest[cuts * len(ks) : -2 - len(parts)]
    for at, acc in enumerate(accs):
        acc[...] = rest[at][...] if started else jnp.zeros_like(acc)
    for at, (k, slot_ref) in enumerate(zip(ks, slot_refs)):
        tiles[...] = slot_ref[pl.ds(0, tiles.shape[0]), :].astype(F32)
        source = arrays[at]
        if cuts > 1:
            source, span = grads, grads.shape[0] // cuts
            for c in range(cuts):
                grads[pl.ds(c * span, span)] = arrays[cuts * at + c][...]

        def product(dense, block, target, source=source):
            return (block, rows_by_cols(dense, source[target]))

        for part, acc in zip(parts, accs):
            walk_list(list_ref, total_ref, 2 * k + part, tiles, product, acc)
    if parts == (1,):
        half = accs[0].shape[0] // 2
        for at, out_ref in enumerate(rest[-2:]):
            out_ref[...] = accs[0][pl.ds(at * half, half)].astype(out_ref.dtype)
    else:
        for out_ref, acc in zip(rest[-len(parts) :], accs):
            out_ref[...] = acc[...]


def backward_tiles(ks, parts, sizes, kinds, lists, totals, tiles, arrays, started, follow=()):
    cuts = len(arrays[0])
    cubes = [array.reshape(-1, SIDE, SIDE) for group in arrays for array in group]
    accs = [sum(sizes)] if len(sizes) > len(parts) else sizes
    return pl.pallas_call(
        functools.partial(backward_kernel, ks, cuts, parts, bool(started)),
        out_shape=tuple(jax.ShapeDtypeStruct((size, SIDE, SIDE), kind) for size, kind in zip(sizes, kinds)),
        in_specs=[SMEM, SMEM] + [VMEM] * (len(ks) + len(cubes) + len(started)) + [ANY] * len(follow),
        out_specs=(VMEM,) * len(sizes),
        scratch_shapes=[pltpu.VMEM((tiles[0].shape[0] - SIDE - 16, SIDE), F32), pltpu.VMEM((cuts * cubes[0].shape[0], SIDE, SIDE), BF16)]
        + [pltpu.VMEM((size, SIDE, SIDE), F32) for size in accs],
        compiler_params=PARAMS,
        cost_estimate=cost(2_000_000_000 * len(ks), 4_000_000),
        name="backward_tiles",
    )(lists, totals, *[tiles[k] for k in ks], *cubes, *started, *follow)


def last_kernel(
    pos_ref, rows_ref, count_ref, own_ref, lower_ref, upper_ref, msg_ref, dwin_ref, dwout_ref, dgain_ref,
    feat_ref, slope_ref, base_ref,
    dnode_ref, r0_ref, r1_ref, r2_ref, r3_ref, back, dw, acc,
):
    halo = rows_ref.shape[1]
    acc[...] = own_ref[...]
    group = 16
    for k, ref in enumerate((lower_ref, upper_ref)):
        count = count_ref[k]
        slots = lax.broadcasted_iota(jnp.int32, (halo, SIDE), 0)
        back[...] = jnp.where(slots < count, ref[...].astype(F32), 0.0)

        def body(step, carry):
            rows = [rows_ref[k, step * group + u] for u in range(group)]
            added = [
                acc[pl.ds(row, 1), :] + back[pl.ds(step * group + u, 1), :] for u, row in enumerate(rows)
            ]
            for row, value in zip(rows, added):
                acc[pl.ds(row, 1), :] = value
            return carry

        lax.fori_loop(0, (count + group - 1) // group, body, 0)
    w_msg = msg_ref[...]
    dw[...] = jnp.zeros_like(dw)
    chunk = 512

    def step_rows(step, carry):
        at = pl.ds(pl.multiple_of(step * chunk, chunk), chunk)
        d_pre = (acc[at, :] * slope_ref[at, :]).astype(BF16)
        dw[...] += contract_rows(feat_ref[at, :], d_pre)
        dnode_ref[at, :] = (base_ref[at, :] + contract_cols(d_pre, w_msg)).astype(BF16)
        return carry

    lax.fori_loop(0, acc.shape[0] // chunk, step_rows, 0)
    outs = (r0_ref, r1_ref, r2_ref, r3_ref)
    share = SIDE // len(outs)
    for k, out in enumerate(outs):
        device = lax.rem(pos_ref[0] + k, len(outs))
        start = pl.multiple_of(device * share, share)
        gain = jnp.zeros((16, SIDE), F32)
        for j in range(len(outs)):
            wide = jnp.broadcast_to(dgain_ref[...], (16, SIDE))
            gain = jnp.where(device == j, pltpu.roll(wide, (SIDE - j * share) % SIDE, 1), gain)
        out[pl.ds(0, share), :] = dw[pl.ds(start, share), :].astype(out.dtype)
        at = pl.ds(pl.multiple_of(2 * start, 2 * share), 2 * share)
        out[pl.ds(share, 2 * share), :] = dwin_ref[at, :].astype(out.dtype)
        out[pl.ds(3 * share, share), :] = dwout_ref[pl.ds(start, share), :].astype(out.dtype)
        out[pl.ds(4 * share, 16), :] = gain.astype(out.dtype)


def last_products(position, halo_rows, halo_count, own, lower, upper, w_msg, sums, feat, slope, base):
    rows = feat.shape[0]
    piece = jax.ShapeDtypeStruct((SIDE + 16, SIDE), BF16)
    return pl.pallas_call(
        last_kernel,
        out_shape=(jax.ShapeDtypeStruct((rows, SIDE), BF16), piece, piece, piece, piece),
        in_specs=[SMEM] * 3 + [VMEM] * 10,
        out_specs=(VMEM,) * 5,
        scratch_shapes=[
            pltpu.VMEM((halo_rows.shape[1], SIDE), F32),
            pltpu.VMEM((SIDE, SIDE), F32),
            pltpu.VMEM((rows, SIDE), F32),
        ],
        compiler_params=PARAMS,
        name="last_products",
    )(position, halo_rows, halo_count, own, lower, upper, w_msg, *sums, feat, slope, base)


def shift_wsh(value, step):
    parties = lax.axis_size("wsh")
    return lax.ppermute(value, "wsh", [(i, (i + step) % parties) for i in range(parties)])


def shift_slab(value, step):
    count = lax.axis_size("slab")
    pairs = [(i, i + step) for i in range(count) if 0 <= i + step < count]
    return lax.ppermute(value, "slab", pairs)


def sum_group(terms):
    total = terms[0].astype(F32)
    for term in terms[1:]:
        total = total + term.astype(F32)
    return total.astype(BF16)


def sum_everywhere(pieces):
    count = lax.axis_size("slab")
    value = sum_group([pieces[0]] + [shift_wsh(pieces[k], k) for k in range(1, len(pieces))])
    for stride, size in ((8, 4), (2, 4)):
        span = stride * size
        turns = [[(i, (i // span) * span + (i + stride * k) % span) for i in range(count)] for k in range(1, size)]
        value = sum_group([value] + [lax.ppermute(value, "slab", pairs) for pairs in turns])
    return value, lax.ppermute(value, "slab", [(i, i ^ 1) for i in range(count)])


def finish_kernel(one_ref, two_ref, msg_ref, in_ref, out_w_ref, gain_ref):
    share = msg_ref.shape[0]
    total = one_ref[...].astype(F32) + two_ref[...].astype(F32)
    msg_ref[...] = total[:share]
    in_ref[...] = total[share : 3 * share]
    out_w_ref[...] = total[3 * share : 4 * share]
    gain_ref[...] = total[4 * share : 4 * share + 1, :share]


def finish(one, two):
    share = SIDE // 4
    shapes = [(share, SIDE), (2 * share, SIDE), (share, SIDE), (1, share)]
    return pl.pallas_call(
        finish_kernel,
        out_shape=tuple(jax.ShapeDtypeStruct(shape, F32) for shape in shapes),
        in_specs=[VMEM, VMEM],
        out_specs=(VMEM,) * 4,
        name="finish",
    )(one, two)


def on_device(
    node_feat, cotangent, w_msg, w_in, w_out, ln_gain,
    tile_values, tile_cols, tile_dst, tile_src, tile_count, halo_rows, halo_count,
):
    node_rows = node_feat.shape[0]
    slots, entries, side = tile_values.shape
    halo = halo_rows.shape[2]
    parties = lax.axis_size("wsh")
    me = lax.axis_index("wsh").astype(jnp.int32)
    position = me.reshape(1)
    share = w_msg.shape[0]
    own_blocks = node_rows // side
    rim_blocks = 2 * halo // side

    tile = pack_shares(tile_count, tile_values, tile_cols, w_msg, w_in, w_out, ln_gain, tile_dst, tile_src)
    tiles = [tile] + [shift_wsh(tile, -k) for k in range(1, parties)]

    rows = halo_rows.reshape(2, halo)
    counts = halo_count.reshape(2)
    picked = pick_rows(rows, counts, node_feat)
    low, high, full_msg, full_in, full_out, gain, codes = prepare(
        position, tiles, picked, own_blocks, own_blocks + rim_blocks
    )
    lower = shift_slab(high, 1).reshape(rim_blocks // 2, side, side)
    upper = shift_slab(low, -1).reshape(rim_blocks // 2, side, side)
    message = messages(node_feat, full_msg)
    lists, totals = build_lists(codes)
    forward = functools.partial(
        forward_tiles, lists=lists, totals=totals, own=message.reshape(own_blocks, side, side), lower=lower,
        upper=upper, tiles=tiles,
    )

    far_first, far_second = forward((2,), kind=BF16)
    from_right = shift_wsh(far_first, -1)
    from_left = shift_wsh(far_second, 1)
    after_first, after_second, prior_first, prior_second = forward((1, 3), kind=BF16)
    left_first = shift_wsh(after_first, 1)
    right_second = shift_wsh(prior_second, -1)
    mine_first, mine_second = forward((0,), kind=F32)
    to_after, to_prior = join(after_second, from_left, prior_first, from_right)
    left_second = shift_wsh(to_after, 1)
    right_first = shift_wsh(to_prior, -1)
    parts = (mine_first, mine_second, left_first, right_first, left_second, right_second)
    parts = [part.reshape(-1, side) for part in parts]
    node_out, d_hidden, d_agg, *sums = node_update(node_feat, cotangent, parts, full_in, full_out, gain)
    from_prior = shift_wsh(d_agg, 1)
    from_after = shift_wsh(d_agg, -1)
    half = node_rows // 2
    far_first = shift_wsh(from_prior[:half], 1)
    far_second = shift_wsh(from_after[half:], -1)
    slope, base = ahead(node_feat, cotangent, d_hidden, full_msg, full_in)

    backward = functools.partial(backward_tiles, lists=lists, totals=totals, tiles=tiles)
    own_part, rim_part = backward(
        (0, 1, 3), (0, 1), (own_blocks, rim_blocks), (F32, F32), arrays=((d_agg,), (from_after,), (from_prior,)),
        started=(),
    )
    far = ((far_first, far_second),)
    back_low, back_high = backward(
        (2,), (1,), (rim_blocks // 2,) * 2, (BF16,) * 2, arrays=far, started=(rim_part,), follow=(slope,)
    )
    back_upper = shift_slab(back_low.reshape(halo, side), -1)
    back_lower = shift_slab(back_high.reshape(halo, side), 1)
    (d_own,) = backward((2,), (0,), (own_blocks,), (F32,), arrays=far, started=(own_part,))
    d_node, *pieces = last_products(
        position, rows, counts, d_own.reshape(node_rows, side), back_lower, back_upper, full_msg, sums, node_feat,
        slope, base,
    )
    d_w_msg, d_w_in, d_w_out, d_gain = finish(*sum_everywhere(pieces))
    return (node_out, d_node, d_w_msg, d_w_in, d_w_out, d_gain.reshape(share))


def solution(mesh):
    both = ("slab", "wsh")
    tall, split, line = P(both, None), P("wsh", None), P(both)
    cube = P(both, None, None)
    return jax.shard_map(
        on_device,
        mesh=mesh,
        in_specs=(
            tall, tall, split, split, split, P("wsh"), cube, cube, line, line, line, cube, tall,
        ),
        out_specs=(tall, tall, split, split, split, P("wsh")),
        check_vma=False,
    )
```

```python
import functools

import jax
import jax.numpy as jnp
from jax import lax
from jax.experimental import pallas as pl
from jax.experimental.pallas import tpu as pltpu
from jax.sharding import PartitionSpec as P

F32 = jnp.float32
BF16 = jnp.bfloat16
SIDE = 128
UNROLL = 4
PARAMS = pltpu.CompilerParams(vmem_limit_bytes=20 * 2**20)
ROOMY = pltpu.CompilerParams(vmem_limit_bytes=60 * 2**20)
VMEM = pl.BlockSpec(memory_space=pltpu.VMEM)
SMEM = pl.BlockSpec(memory_space=pltpu.SMEM)
ANY = pl.BlockSpec(memory_space=pl.ANY)


def cost(flops, size):
    return pl.CostEstimate(flops=flops, bytes_accessed=size, transcendentals=0)


def dot(left, right, dims):
    return lax.dot_general(left, right, (dims, ((), ())), preferred_element_type=F32)


def rows_by_cols(left, right):
    return dot(left, right, ((1,), (0,)))


def contract_rows(left, right):
    return dot(left, right, ((0,), (0,)))


def contract_cols(left, right):
    return dot(left, right, ((1,), (1,)))


def sigmoid(v):
    return 1.0 / (1.0 + jnp.exp(-v))


def silu_slope(v):
    g = sigmoid(v)
    return g * (1.0 + v * (1.0 - g))


def pick_kernel(rows_ref, count_ref, feat_ref, out_ref, wide, picked):
    halo = rows_ref.shape[1]
    wide[...] = feat_ref[...].astype(F32)
    group = 16
    for k in range(2):
        count = count_ref[k]

        def body(step, carry):
            for u in range(group):
                slot = step * group + u
                row = rows_ref[k, slot]
                picked[pl.ds(slot, 1), :] = wide[pl.ds(row, 1), :]
            return carry

        lax.fori_loop(0, (count + group - 1) // group, body, 0)
        slots = lax.broadcasted_iota(jnp.int32, (halo, SIDE), 0)
        kept = jnp.where(slots < count, picked[...], 0.0)
        out_ref[pl.ds(k * halo, halo), :] = kept.astype(BF16)


def pick_rows(halo_rows, halo_count, node_feat):
    halo = halo_rows.shape[1]
    return pl.pallas_call(
        pick_kernel,
        out_shape=jax.ShapeDtypeStruct((2 * halo, SIDE), BF16),
        in_specs=[SMEM, SMEM, VMEM],
        out_specs=VMEM,
        scratch_shapes=[pltpu.VMEM(node_feat.shape, F32), pltpu.VMEM((halo, SIDE), F32)],
        compiler_params=ROOMY,
        name="pick_rows",
    )(halo_rows, halo_count, node_feat)


def pack_kernel(
    count_ref, values_ref, cols_ref, msg_ref, in_ref, out_w_ref, gain_ref, dst_ref, src_ref, tiles_ref, pack_ref, lines
):
    share, edges = msg_ref.shape[0], values_ref.shape[0]
    tiles_ref[pl.ds(0, edges), :] = values_ref[...]
    tiles_ref[pl.ds(edges, edges), :] = cols_ref[...].astype(F32).astype(BF16)
    pack_ref[pl.ds(0, share), :] = msg_ref[...]
    pack_ref[pl.ds(share, 2 * share), :] = in_ref[...]
    pack_ref[pl.ds(3 * share, share), :] = out_w_ref[...]
    lines[...] = jnp.zeros_like(lines)
    gain = gain_ref[...].astype(F32)
    for j in range(SIDE // share):
        lines[0:1, j * share : (j + 1) * share] = gain
    lines[1:2, :] = dst_ref[...].astype(F32)
    lines[2:3, :] = src_ref[...].astype(F32)
    lines[3:4, :] = jnp.full((1, SIDE), count_ref[0]).astype(F32)
    pack_ref[pl.ds(4 * share, 16), :] = lines[...].astype(BF16)


def pack_shares(tile_count, tile_values, tile_cols, w_msg, w_in, w_out, ln_gain, tile_dst, tile_src):
    share = w_msg.shape[0]
    values, cols = (array.reshape(-1, SIDE) for array in (tile_values, tile_cols))
    return pl.pallas_call(
        pack_kernel,
        out_shape=(
            jax.ShapeDtypeStruct((2 * values.shape[0], SIDE), BF16),
            jax.ShapeDtypeStruct((4 * share + 16, SIDE), BF16),
        ),
        in_specs=[SMEM] + [VMEM] * 8,
        out_specs=(VMEM, VMEM),
        scratch_shapes=[pltpu.VMEM((16, SIDE), F32)],
        compiler_params=ROOMY,
        name="pack_shares",
    )(
        tile_count, values, cols, w_msg, w_in, w_out, ln_gain.reshape(1, share), tile_dst.reshape(1, SIDE),
        tile_src.reshape(1, SIDE),
    )


def prepare_kernel(
    own_blocks, here_blocks, pos_ref, s0_ref, s1_ref, s2_ref, s3_ref, picked_ref,
    low_ref, high_ref, msg_ref, in_ref, out_w_ref, gain_ref, code_ref,
):
    me = pos_ref[0]
    smalls = (s0_ref, s1_ref, s2_ref, s3_ref)
    parties = len(smalls)
    share = SIDE // parties
    lane = lax.broadcasted_iota(jnp.int32, (1, SIDE), 1)
    gain = jnp.zeros((1, SIDE), F32)
    for k, ref in enumerate(smalls):
        device = lax.rem(me + k, parties)
        at = pl.multiple_of(device * share, share)
        msg_ref[pl.ds(at, share), :] = ref[pl.ds(0, share), :]
        in_ref[pl.ds(pl.multiple_of(2 * at, 2 * share), 2 * share), :] = ref[pl.ds(share, 2 * share), :]
        out_w_ref[pl.ds(at, share), :] = ref[pl.ds(3 * share, share), :]
        lines = ref[pl.ds(4 * share, 16), :].astype(F32)
        gain = jnp.where((lane >= at) & (lane < at + share), lines[0:1, :], gain)
        dst, src, count = (lines[i : i + 1, :].astype(jnp.int32) for i in (1, 2, 3))
        block = src - me * here_blocks
        used = (lane < count) & (block >= 0) & (block < here_blocks)
        is_rim = block >= own_blocks
        place = jnp.where(is_rim, block - own_blocks, block)
        code = lane + (place << 7) + (dst << 13) + jnp.where(is_rim, 2 << 20, 1 << 20)
        code_ref[k : k + 1, :] = jnp.where(used, code, 0)
        code_ref[parties + k : parties + k + 1, :] = count
    gain_ref[...] = gain
    half = low_ref.shape[0]
    w_msg = msg_ref[...]
    for k, ref in enumerate((low_ref, high_ref)):
        pre = rows_by_cols(picked_ref[pl.ds(k * half, half), :], w_msg)
        ref[...] = (pre * sigmoid(pre)).astype(BF16)


def prepare(position, smalls, picked, own_blocks, here_blocks):
    half = picked.shape[0] // 2
    return pl.pallas_call(
        functools.partial(prepare_kernel, own_blocks, here_blocks),
        out_shape=(
            jax.ShapeDtypeStruct((half, SIDE), BF16),
            jax.ShapeDtypeStruct((half, SIDE), BF16),
            jax.ShapeDtypeStruct((SIDE, SIDE), BF16),
            jax.ShapeDtypeStruct((2 * SIDE, SIDE), BF16),
            jax.ShapeDtypeStruct((SIDE, SIDE), BF16),
            jax.ShapeDtypeStruct((1, SIDE), F32),
            jax.ShapeDtypeStruct((8, SIDE), jnp.int32),
        ),
        in_specs=[SMEM] + [VMEM] * 5,
        out_specs=(VMEM,) * 7,
        compiler_params=ROOMY,
        name="prepare",
    )(position, *smalls, picked)


def message_kernel(feat_ref, msg_ref, *rest):
    out_ref = rest[-1]
    pre = rows_by_cols(feat_ref[...], msg_ref[...])
    out_ref[...] = (pre * sigmoid(pre)).astype(BF16)


def messages(feat, w_msg, follow):
    rows = feat.shape[0]
    steps = 2
    tall = pl.BlockSpec((rows // steps, SIDE), lambda i: (i, 0))
    return pl.pallas_call(
        message_kernel,
        grid=(steps,),
        out_shape=jax.ShapeDtypeStruct((rows, SIDE), BF16),
        in_specs=[tall, pl.BlockSpec(w_msg.shape, lambda i: (0, 0))] + [ANY] * len(follow),
        out_specs=tall,
        compiler_params=PARAMS,
        name="messages",
    )(feat, w_msg, *follow)


def list_kernel(code_ref, list_ref, total_ref):
    parties = code_ref.shape[0] // 2
    group = 8
    for k in range(parties):

        def body(step, carry):
            own, rim = carry
            codes = [code_ref[k, step * group + u] for u in range(group)]
            for code in codes:
                list_ref[2 * k, own] = code
                list_ref[2 * k + 1, rim] = code
                own = own + ((code >> 20) & 1)
                rim = rim + (code >> 21)
            return (own, rim)

        steps = (code_ref[parties + k, 0] + group - 1) // group
        own, rim = lax.fori_loop(0, steps, body, (jnp.int32(0), jnp.int32(0)))
        total_ref[2 * k] = own
        total_ref[2 * k + 1] = rim


def build_lists(codes):
    parties, slots = codes.shape[0] // 2, codes.shape[1]
    return pl.pallas_call(
        list_kernel,
        out_shape=(
            jax.ShapeDtypeStruct((2 * parties, slots + 16), jnp.int32),
            jax.ShapeDtypeStruct((2 * parties,), jnp.int32),
        ),
        in_specs=[SMEM],
        out_specs=(SMEM, SMEM),
        name="tile_lists",
    )(codes)


def dense_tile(tiles_ref, slot, keep):
    column = lax.broadcasted_iota(jnp.int32, (SIDE, SIDE), 0).astype(F32)
    edges = tiles_ref.shape[0] // 2
    entries = edges // SIDE
    total = None
    for e in range(entries):
        at = slot * entries + e
        weight = tiles_ref[pl.ds(at, 1), :] * keep
        term = jnp.where(column == tiles_ref[pl.ds(edges + at, 1), :], weight, 0.0)
        total = term if total is None else total + term
    return total.astype(BF16)


def walk_list(list_ref, total_ref, which, tiles_ref, product, acc):
    count = total_ref[which]

    def body(step, carry):
        found = []
        for u in range(UNROLL):
            index = step * UNROLL + u
            used = index < count
            entry = jnp.where(used, list_ref[which, index], 0)
            dense = dense_tile(tiles_ref, entry & 127, jnp.where(used, 1.0, 0.0))
            found.append(product(dense, (entry >> 7) & 63, (entry >> 13) & 31))
        for target, value in found:
            acc[target] += value
        return carry

    lax.fori_loop(0, (count + UNROLL - 1) // UNROLL, body, 0)


def forward_kernel(ks, list_ref, total_ref, own_ref, lower_ref, upper_ref, *rest):
    slot_refs, rest = rest[: len(ks)], rest[len(ks) :]
    outs, (acc, rims, tiles) = rest[: 2 * len(ks)], rest[2 * len(ks) :]
    half = lower_ref.shape[0]
    rims[pl.ds(0, half)] = lower_ref[...]
    rims[pl.ds(half, half)] = upper_ref[...]
    for at, (k, slot_ref) in enumerate(zip(ks, slot_refs)):
        acc[...] = jnp.zeros_like(acc)
        tiles[...] = slot_ref[...].astype(F32)
        for part, ref in enumerate((own_ref, rims)):

            def product(dense, block, target, ref=ref):
                return (target, contract_rows(dense, ref[block]))

            walk_list(list_ref, total_ref, 2 * k + part, tiles, product, acc)
        for h in range(2):
            out_ref = outs[2 * at + h]
            span = out_ref.shape[0]
            out_ref[...] = acc[pl.ds(h * span, span)].astype(out_ref.dtype)


def forward_tiles(ks, lists, totals, own, lower, upper, tiles, kind):
    blocks = own.shape[0]
    half = jax.ShapeDtypeStruct((blocks // 2,) + own.shape[1:], kind)
    return pl.pallas_call(
        functools.partial(forward_kernel, ks),
        out_shape=(half,) * (2 * len(ks)),
        in_specs=[SMEM, SMEM] + [VMEM] * (3 + len(ks)),
        out_specs=(VMEM,) * (2 * len(ks)),
        scratch_shapes=[
            pltpu.VMEM(own.shape, F32),
            pltpu.VMEM((2 * lower.shape[0],) + lower.shape[1:], BF16),
            pltpu.VMEM(tiles[0].shape, F32),
        ],
        compiler_params=PARAMS,
        cost_estimate=cost(1_000_000_000 * len(ks), 4_000_000 * len(ks)),
        name="forward_tiles",
    )(lists, totals, own, lower, upper, *[tiles[k] for k in ks])


def join_kernel(after_ref, left_ref, prior_ref, right_ref, *outs):
    for mine, theirs, out_ref in ((after_ref, left_ref, outs[0]), (prior_ref, right_ref, outs[1])):
        out_ref[...] = (mine[...].astype(F32) + theirs[...].astype(F32)).astype(BF16)


def join(after, from_left, prior, from_right):
    kind = jax.ShapeDtypeStruct(after.shape, BF16)
    return pl.pallas_call(
        join_kernel,
        out_shape=(kind, kind),
        in_specs=[VMEM] * 4,
        out_specs=(VMEM, VMEM),
        compiler_params=PARAMS,
        name="join",
    )(after, from_left, prior, from_right)


def node_kernel(
    continued, feat_ref, cot_ref, own_ref, left_ref, right_ref, in_ref, out_w_ref, gain_ref, *rest,
):
    node_ref, dhid_ref, dagg_ref, dwin_ref, dwout_ref, dgain_ref = rest[-6:]
    step = pl.program_id(0)

    @pl.when(step == 0)
    def _():
        for at, ref in enumerate((dwin_ref, dwout_ref, dgain_ref)):
            ref[...] = rest[2 + at][...] if continued else jnp.zeros_like(ref)

    feat = feat_ref[...]
    agg = (own_ref[...] + (left_ref[...].astype(F32) + right_ref[...].astype(F32))).astype(BF16)
    w_feat, w_agg, w_out = in_ref[:SIDE, :], in_ref[SIDE:, :], out_w_ref[...]
    gain = gain_ref[...]
    pre = rows_by_cols(feat, w_feat) + rows_by_cols(agg, w_agg)
    logistic = sigmoid(pre)
    hidden = (pre * logistic).astype(BF16)
    slope = logistic * (1.0 + pre * (1.0 - logistic))
    update = rows_by_cols(hidden, w_out)
    centre = update - jnp.mean(update, axis=-1, keepdims=True)
    inverse = lax.rsqrt(jnp.mean(centre * centre, axis=-1, keepdims=True) + 1e-05)
    normed = centre * inverse
    node_ref[...] = (feat.astype(F32) + gain * normed).astype(BF16)
    upstream = cot_ref[...].astype(F32)
    d_normed = upstream * gain
    dgain_ref[...] += jnp.sum(upstream * normed, axis=0, keepdims=True)
    d_update = (
        d_normed
        - jnp.mean(d_normed, axis=-1, keepdims=True)
        - normed * jnp.mean(d_normed * normed, axis=-1, keepdims=True)
    ) * inverse
    d_update = d_update.astype(BF16)
    d_hidden = (contract_cols(d_update, w_out) * slope).astype(BF16)
    dhid_ref[...] = d_hidden
    dagg_ref[...] = contract_cols(d_hidden, w_agg).astype(BF16)
    dwout_ref[...] += contract_rows(hidden, d_update)
    dwin_ref[:SIDE, :] += contract_rows(feat, d_hidden)
    dwin_ref[SIDE:, :] += contract_rows(agg, d_hidden)


def node_update(h, node_feat, cotangent, parts, w_in, w_out, gain, before):
    rows = node_feat.shape[0]
    chunk = 512
    steps = rows // 2 // chunk

    def whole(shape):
        return pl.BlockSpec(shape, lambda i: (0, 0))

    tall = pl.BlockSpec((chunk, SIDE), lambda i: (h * steps + i, 0))
    part = pl.BlockSpec((chunk, SIDE), lambda i: (i, 0))
    wide = jax.ShapeDtypeStruct((rows, SIDE), BF16)
    half = jax.ShapeDtypeStruct((rows // 2, SIDE), BF16)
    sums = [(2 * SIDE, SIDE), (SIDE, SIDE), (1, SIDE)]
    return pl.pallas_call(
        functools.partial(node_kernel, bool(before)),
        grid=(steps,),
        out_shape=(wide, wide, half) + tuple(jax.ShapeDtypeStruct(shape, F32) for shape in sums),
        in_specs=[tall, tall, part, part, part]
        + [whole((2 * SIDE, SIDE)), whole((SIDE, SIDE)), whole((1, SIDE))]
        + ([ANY, ANY] + [whole(shape) for shape in sums] if before else []),
        out_specs=(tall, tall, part) + tuple(whole(shape) for shape in sums),
        input_output_aliases={8: 0, 9: 1} if before else {},
        compiler_params=PARAMS,
        cost_estimate=cost(5_000_000_000, 10_000_000),
        name="node_update",
    )(node_feat, cotangent, *parts, w_in, w_out, gain, *before)


def ahead_kernel(feat_ref, cot_ref, dhid_ref, picked_ref, msg_ref, in_ref, slope_ref, base_ref, far_ref):
    w_msg = msg_ref[...]
    slope_ref[...] = silu_slope(rows_by_cols(feat_ref[...], w_msg))
    far_ref[...] = silu_slope(rows_by_cols(picked_ref[...], w_msg))
    base_ref[...] = cot_ref[...].astype(F32) + contract_cols(dhid_ref[...], in_ref[:SIDE, :])


def ahead(feat, cot, dhid, picked, w_msg, w_in):
    rows = feat.shape[0]
    steps = 4
    tall = pl.BlockSpec((rows // steps, SIDE), lambda i: (i, 0))
    short = pl.BlockSpec((picked.shape[0] // steps, SIDE), lambda i: (i, 0))
    wide = jax.ShapeDtypeStruct((rows, SIDE), F32)
    return pl.pallas_call(
        ahead_kernel,
        grid=(steps,),
        out_shape=(wide, wide, jax.ShapeDtypeStruct(picked.shape, F32)),
        in_specs=[tall] * 3 + [short] + [pl.BlockSpec(w.shape, lambda i: (0, 0)) for w in (w_msg, w_in)],
        out_specs=(tall, tall, short),
        compiler_params=PARAMS,
        cost_estimate=cost(3_000_000_000, 7_000_000),
        name="ahead",
    )(feat, cot, dhid, picked, w_msg, w_in)


def backward_kernel(ks, cuts, parts, started, list_ref, total_ref, *rest):
    slot_refs, rest = rest[: len(ks)], rest[len(ks) :]
    tiles, grads, accs = rest[-2 - len(parts)], rest[-1 - len(parts)], rest[-len(parts) :]
    arrays, rest = rest[: cuts * len(ks)], rest[cuts * len(ks) : -2 - len(parts)]
    for at, acc in enumerate(accs):
        acc[...] = rest[at][...] if started else jnp.zeros_like(acc)
    for at, (k, slot_ref) in enumerate(zip(ks, slot_refs)):
        tiles[...] = slot_ref[...].astype(F32)
        source = arrays[at]
        if cuts > 1:
            source, span = grads, grads.shape[0] // cuts
            for c in range(cuts):
                grads[pl.ds(c * span, span)] = arrays[cuts * at + c][...]

        def product(dense, block, target, source=source):
            return (block, rows_by_cols(dense, source[target]))

        for part, acc in zip(parts, accs):
            walk_list(list_ref, total_ref, 2 * k + part, tiles, product, acc)
    if parts == (1,):
        half = accs[0].shape[0] // 2
        for at, out_ref in enumerate(rest[-2:]):
            out_ref[...] = accs[0][pl.ds(at * half, half)].astype(out_ref.dtype)
    else:
        for out_ref, acc in zip(rest[-len(parts) :], accs):
            out_ref[...] = acc[...]


def backward_tiles(ks, parts, sizes, kinds, lists, totals, tiles, arrays, started, follow=()):
    cuts = len(arrays[0])
    cubes = [array.reshape(-1, SIDE, SIDE) for group in arrays for array in group]
    accs = [sum(sizes)] if len(sizes) > len(parts) else sizes
    return pl.pallas_call(
        functools.partial(backward_kernel, ks, cuts, parts, bool(started)),
        out_shape=tuple(jax.ShapeDtypeStruct((size, SIDE, SIDE), kind) for size, kind in zip(sizes, kinds)),
        in_specs=[SMEM, SMEM] + [VMEM] * (len(ks) + len(cubes) + len(started)) + [ANY] * len(follow),
        out_specs=(VMEM,) * len(sizes),
        scratch_shapes=[pltpu.VMEM(tiles[0].shape, F32), pltpu.VMEM((cuts * cubes[0].shape[0], SIDE, SIDE), BF16)]
        + [pltpu.VMEM((size, SIDE, SIDE), F32) for size in accs],
        compiler_params=PARAMS,
        cost_estimate=cost(2_000_000_000 * len(ks), 4_000_000),
        name="backward_tiles",
    )(lists, totals, *[tiles[k] for k in ks], *cubes, *started, *follow)


def own_kernel(feat_ref, slope_ref, base_ref, own_ref, msg_ref, sum_ref, dw_ref):
    @pl.when(pl.program_id(0) == 0)
    def _():
        dw_ref[...] = jnp.zeros_like(dw_ref)

    d_pre = (own_ref[...] * slope_ref[...]).astype(BF16)
    dw_ref[...] += contract_rows(feat_ref[...], d_pre)
    sum_ref[...] = base_ref[...] + contract_cols(d_pre, msg_ref[...])


def own_products(feat, slope, base, own, w_msg):
    rows = feat.shape[0]
    steps = 4
    tall = pl.BlockSpec((rows // steps, SIDE), lambda i: (i, 0))
    square = pl.BlockSpec((SIDE, SIDE), lambda i: (0, 0))
    return pl.pallas_call(
        own_kernel,
        grid=(steps,),
        out_shape=(jax.ShapeDtypeStruct((rows, SIDE), F32), jax.ShapeDtypeStruct((SIDE, SIDE), F32)),
        in_specs=[tall] * 4 + [square],
        out_specs=(tall, square),
        compiler_params=PARAMS,
        cost_estimate=cost(3_000_000_000, 7_000_000),
        name="own_products",
    )(feat, slope, base, own, w_msg)


def rim_kernel(
    pos_ref, count_ref, lower_ref, upper_ref, picked_ref, far_ref, dw_ref, dwin_ref, dwout_ref, dgain_ref,
    dpre_ref, r0_ref, r1_ref, r2_ref, r3_ref, dw,
):
    halo = lower_ref.shape[0]
    dw[...] = dw_ref[...]
    for k, ref in enumerate((lower_ref, upper_ref)):
        at = pl.ds(k * halo, halo)
        slots = lax.broadcasted_iota(jnp.int32, (halo, SIDE), 0)
        d_pre = jnp.where(slots < count_ref[k], ref[...].astype(F32) * far_ref[at, :], 0.0).astype(BF16)
        dpre_ref[at, :] = d_pre
        dw[...] += contract_rows(picked_ref[at, :], d_pre)
    outs = (r0_ref, r1_ref, r2_ref, r3_ref)
    share = SIDE // len(outs)
    for k, out in enumerate(outs):
        device = lax.rem(pos_ref[0] + k, len(outs))
        start = pl.multiple_of(device * share, share)
        gain = jnp.zeros((16, SIDE), F32)
        for j in range(len(outs)):
            wide = jnp.broadcast_to(dgain_ref[...], (16, SIDE))
            gain = jnp.where(device == j, pltpu.roll(wide, (SIDE - j * share) % SIDE, 1), gain)
        out[pl.ds(0, share), :] = dw[pl.ds(start, share), :].astype(out.dtype)
        at = pl.ds(pl.multiple_of(2 * start, 2 * share), 2 * share)
        out[pl.ds(share, 2 * share), :] = dwin_ref[at, :].astype(out.dtype)
        out[pl.ds(3 * share, share), :] = dwout_ref[pl.ds(start, share), :].astype(out.dtype)
        out[pl.ds(4 * share, 16), :] = gain.astype(out.dtype)


def rim_products(position, halo_count, lower, upper, picked, far, dw, sums):
    piece = jax.ShapeDtypeStruct((SIDE + 16, SIDE), BF16)
    return pl.pallas_call(
        rim_kernel,
        out_shape=(jax.ShapeDtypeStruct(picked.shape, BF16), piece, piece, piece, piece),
        in_specs=[SMEM] * 2 + [VMEM] * 8,
        out_specs=(VMEM,) * 5,
        scratch_shapes=[pltpu.VMEM((SIDE, SIDE), F32)],
        compiler_params=PARAMS,
        name="rim_products",
    )(position, halo_count, lower, upper, picked, far, dw, *sums)


def place_kernel(k, rows_ref, count_ref, sum_ref, dpre_ref, msg_ref, *rest):
    out_ref, token_ref, acc, added = rest[-4:]
    token_ref[...] = jnp.zeros_like(token_ref)
    halo = rows_ref.shape[1]
    acc[...] = sum_ref[...]
    added[...] = contract_cols(dpre_ref[pl.ds(k * halo, halo), :], msg_ref[...])
    group = 16

    def body(step, carry):
        rows = [rows_ref[k, step * group + u] for u in range(group)]
        values = [acc[pl.ds(row, 1), :] + added[pl.ds(step * group + u, 1), :] for u, row in enumerate(rows)]
        for row, value in zip(rows, values):
            acc[pl.ds(row, 1), :] = value
        return carry

    lax.fori_loop(0, (count_ref[k] + group - 1) // group, body, 0)
    out_ref[...] = acc[...].astype(out_ref.dtype)


def place_rows(k, kind, halo_rows, halo_count, total, d_pre, w_msg, follow):
    return pl.pallas_call(
        functools.partial(place_kernel, k),
        out_shape=(jax.ShapeDtypeStruct(total.shape, kind), jax.ShapeDtypeStruct((8, SIDE), F32)),
        in_specs=[SMEM] * 2 + [VMEM] * 3 + [ANY] * len(follow),
        out_specs=(VMEM, VMEM),
        scratch_shapes=[pltpu.VMEM(total.shape, F32), pltpu.VMEM((halo_rows.shape[1], SIDE), F32)],
        compiler_params=PARAMS,
        cost_estimate=cost(4_000_000_000, 7_000_000),
        name="place_rows",
    )(halo_rows, halo_count, total, d_pre, w_msg, *follow)


def shift_wsh(value, step):
    parties = lax.axis_size("wsh")
    return lax.ppermute(value, "wsh", [(i, (i + step) % parties) for i in range(parties)])


def shift_slab(value, step):
    count = lax.axis_size("slab")
    pairs = [(i, i + step) for i in range(count) if 0 <= i + step < count]
    return lax.ppermute(value, "slab", pairs)


def sum_kernel(count, *refs):
    total = refs[0][...].astype(F32)
    for ref in refs[1:count]:
        total = total + ref[...].astype(F32)
    refs[-1][...] = total.astype(BF16)


def sum_group(terms, follow=()):
    return pl.pallas_call(
        functools.partial(sum_kernel, len(terms)),
        out_shape=jax.ShapeDtypeStruct(terms[0].shape, BF16),
        in_specs=[VMEM] * len(terms) + [ANY] * len(follow),
        out_specs=VMEM,
        compiler_params=PARAMS,
        name="sum_group",
    )(*terms, *follow)


def sum_wsh(pieces, follow):
    return sum_group([pieces[0]] + [shift_wsh(pieces[k], k) for k in range(1, len(pieces))], follow)


def sum_slab(value, stride, size, follow=()):
    count = lax.axis_size("slab")
    span = stride * size
    turns = [[(i, (i // span) * span + (i + stride * k) % span) for i in range(count)] for k in range(1, size)]
    return sum_group([value] + [lax.ppermute(value, "slab", pairs) for pairs in turns], follow)


def other_core(value):
    return lax.ppermute(value, "slab", [(i, i ^ 1) for i in range(lax.axis_size("slab"))])


def finish_kernel(one_ref, two_ref, msg_ref, in_ref, out_w_ref, gain_ref):
    share = msg_ref.shape[0]
    total = one_ref[...].astype(F32) + two_ref[...].astype(F32)
    msg_ref[...] = total[:share]
    in_ref[...] = total[share : 3 * share]
    out_w_ref[...] = total[3 * share : 4 * share]
    gain_ref[...] = total[4 * share : 4 * share + 1, :share]


def finish(one, two):
    share = SIDE // 4
    shapes = [(share, SIDE), (2 * share, SIDE), (share, SIDE), (1, share)]
    return pl.pallas_call(
        finish_kernel,
        out_shape=tuple(jax.ShapeDtypeStruct(shape, F32) for shape in shapes),
        in_specs=[VMEM, VMEM],
        out_specs=(VMEM,) * 4,
        name="finish",
    )(one, two)


def on_device(
    node_feat, cotangent, w_msg, w_in, w_out, ln_gain,
    tile_values, tile_cols, tile_dst, tile_src, tile_count, halo_rows, halo_count,
):
    node_rows = node_feat.shape[0]
    slots, entries, side = tile_values.shape
    halo = halo_rows.shape[2]
    parties = lax.axis_size("wsh")
    me = lax.axis_index("wsh").astype(jnp.int32)
    position = me.reshape(1)
    share = w_msg.shape[0]
    own_blocks = node_rows // side
    rim_blocks = 2 * halo // side

    tile, small = pack_shares(tile_count, tile_values, tile_cols, w_msg, w_in, w_out, ln_gain, tile_dst, tile_src)
    smalls = [small] + [shift_wsh(small, -k) for k in range(1, parties)]
    tiles = [tile] + [shift_wsh(tile, -k) for k in range(1, parties)]

    rows = halo_rows.reshape(2, halo)
    counts = halo_count.reshape(2)
    picked = pick_rows(rows, counts, node_feat)
    low, high, full_msg, full_in, full_out, gain, codes = prepare(
        position, smalls, picked, own_blocks, own_blocks + rim_blocks
    )
    lower = shift_slab(high, 1).reshape(rim_blocks // 2, side, side)
    upper = shift_slab(low, -1).reshape(rim_blocks // 2, side, side)
    message = messages(node_feat, full_msg, tiles[1:])
    lists, totals = build_lists(codes)
    forward = functools.partial(
        forward_tiles, lists=lists, totals=totals, own=message.reshape(own_blocks, side, side), lower=lower,
        upper=upper, tiles=tiles,
    )

    far_first, far_second = forward((2,), kind=BF16)
    from_right = shift_wsh(far_first, -1)
    from_left = shift_wsh(far_second, 1)
    after_first, after_second, prior_first, prior_second = forward((1, 3), kind=BF16)
    left_first = shift_wsh(after_first, 1)
    right_second = shift_wsh(prior_second, -1)
    mine_first, mine_second = forward((0,), kind=F32)
    to_after, to_prior = join(after_second, from_left, prior_first, from_right)
    left_second = shift_wsh(to_after, 1)
    right_first = shift_wsh(to_prior, -1)
    parts = ((mine_first, left_first, right_first), (mine_second, left_second, right_second))
    before, d_agg, from_prior, from_after = (), [], [], []
    for h in (0, 1):
        pieces = [part.reshape(-1, side) for part in parts[h]]
        node_out, d_hidden, half, *sums = node_update(
            h, node_feat, cotangent, pieces, full_in, full_out, gain, before
        )
        before = (node_out, d_hidden, *sums)
        d_agg.append(half)
        from_prior.append(shift_wsh(half, 1))
        from_after.append(shift_wsh(half, -1))
    quarter = node_rows // 4
    far = []
    for h in (0, 1):
        far.append(shift_wsh(from_prior[h][:quarter], 1))
        far.append(shift_wsh(from_after[h][quarter:], -1))
    slope, base, far_slope = ahead(node_feat, cotangent, d_hidden, picked, full_msg, full_in)

    backward = functools.partial(backward_tiles, lists=lists, totals=totals, tiles=tiles)
    own_part, rim_part = backward(
        (0, 1, 3), (0, 1), (own_blocks, rim_blocks), (F32, F32), arrays=(d_agg, from_after, from_prior),
        started=(),
    )
    back_low, back_high = backward(
        (2,), (1,), (rim_blocks // 2,) * 2, (BF16,) * 2, arrays=(far,), started=(rim_part,), follow=(slope,)
    )
    back_upper = shift_slab(back_low.reshape(halo, side), -1)
    back_lower = shift_slab(back_high.reshape(halo, side), 1)
    (d_own,) = backward((2,), (0,), (own_blocks,), (F32,), arrays=(far,), started=(own_part,))
    total, d_w_own = own_products(node_feat, slope, base, d_own.reshape(node_rows, side), full_msg)
    d_pre, *pieces = rim_products(
        position, counts, back_lower, back_upper, picked, far_slope, d_w_own, sums
    )
    place = functools.partial(place_rows, halo_rows=rows, halo_count=counts, d_pre=d_pre, w_msg=full_msg)
    total, token = place(0, F32, total=total, follow=())
    value = sum_wsh(pieces, (token,))
    d_node, token = place(1, BF16, total=total, follow=(value,))
    value = sum_slab(value, 8, 4, (token,))
    value = sum_slab(value, 2, 4)
    d_w_msg, d_w_in, d_w_out, d_gain = finish(value, other_core(value))
    return (node_out, d_node, d_w_msg, d_w_in, d_w_out, d_gain.reshape(share))


def solution(mesh):
    both = ("slab", "wsh")
    tall, split, line = P(both, None), P("wsh", None), P(both)
    cube = P(both, None, None)
    return jax.shard_map(
        on_device,
        mesh=mesh,
        in_specs=(
            tall, tall, split, split, split, P("wsh"), cube, cube, line, line, line, cube, tall,
        ),
        out_specs=(tall, tall, split, split, split, P("wsh")),
        check_vma=False,
    )
```

```python
import functools

import jax
import jax.numpy as jnp
from jax import lax
from jax.experimental import pallas as pl
from jax.experimental.pallas import tpu as pltpu
from jax.sharding import PartitionSpec as P

F32 = jnp.float32
BF16 = jnp.bfloat16
SIDE = 128
UNROLL = 4
PARAMS = pltpu.CompilerParams(vmem_limit_bytes=20 * 2**20)
SMALL = pltpu.CompilerParams(vmem_limit_bytes=4 * 2**20)
ROOMY = pltpu.CompilerParams(vmem_limit_bytes=60 * 2**20)
VMEM = pl.BlockSpec(memory_space=pltpu.VMEM)
SMEM = pl.BlockSpec(memory_space=pltpu.SMEM)
ANY = pl.BlockSpec(memory_space=pl.ANY)


def cost(flops, size):
    return pl.CostEstimate(flops=flops, bytes_accessed=size, transcendentals=0)


def dot(left, right, dims):
    return lax.dot_general(left, right, (dims, ((), ())), preferred_element_type=F32)


def rows_by_cols(left, right):
    return dot(left, right, ((1,), (0,)))


def contract_rows(left, right):
    return dot(left, right, ((0,), (0,)))


def contract_cols(left, right):
    return dot(left, right, ((1,), (1,)))


def sigmoid(v):
    return 1.0 / (1.0 + jnp.exp(-v))


def silu_slope(v):
    g = sigmoid(v)
    return g * (1.0 + v * (1.0 - g))


def pick_kernel(rows_ref, count_ref, feat_ref, out_ref, wide, picked):
    halo = rows_ref.shape[1]
    wide[...] = feat_ref[...].astype(F32)
    group = 16
    for k in range(2):
        count = count_ref[k]

        def body(step, carry):
            for u in range(group):
                slot = step * group + u
                row = rows_ref[k, slot]
                picked[pl.ds(slot, 1), :] = wide[pl.ds(row, 1), :]
            return carry

        lax.fori_loop(0, (count + group - 1) // group, body, 0)
        slots = lax.broadcasted_iota(jnp.int32, (halo, SIDE), 0)
        kept = jnp.where(slots < count, picked[...], 0.0)
        out_ref[pl.ds(k * halo, halo), :] = kept.astype(BF16)


def pick_rows(halo_rows, halo_count, node_feat):
    halo = halo_rows.shape[1]
    return pl.pallas_call(
        pick_kernel,
        out_shape=jax.ShapeDtypeStruct((2 * halo, SIDE), BF16),
        in_specs=[SMEM, SMEM, VMEM],
        out_specs=VMEM,
        scratch_shapes=[pltpu.VMEM(node_feat.shape, F32), pltpu.VMEM((halo, SIDE), F32)],
        compiler_params=ROOMY,
        name="pick_rows",
    )(halo_rows, halo_count, node_feat)


def pack_kernel(
    count_ref, values_ref, cols_ref, msg_ref, in_ref, out_w_ref, gain_ref, dst_ref, src_ref, tiles_ref, pack_ref, lines
):
    share, edges = msg_ref.shape[0], values_ref.shape[0]
    tiles_ref[pl.ds(0, edges), :] = values_ref[...]
    tiles_ref[pl.ds(edges, edges), :] = cols_ref[...].astype(F32).astype(BF16)
    pack_ref[pl.ds(0, share), :] = msg_ref[...]
    pack_ref[pl.ds(share, 2 * share), :] = in_ref[...]
    pack_ref[pl.ds(3 * share, share), :] = out_w_ref[...]
    lines[...] = jnp.zeros_like(lines)
    gain = gain_ref[...].astype(F32)
    for j in range(SIDE // share):
        lines[0:1, j * share : (j + 1) * share] = gain
    lines[1:2, :] = dst_ref[...].astype(F32)
    lines[2:3, :] = src_ref[...].astype(F32)
    lines[3:4, :] = jnp.full((1, SIDE), count_ref[0]).astype(F32)
    pack_ref[pl.ds(4 * share, 16), :] = lines[...].astype(BF16)


def pack_shares(tile_count, tile_values, tile_cols, w_msg, w_in, w_out, ln_gain, tile_dst, tile_src):
    share = w_msg.shape[0]
    values, cols = (array.reshape(-1, SIDE) for array in (tile_values, tile_cols))
    return pl.pallas_call(
        pack_kernel,
        out_shape=(
            jax.ShapeDtypeStruct((2 * values.shape[0], SIDE), BF16),
            jax.ShapeDtypeStruct((4 * share + 16, SIDE), BF16),
        ),
        in_specs=[SMEM] + [VMEM] * 8,
        out_specs=(VMEM, VMEM),
        scratch_shapes=[pltpu.VMEM((16, SIDE), F32)],
        compiler_params=ROOMY,
        name="pack_shares",
    )(
        tile_count, values, cols, w_msg, w_in, w_out, ln_gain.reshape(1, share), tile_dst.reshape(1, SIDE),
        tile_src.reshape(1, SIDE),
    )


def prepare_kernel(
    own_blocks, here_blocks, pos_ref, s0_ref, s1_ref, s2_ref, s3_ref, picked_ref,
    low_ref, high_ref, msg_ref, in_ref, out_w_ref, gain_ref, code_ref,
):
    me = pos_ref[0]
    smalls = (s0_ref, s1_ref, s2_ref, s3_ref)
    parties = len(smalls)
    share = SIDE // parties
    lane = lax.broadcasted_iota(jnp.int32, (1, SIDE), 1)
    gain = jnp.zeros((1, SIDE), F32)
    for k, ref in enumerate(smalls):
        device = lax.rem(me + k, parties)
        at = pl.multiple_of(device * share, share)
        msg_ref[pl.ds(at, share), :] = ref[pl.ds(0, share), :]
        in_ref[pl.ds(pl.multiple_of(2 * at, 2 * share), 2 * share), :] = ref[pl.ds(share, 2 * share), :]
        out_w_ref[pl.ds(at, share), :] = ref[pl.ds(3 * share, share), :]
        lines = ref[pl.ds(4 * share, 16), :].astype(F32)
        gain = jnp.where((lane >= at) & (lane < at + share), lines[0:1, :], gain)
        dst, src, count = (lines[i : i + 1, :].astype(jnp.int32) for i in (1, 2, 3))
        block = src - me * here_blocks
        used = (lane < count) & (block >= 0) & (block < here_blocks)
        is_rim = block >= own_blocks
        place = jnp.where(is_rim, block - own_blocks, block)
        code = lane + (place << 7) + (dst << 13) + jnp.where(is_rim, 2 << 20, 1 << 20)
        code_ref[k : k + 1, :] = jnp.where(used, code, 0)
        code_ref[parties + k : parties + k + 1, :] = count
    gain_ref[...] = gain
    half = low_ref.shape[0]
    w_msg = msg_ref[...]
    for k, ref in enumerate((low_ref, high_ref)):
        pre = rows_by_cols(picked_ref[pl.ds(k * half, half), :], w_msg)
        ref[...] = (pre * sigmoid(pre)).astype(BF16)


def prepare(position, smalls, picked, own_blocks, here_blocks):
    half = picked.shape[0] // 2
    return pl.pallas_call(
        functools.partial(prepare_kernel, own_blocks, here_blocks),
        out_shape=(
            jax.ShapeDtypeStruct((half, SIDE), BF16),
            jax.ShapeDtypeStruct((half, SIDE), BF16),
            jax.ShapeDtypeStruct((SIDE, SIDE), BF16),
            jax.ShapeDtypeStruct((2 * SIDE, SIDE), BF16),
            jax.ShapeDtypeStruct((SIDE, SIDE), BF16),
            jax.ShapeDtypeStruct((1, SIDE), F32),
            jax.ShapeDtypeStruct((8, SIDE), jnp.int32),
        ),
        in_specs=[SMEM] + [VMEM] * 5,
        out_specs=(VMEM,) * 7,
        compiler_params=ROOMY,
        name="prepare",
    )(position, *smalls, picked)


def message_kernel(feat_ref, msg_ref, *rest):
    out_ref = rest[-1]
    pre = rows_by_cols(feat_ref[...], msg_ref[...])
    out_ref[...] = (pre * sigmoid(pre)).astype(BF16)


def messages(feat, w_msg, follow):
    rows = feat.shape[0]
    steps = 2
    tall = pl.BlockSpec((rows // steps, SIDE), lambda i: (i, 0))
    return pl.pallas_call(
        message_kernel,
        grid=(steps,),
        out_shape=jax.ShapeDtypeStruct((rows, SIDE), BF16),
        in_specs=[tall, pl.BlockSpec(w_msg.shape, lambda i: (0, 0))] + [ANY] * len(follow),
        out_specs=tall,
        compiler_params=PARAMS,
        name="messages",
    )(feat, w_msg, *follow)


def list_kernel(ks, code_ref, *rest):
    list_ref, total_ref = rest[-2:]
    parties = code_ref.shape[0] // 2
    group = 8
    for k in ks:

        def body(step, carry):
            own, rim = carry
            codes = [code_ref[k, step * group + u] for u in range(group)]
            for code in codes:
                list_ref[2 * k, own] = code
                list_ref[2 * k + 1, rim] = code
                own = own + ((code >> 20) & 1)
                rim = rim + (code >> 21)
            return (own, rim)

        steps = (code_ref[parties + k, 0] + group - 1) // group
        own, rim = lax.fori_loop(0, steps, body, (jnp.int32(0), jnp.int32(0)))
        total_ref[2 * k] = own
        total_ref[2 * k + 1] = rim


def build_lists(ks, codes, follow):
    parties, slots = codes.shape[0] // 2, codes.shape[1]
    return pl.pallas_call(
        functools.partial(list_kernel, ks),
        out_shape=(
            jax.ShapeDtypeStruct((2 * parties, slots + 16), jnp.int32),
            jax.ShapeDtypeStruct((2 * parties,), jnp.int32),
        ),
        in_specs=[SMEM] + [ANY] * len(follow),
        out_specs=(SMEM, SMEM),
        compiler_params=SMALL,
        name="tile_lists",
    )(codes, *follow)


def dense_tile(tiles_ref, slot, keep):
    column = lax.broadcasted_iota(jnp.int32, (SIDE, SIDE), 0).astype(F32)
    edges = tiles_ref.shape[0] // 2
    entries = edges // SIDE
    total = None
    for e in range(entries):
        at = slot * entries + e
        weight = tiles_ref[pl.ds(at, 1), :] * keep
        term = jnp.where(column == tiles_ref[pl.ds(edges + at, 1), :], weight, 0.0)
        total = term if total is None else total + term
    return total.astype(BF16)


def walk_list(list_ref, total_ref, which, tiles_ref, product, acc):
    count = total_ref[which]

    def body(step, carry):
        found = []
        for u in range(UNROLL):
            index = step * UNROLL + u
            used = index < count
            entry = jnp.where(used, list_ref[which, index], 0)
            dense = dense_tile(tiles_ref, entry & 127, jnp.where(used, 1.0, 0.0))
            found.append(product(dense, (entry >> 7) & 63, (entry >> 13) & 31))
        for target, value in found:
            acc[target] += value
        return carry

    lax.fori_loop(0, (count + UNROLL - 1) // UNROLL, body, 0)


def forward_kernel(ks, list_ref, total_ref, own_ref, lower_ref, upper_ref, *rest):
    slot_refs, rest = rest[: len(ks)], rest[len(ks) :]
    outs, (token_ref, acc, rims, tiles) = rest[:-4], rest[-4:]
    token_ref[...] = jnp.zeros_like(token_ref)
    half = lower_ref.shape[0]
    rims[pl.ds(0, half)] = lower_ref[...]
    rims[pl.ds(half, half)] = upper_ref[...]
    for at, (k, slot_ref) in enumerate(zip(ks, slot_refs)):
        acc[...] = jnp.zeros_like(acc)
        tiles[...] = slot_ref[...].astype(F32)
        for part, ref in enumerate((own_ref, rims)):

            def product(dense, block, target, ref=ref):
                return (target, contract_rows(dense, ref[block]))

            walk_list(list_ref, total_ref, 2 * k + part, tiles, product, acc)
        for h in range(2):
            out_ref = outs[2 * at + h]
            span = out_ref.shape[0]
            out_ref[...] = acc[pl.ds(h * span, span)].astype(out_ref.dtype)


def forward_tiles(ks, lists, totals, own, lower, upper, tiles, kind):
    blocks = own.shape[0]
    half = jax.ShapeDtypeStruct((blocks // 2,) + own.shape[1:], kind)
    return pl.pallas_call(
        functools.partial(forward_kernel, ks),
        out_shape=(half,) * (2 * len(ks)) + (jax.ShapeDtypeStruct((8, SIDE), F32),),
        in_specs=[SMEM, SMEM] + [VMEM] * (3 + len(ks)),
        out_specs=(VMEM,) * (2 * len(ks) + 1),
        scratch_shapes=[
            pltpu.VMEM(own.shape, F32),
            pltpu.VMEM((2 * lower.shape[0],) + lower.shape[1:], BF16),
            pltpu.VMEM(tiles[0].shape, F32),
        ],
        compiler_params=PARAMS,
        cost_estimate=cost(1_000_000_000 * len(ks), 4_000_000 * len(ks)),
        name="forward_tiles",
    )(lists, totals, own, lower, upper, *[tiles[k] for k in ks])


def join_kernel(after_ref, left_ref, prior_ref, right_ref, *outs):
    for mine, theirs, out_ref in ((after_ref, left_ref, outs[0]), (prior_ref, right_ref, outs[1])):
        out_ref[...] = (mine[...].astype(F32) + theirs[...].astype(F32)).astype(BF16)


def join(after, from_left, prior, from_right):
    kind = jax.ShapeDtypeStruct(after.shape, BF16)
    return pl.pallas_call(
        join_kernel,
        out_shape=(kind, kind),
        in_specs=[VMEM] * 4,
        out_specs=(VMEM, VMEM),
        compiler_params=PARAMS,
        name="join",
    )(after, from_left, prior, from_right)


def node_kernel(
    continued, feat_ref, cot_ref, own_ref, left_ref, right_ref, in_ref, out_w_ref, gain_ref, *rest,
):
    node_ref, dhid_ref, dagg_ref, dwin_ref, dwout_ref, dgain_ref = rest[-6:]
    step = pl.program_id(0)

    @pl.when(step == 0)
    def _():
        for at, ref in enumerate((dwin_ref, dwout_ref, dgain_ref)):
            ref[...] = rest[2 + at][...] if continued else jnp.zeros_like(ref)

    feat = feat_ref[...]
    agg = (own_ref[...] + (left_ref[...].astype(F32) + right_ref[...].astype(F32))).astype(BF16)
    w_feat, w_agg, w_out = in_ref[:SIDE, :], in_ref[SIDE:, :], out_w_ref[...]
    gain = gain_ref[...]
    pre = rows_by_cols(feat, w_feat) + rows_by_cols(agg, w_agg)
    logistic = sigmoid(pre)
    hidden = (pre * logistic).astype(BF16)
    slope = logistic * (1.0 + pre * (1.0 - logistic))
    update = rows_by_cols(hidden, w_out)
    centre = update - jnp.mean(update, axis=-1, keepdims=True)
    inverse = lax.rsqrt(jnp.mean(centre * centre, axis=-1, keepdims=True) + 1e-05)
    normed = centre * inverse
    node_ref[...] = (feat.astype(F32) + gain * normed).astype(BF16)
    upstream = cot_ref[...].astype(F32)
    d_normed = upstream * gain
    dgain_ref[...] += jnp.sum(upstream * normed, axis=0, keepdims=True)
    d_update = (
        d_normed
        - jnp.mean(d_normed, axis=-1, keepdims=True)
        - normed * jnp.mean(d_normed * normed, axis=-1, keepdims=True)
    ) * inverse
    d_update = d_update.astype(BF16)
    d_hidden = (contract_cols(d_update, w_out) * slope).astype(BF16)
    dhid_ref[...] = d_hidden
    dagg_ref[...] = contract_cols(d_hidden, w_agg).astype(BF16)
    dwout_ref[...] += contract_rows(hidden, d_update)
    dwin_ref[:SIDE, :] += contract_rows(feat, d_hidden)
    dwin_ref[SIDE:, :] += contract_rows(agg, d_hidden)


def node_update(h, node_feat, cotangent, parts, w_in, w_out, gain, before, follow):
    rows = node_feat.shape[0]
    chunk = 512
    steps = rows // 2 // chunk

    def whole(shape):
        return pl.BlockSpec(shape, lambda i: (0, 0))

    tall = pl.BlockSpec((chunk, SIDE), lambda i: (h * steps + i, 0))
    part = pl.BlockSpec((chunk, SIDE), lambda i: (i, 0))
    wide = jax.ShapeDtypeStruct((rows, SIDE), BF16)
    half = jax.ShapeDtypeStruct((rows // 2, SIDE), BF16)
    sums = [(2 * SIDE, SIDE), (SIDE, SIDE), (1, SIDE)]
    return pl.pallas_call(
        functools.partial(node_kernel, bool(before)),
        grid=(steps,),
        out_shape=(wide, wide, half) + tuple(jax.ShapeDtypeStruct(shape, F32) for shape in sums),
        in_specs=[tall, tall, part, part, part]
        + [whole((2 * SIDE, SIDE)), whole((SIDE, SIDE)), whole((1, SIDE))]
        + ([ANY, ANY] + [whole(shape) for shape in sums] if before else [])
        + [ANY] * len(follow),
        out_specs=(tall, tall, part) + tuple(whole(shape) for shape in sums),
        input_output_aliases={8: 0, 9: 1} if before else {},
        compiler_params=PARAMS,
        cost_estimate=cost(5_000_000_000, 10_000_000),
        name="node_update",
    )(node_feat, cotangent, *parts, w_in, w_out, gain, *before, *follow)


def ahead_kernel(feat_ref, cot_ref, dhid_ref, picked_ref, msg_ref, in_ref, slope_ref, base_ref, far_ref):
    w_msg = msg_ref[...]
    slope_ref[...] = silu_slope(rows_by_cols(feat_ref[...], w_msg))
    far_ref[...] = silu_slope(rows_by_cols(picked_ref[...], w_msg))
    base_ref[...] = cot_ref[...].astype(F32) + contract_cols(dhid_ref[...], in_ref[:SIDE, :])


def ahead(feat, cot, dhid, picked, w_msg, w_in):
    rows = feat.shape[0]
    steps = 4
    tall = pl.BlockSpec((rows // steps, SIDE), lambda i: (i, 0))
    short = pl.BlockSpec((picked.shape[0] // steps, SIDE), lambda i: (i, 0))
    wide = jax.ShapeDtypeStruct((rows, SIDE), F32)
    return pl.pallas_call(
        ahead_kernel,
        grid=(steps,),
        out_shape=(wide, wide, jax.ShapeDtypeStruct(picked.shape, F32)),
        in_specs=[tall] * 3 + [short] + [pl.BlockSpec(w.shape, lambda i: (0, 0)) for w in (w_msg, w_in)],
        out_specs=(tall, tall, short),
        compiler_params=PARAMS,
        cost_estimate=cost(3_000_000_000, 7_000_000),
        name="ahead",
    )(feat, cot, dhid, picked, w_msg, w_in)


def backward_kernel(ks, cuts, parts, started, list_ref, total_ref, *rest):
    slot_refs, rest = rest[: len(ks)], rest[len(ks) :]
    tiles, grads, accs = rest[-2 - len(parts)], rest[-1 - len(parts)], rest[-len(parts) :]
    arrays, rest = rest[: cuts * len(ks)], rest[cuts * len(ks) : -2 - len(parts)]
    for at, acc in enumerate(accs):
        acc[...] = rest[at][...] if started else jnp.zeros_like(acc)
    for at, (k, slot_ref) in enumerate(zip(ks, slot_refs)):
        tiles[...] = slot_ref[...].astype(F32)
        source = arrays[at]
        if cuts > 1:
            source, span = grads, grads.shape[0] // cuts
            for c in range(cuts):
                grads[pl.ds(c * span, span)] = arrays[cuts * at + c][...]

        def product(dense, block, target, source=source):
            return (block, rows_by_cols(dense, source[target]))

        for part, acc in zip(parts, accs):
            walk_list(list_ref, total_ref, 2 * k + part, tiles, product, acc)
    if parts == (1,):
        half = accs[0].shape[0] // 2
        for at, out_ref in enumerate(rest[-2:]):
            out_ref[...] = accs[0][pl.ds(at * half, half)].astype(out_ref.dtype)
    else:
        for out_ref, acc in zip(rest[-len(parts) :], accs):
            out_ref[...] = acc[...]


def backward_tiles(ks, lists, parts, sizes, kinds, tiles, arrays, started, follow=()):
    cuts = len(arrays[0])
    cubes = [array.reshape(-1, SIDE, SIDE) for group in arrays for array in group]
    accs = [sum(sizes)] if len(sizes) > len(parts) else sizes
    return pl.pallas_call(
        functools.partial(backward_kernel, ks, cuts, parts, bool(started)),
        out_shape=tuple(jax.ShapeDtypeStruct((size, SIDE, SIDE), kind) for size, kind in zip(sizes, kinds)),
        in_specs=[SMEM, SMEM] + [VMEM] * (len(ks) + len(cubes) + len(started)) + [ANY] * len(follow),
        out_specs=(VMEM,) * len(sizes),
        scratch_shapes=[pltpu.VMEM(tiles[0].shape, F32), pltpu.VMEM((cuts * cubes[0].shape[0], SIDE, SIDE), BF16)]
        + [pltpu.VMEM((size, SIDE, SIDE), F32) for size in accs],
        compiler_params=PARAMS,
        cost_estimate=cost(2_000_000_000 * len(ks), 4_000_000),
        name="backward_tiles",
    )(*lists, *[tiles[k] for k in ks], *cubes, *started, *follow)


def own_kernel(feat_ref, slope_ref, base_ref, own_ref, msg_ref, sum_ref, dw_ref):
    @pl.when(pl.program_id(0) == 0)
    def _():
        dw_ref[...] = jnp.zeros_like(dw_ref)

    d_pre = (own_ref[...] * slope_ref[...]).astype(BF16)
    dw_ref[...] += contract_rows(feat_ref[...], d_pre)
    sum_ref[...] = base_ref[...] + contract_cols(d_pre, msg_ref[...])


def own_products(feat, slope, base, own, w_msg):
    rows = feat.shape[0]
    steps = 4
    tall = pl.BlockSpec((rows // steps, SIDE), lambda i: (i, 0))
    square = pl.BlockSpec((SIDE, SIDE), lambda i: (0, 0))
    return pl.pallas_call(
        own_kernel,
        grid=(steps,),
        out_shape=(jax.ShapeDtypeStruct((rows, SIDE), F32), jax.ShapeDtypeStruct((SIDE, SIDE), F32)),
        in_specs=[tall] * 4 + [square],
        out_specs=(tall, square),
        compiler_params=PARAMS,
        cost_estimate=cost(3_000_000_000, 7_000_000),
        name="own_products",
    )(feat, slope, base, own, w_msg)


def rim_kernel(
    pos_ref, count_ref, lower_ref, upper_ref, picked_ref, far_ref, dw_ref, dwin_ref, dwout_ref, dgain_ref,
    dpre_ref, r0_ref, r1_ref, r2_ref, r3_ref, dw,
):
    halo = lower_ref.shape[0]
    dw[...] = dw_ref[...]
    for k, ref in enumerate((lower_ref, upper_ref)):
        at = pl.ds(k * halo, halo)
        slots = lax.broadcasted_iota(jnp.int32, (halo, SIDE), 0)
        d_pre = jnp.where(slots < count_ref[k], ref[...].astype(F32) * far_ref[at, :], 0.0).astype(BF16)
        dpre_ref[at, :] = d_pre
        dw[...] += contract_rows(picked_ref[at, :], d_pre)
    outs = (r0_ref, r1_ref, r2_ref, r3_ref)
    share = SIDE // len(outs)
    for k, out in enumerate(outs):
        device = lax.rem(pos_ref[0] + k, len(outs))
        start = pl.multiple_of(device * share, share)
        gain = jnp.zeros((16, SIDE), F32)
        for j in range(len(outs)):
            wide = jnp.broadcast_to(dgain_ref[...], (16, SIDE))
            gain = jnp.where(device == j, pltpu.roll(wide, (SIDE - j * share) % SIDE, 1), gain)
        out[pl.ds(0, share), :] = dw[pl.ds(start, share), :].astype(out.dtype)
        at = pl.ds(pl.multiple_of(2 * start, 2 * share), 2 * share)
        out[pl.ds(share, 2 * share), :] = dwin_ref[at, :].astype(out.dtype)
        out[pl.ds(3 * share, share), :] = dwout_ref[pl.ds(start, share), :].astype(out.dtype)
        out[pl.ds(4 * share, 16), :] = gain.astype(out.dtype)


def rim_products(position, halo_count, lower, upper, picked, far, dw, sums):
    piece = jax.ShapeDtypeStruct((SIDE + 16, SIDE), BF16)
    return pl.pallas_call(
        rim_kernel,
        out_shape=(jax.ShapeDtypeStruct(picked.shape, BF16), piece, piece, piece, piece),
        in_specs=[SMEM] * 2 + [VMEM] * 8,
        out_specs=(VMEM,) * 5,
        scratch_shapes=[pltpu.VMEM((SIDE, SIDE), F32)],
        compiler_params=PARAMS,
        name="rim_products",
    )(position, halo_count, lower, upper, picked, far, dw, *sums)


def place_kernel(k, rows_ref, count_ref, sum_ref, dpre_ref, msg_ref, *rest):
    out_ref, token_ref, acc, added = rest[-4:]
    token_ref[...] = jnp.zeros_like(token_ref)
    halo = rows_ref.shape[1]
    acc[...] = sum_ref[...]
    added[...] = contract_cols(dpre_ref[pl.ds(k * halo, halo), :], msg_ref[...])
    group = 16

    def body(step, carry):
        rows = [rows_ref[k, step * group + u] for u in range(group)]
        values = [acc[pl.ds(row, 1), :] + added[pl.ds(step * group + u, 1), :] for u, row in enumerate(rows)]
        for row, value in zip(rows, values):
            acc[pl.ds(row, 1), :] = value
        return carry

    lax.fori_loop(0, (count_ref[k] + group - 1) // group, body, 0)
    out_ref[...] = acc[...].astype(out_ref.dtype)


def place_rows(k, kind, halo_rows, halo_count, total, d_pre, w_msg, follow):
    return pl.pallas_call(
        functools.partial(place_kernel, k),
        out_shape=(jax.ShapeDtypeStruct(total.shape, kind), jax.ShapeDtypeStruct((8, SIDE), F32)),
        in_specs=[SMEM] * 2 + [VMEM] * 3 + [ANY] * len(follow),
        out_specs=(VMEM, VMEM),
        scratch_shapes=[pltpu.VMEM(total.shape, F32), pltpu.VMEM((halo_rows.shape[1], SIDE), F32)],
        compiler_params=PARAMS,
        cost_estimate=cost(4_000_000_000, 7_000_000),
        name="place_rows",
    )(halo_rows, halo_count, total, d_pre, w_msg, *follow)


def shift_wsh(value, step):
    parties = lax.axis_size("wsh")
    return lax.ppermute(value, "wsh", [(i, (i + step) % parties) for i in range(parties)])


def shift_slab(value, step):
    count = lax.axis_size("slab")
    pairs = [(i, i + step) for i in range(count) if 0 <= i + step < count]
    return lax.ppermute(value, "slab", pairs)


def sum_kernel(count, *refs):
    total = refs[0][...].astype(F32)
    for ref in refs[1:count]:
        total = total + ref[...].astype(F32)
    refs[-1][...] = total.astype(BF16)


def sum_group(terms, follow=()):
    return pl.pallas_call(
        functools.partial(sum_kernel, len(terms)),
        out_shape=jax.ShapeDtypeStruct(terms[0].shape, BF16),
        in_specs=[VMEM] * len(terms) + [ANY] * len(follow),
        out_specs=VMEM,
        compiler_params=PARAMS,
        name="sum_group",
    )(*terms, *follow)


def sum_wsh(pieces, follow):
    return sum_group([pieces[0]] + [shift_wsh(pieces[k], k) for k in range(1, len(pieces))], follow)


def sum_slab(value, stride, size, follow=()):
    count = lax.axis_size("slab")
    span = stride * size
    turns = [[(i, (i // span) * span + (i + stride * k) % span) for i in range(count)] for k in range(1, size)]
    return sum_group([value] + [lax.ppermute(value, "slab", pairs) for pairs in turns], follow)


def other_core(value):
    return lax.ppermute(value, "slab", [(i, i ^ 1) for i in range(lax.axis_size("slab"))])


def finish_kernel(one_ref, two_ref, msg_ref, in_ref, out_w_ref, gain_ref):
    share = msg_ref.shape[0]
    total = one_ref[...].astype(F32) + two_ref[...].astype(F32)
    msg_ref[...] = total[:share]
    in_ref[...] = total[share : 3 * share]
    out_w_ref[...] = total[3 * share : 4 * share]
    gain_ref[...] = total[4 * share : 4 * share + 1, :share]


def finish(one, two):
    share = SIDE // 4
    shapes = [(share, SIDE), (2 * share, SIDE), (share, SIDE), (1, share)]
    return pl.pallas_call(
        finish_kernel,
        out_shape=tuple(jax.ShapeDtypeStruct(shape, F32) for shape in shapes),
        in_specs=[VMEM, VMEM],
        out_specs=(VMEM,) * 4,
        compiler_params=SMALL,
        name="finish",
    )(one, two)


def on_device(
    node_feat, cotangent, w_msg, w_in, w_out, ln_gain,
    tile_values, tile_cols, tile_dst, tile_src, tile_count, halo_rows, halo_count,
):
    node_rows = node_feat.shape[0]
    slots, entries, side = tile_values.shape
    halo = halo_rows.shape[2]
    parties = lax.axis_size("wsh")
    me = lax.axis_index("wsh").astype(jnp.int32)
    position = me.reshape(1)
    share = w_msg.shape[0]
    own_blocks = node_rows // side
    rim_blocks = 2 * halo // side

    tile, small = pack_shares(tile_count, tile_values, tile_cols, w_msg, w_in, w_out, ln_gain, tile_dst, tile_src)
    smalls = [small] + [shift_wsh(small, -k) for k in range(1, parties)]
    tiles = [tile] + [shift_wsh(tile, -k) for k in range(1, parties)]

    rows = halo_rows.reshape(2, halo)
    counts = halo_count.reshape(2)
    picked = pick_rows(rows, counts, node_feat)
    low, high, full_msg, full_in, full_out, gain, codes = prepare(
        position, smalls, picked, own_blocks, own_blocks + rim_blocks
    )
    lower = shift_slab(high, 1).reshape(rim_blocks // 2, side, side)
    upper = shift_slab(low, -1).reshape(rim_blocks // 2, side, side)
    message = messages(node_feat, full_msg, tiles[1:])
    far_lists = build_lists((2,), codes, ())
    forward = functools.partial(
        forward_tiles, own=message.reshape(own_blocks, side, side), lower=lower,
        upper=upper, tiles=tiles,
    )

    far_first, far_second, token = forward((2,), *far_lists, kind=BF16)
    lists = build_lists((0, 1, 3), codes, (token,))
    from_right = shift_wsh(far_first, -1)
    from_left = shift_wsh(far_second, 1)
    after_first, after_second, prior_first, prior_second, _ = forward((1, 3), *lists, kind=BF16)
    left_first = shift_wsh(after_first, 1)
    right_second = shift_wsh(prior_second, -1)
    mine_first, mine_second, _ = forward((0,), *lists, kind=F32)
    to_after, to_prior = join(after_second, from_left, prior_first, from_right)
    left_second = shift_wsh(to_after, 1)
    right_first = shift_wsh(to_prior, -1)
    parts = ((mine_first, left_first, right_first), (mine_second, left_second, right_second))
    before, d_agg, from_prior, from_after = (), [], [], []
    for h in (0, 1):
        pieces = [part.reshape(-1, side) for part in parts[h]]
        node_out, d_hidden, half, *sums = node_update(
            h, node_feat, cotangent, pieces, full_in, full_out, gain, before, from_prior
        )
        before = (node_out, d_hidden, *sums)
        d_agg.append(half)
        from_prior.append(shift_wsh(half, 1))
        from_after.append(shift_wsh(half, -1))
    quarter = node_rows // 4
    far = []
    for h in (0, 1):
        far.append(shift_wsh(from_prior[h][:quarter], 1))
        far.append(shift_wsh(from_after[h][quarter:], -1))
    slope, base, far_slope = ahead(node_feat, cotangent, d_hidden, picked, full_msg, full_in)

    backward = functools.partial(backward_tiles, tiles=tiles)
    own_part, rim_part = backward(
        (0, 1, 3), lists, (0, 1), (own_blocks, rim_blocks), (F32, F32), arrays=(d_agg, from_after, from_prior),
        started=(),
    )
    back_low, back_high = backward(
        (2,), far_lists, (1,), (rim_blocks // 2,) * 2, (BF16,) * 2, arrays=(far,), started=(rim_part,), follow=(slope,)
    )
    back_upper = shift_slab(back_low.reshape(halo, side), -1)
    back_lower = shift_slab(back_high.reshape(halo, side), 1)
    (d_own,) = backward((2,), far_lists, (0,), (own_blocks,), (F32,), arrays=(far,), started=(own_part,))
    total, d_w_own = own_products(node_feat, slope, base, d_own.reshape(node_rows, side), full_msg)
    d_pre, *pieces = rim_products(
        position, counts, back_lower, back_upper, picked, far_slope, d_w_own, sums
    )
    place = functools.partial(place_rows, halo_rows=rows, halo_count=counts, d_pre=d_pre, w_msg=full_msg)
    total, token = place(0, F32, total=total, follow=())
    value = sum_wsh(pieces, (token,))
    d_node, token = place(1, BF16, total=total, follow=(value,))
    value = sum_slab(value, 8, 4, (token,))
    value = sum_slab(value, 2, 4)
    d_w_msg, d_w_in, d_w_out, d_gain = finish(value, other_core(value))
    return (node_out, d_node, d_w_msg, d_w_in, d_w_out, d_gain.reshape(share))


def solution(mesh):
    both = ("slab", "wsh")
    tall, split, line = P(both, None), P("wsh", None), P(both)
    cube = P(both, None, None)
    return jax.shard_map(
        on_device,
        mesh=mesh,
        in_specs=(
            tall, tall, split, split, split, P("wsh"), cube, cube, line, line, line, cube, tall,
        ),
        out_specs=(tall, tall, split, split, split, P("wsh")),
        check_vma=False,
    )
```

```python
import functools

import jax
import jax.numpy as jnp
from jax import lax
from jax.experimental import pallas as pl
from jax.experimental.pallas import tpu as pltpu
from jax.sharding import PartitionSpec as P

F32 = jnp.float32
BF16 = jnp.bfloat16
SIDE = 128
UNROLL = 8
PARAMS = pltpu.CompilerParams(vmem_limit_bytes=16 * 2**20)
SMALL = pltpu.CompilerParams(vmem_limit_bytes=4 * 2**20)
ROOMY = pltpu.CompilerParams(vmem_limit_bytes=60 * 2**20)
VMEM = pl.BlockSpec(memory_space=pltpu.VMEM)
SMEM = pl.BlockSpec(memory_space=pltpu.SMEM)
ANY = pl.BlockSpec(memory_space=pl.ANY)


def cost(flops, size):
    return pl.CostEstimate(flops=flops, bytes_accessed=size, transcendentals=0)


def dot(left, right, dims):
    return lax.dot_general(left, right, (dims, ((), ())), preferred_element_type=F32)


def rows_by_cols(left, right):
    return dot(left, right, ((1,), (0,)))


def contract_rows(left, right):
    return dot(left, right, ((0,), (0,)))


def contract_cols(left, right):
    return dot(left, right, ((1,), (1,)))


def sigmoid(v):
    return 1.0 / (1.0 + jnp.exp(-v))


def silu_slope(v):
    g = sigmoid(v)
    return g * (1.0 + v * (1.0 - g))


def pick_kernel(rows_ref, count_ref, feat_ref, out_ref, wide, picked):
    halo = rows_ref.shape[1]
    wide[...] = feat_ref[...].astype(F32)
    group = 16
    for k in range(2):
        count = count_ref[k]

        def body(step, carry):
            for u in range(group):
                slot = step * group + u
                row = rows_ref[k, slot]
                picked[pl.ds(slot, 1), :] = wide[pl.ds(row, 1), :]
            return carry

        lax.fori_loop(0, (count + group - 1) // group, body, 0)
        slots = lax.broadcasted_iota(jnp.int32, (halo, SIDE), 0)
        kept = jnp.where(slots < count, picked[...], 0.0)
        out_ref[pl.ds(k * halo, halo), :] = kept.astype(BF16)


def pick_rows(halo_rows, halo_count, node_feat):
    halo = halo_rows.shape[1]
    return pl.pallas_call(
        pick_kernel,
        out_shape=jax.ShapeDtypeStruct((2 * halo, SIDE), BF16),
        in_specs=[SMEM, SMEM, VMEM],
        out_specs=VMEM,
        scratch_shapes=[pltpu.VMEM(node_feat.shape, F32), pltpu.VMEM((halo, SIDE), F32)],
        compiler_params=ROOMY,
        name="pick_rows",
    )(halo_rows, halo_count, node_feat)


def pack_kernel(
    count_ref, values_ref, cols_ref, msg_ref, in_ref, out_w_ref, gain_ref, dst_ref, src_ref, tiles_ref, pack_ref, lines
):
    share, edges = msg_ref.shape[0], values_ref.shape[0]
    tiles_ref[pl.ds(0, edges), :] = values_ref[...]
    tiles_ref[pl.ds(edges, edges), :] = cols_ref[...].astype(F32).astype(BF16)
    pack_ref[pl.ds(0, share), :] = msg_ref[...]
    pack_ref[pl.ds(share, 2 * share), :] = in_ref[...]
    pack_ref[pl.ds(3 * share, share), :] = out_w_ref[...]
    lines[...] = jnp.zeros_like(lines)
    gain = gain_ref[...].astype(F32)
    for j in range(SIDE // share):
        lines[0:1, j * share : (j + 1) * share] = gain
    lines[1:2, :] = dst_ref[...].astype(F32)
    lines[2:3, :] = src_ref[...].astype(F32)
    lines[3:4, :] = jnp.full((1, SIDE), count_ref[0]).astype(F32)
    pack_ref[pl.ds(4 * share, 16), :] = lines[...].astype(BF16)


def pack_shares(tile_count, tile_values, tile_cols, w_msg, w_in, w_out, ln_gain, tile_dst, tile_src):
    share = w_msg.shape[0]
    values, cols = (array.reshape(-1, SIDE) for array in (tile_values, tile_cols))
    return pl.pallas_call(
        pack_kernel,
        out_shape=(
            jax.ShapeDtypeStruct((2 * values.shape[0], SIDE), BF16),
            jax.ShapeDtypeStruct((4 * share + 16, SIDE), BF16),
        ),
        in_specs=[SMEM] + [VMEM] * 8,
        out_specs=(VMEM, VMEM),
        scratch_shapes=[pltpu.VMEM((16, SIDE), F32)],
        compiler_params=ROOMY,
        name="pack_shares",
    )(
        tile_count, values, cols, w_msg, w_in, w_out, ln_gain.reshape(1, share), tile_dst.reshape(1, SIDE),
        tile_src.reshape(1, SIDE),
    )


def prepare_kernel(
    own_blocks, here_blocks, pos_ref, s0_ref, s1_ref, s2_ref, s3_ref, picked_ref,
    low_ref, high_ref, msg_ref, in_ref, out_w_ref, gain_ref, code_ref,
):
    me = pos_ref[0]
    smalls = (s0_ref, s1_ref, s2_ref, s3_ref)
    parties = len(smalls)
    share = SIDE // parties
    lane = lax.broadcasted_iota(jnp.int32, (1, SIDE), 1)
    gain = jnp.zeros((1, SIDE), F32)
    for k, ref in enumerate(smalls):
        device = lax.rem(me + k, parties)
        at = pl.multiple_of(device * share, share)
        msg_ref[pl.ds(at, share), :] = ref[pl.ds(0, share), :]
        in_ref[pl.ds(pl.multiple_of(2 * at, 2 * share), 2 * share), :] = ref[pl.ds(share, 2 * share), :]
        out_w_ref[pl.ds(at, share), :] = ref[pl.ds(3 * share, share), :]
        lines = ref[pl.ds(4 * share, 16), :].astype(F32)
        gain = jnp.where((lane >= at) & (lane < at + share), lines[0:1, :], gain)
        dst, src, count = (lines[i : i + 1, :].astype(jnp.int32) for i in (1, 2, 3))
        block = src - me * here_blocks
        used = (lane < count) & (block >= 0) & (block < here_blocks)
        is_rim = block >= own_blocks
        place = jnp.where(is_rim, block - own_blocks, block)
        code = lane + (place << 7) + (dst << 13) + jnp.where(is_rim, 2 << 20, 1 << 20)
        code_ref[k : k + 1, :] = jnp.where(used, code, 0)
        code_ref[parties + k : parties + k + 1, :] = count
    gain_ref[...] = gain
    half = low_ref.shape[0]
    w_msg = msg_ref[...]
    for k, ref in enumerate((low_ref, high_ref)):
        pre = rows_by_cols(picked_ref[pl.ds(k * half, half), :], w_msg)
        ref[...] = (pre * sigmoid(pre)).astype(BF16)


def prepare(position, smalls, picked, own_blocks, here_blocks):
    half = picked.shape[0] // 2
    return pl.pallas_call(
        functools.partial(prepare_kernel, own_blocks, here_blocks),
        out_shape=(
            jax.ShapeDtypeStruct((half, SIDE), BF16),
            jax.ShapeDtypeStruct((half, SIDE), BF16),
            jax.ShapeDtypeStruct((SIDE, SIDE), BF16),
            jax.ShapeDtypeStruct((2 * SIDE, SIDE), BF16),
            jax.ShapeDtypeStruct((SIDE, SIDE), BF16),
            jax.ShapeDtypeStruct((1, SIDE), F32),
            jax.ShapeDtypeStruct((8, SIDE), jnp.int32),
        ),
        in_specs=[SMEM] + [VMEM] * 5,
        out_specs=(VMEM,) * 7,
        compiler_params=ROOMY,
        name="prepare",
    )(position, *smalls, picked)


def message_kernel(feat_ref, msg_ref, *rest):
    out_ref = rest[-1]
    pre = rows_by_cols(feat_ref[...], msg_ref[...])
    out_ref[...] = (pre * sigmoid(pre)).astype(BF16)


def messages(feat, w_msg, follow):
    rows = feat.shape[0]
    steps = 2
    tall = pl.BlockSpec((rows // steps, SIDE), lambda i: (i, 0))
    return pl.pallas_call(
        message_kernel,
        grid=(steps,),
        out_shape=jax.ShapeDtypeStruct((rows, SIDE), BF16),
        in_specs=[tall, pl.BlockSpec(w_msg.shape, lambda i: (0, 0))] + [ANY] * len(follow),
        out_specs=tall,
        compiler_params=PARAMS,
        name="messages",
    )(feat, w_msg, *follow)


def list_kernel(ks, code_ref, *rest):
    list_ref, total_ref = rest[-2:]
    parties = code_ref.shape[0] // 2
    group = 8
    for k in ks:

        def body(step, carry):
            own, rim = carry
            codes = [code_ref[k, step * group + u] for u in range(group)]
            for code in codes:
                list_ref[2 * k, own] = code
                list_ref[2 * k + 1, rim] = code
                own = own + ((code >> 20) & 1)
                rim = rim + (code >> 21)
            return (own, rim)

        steps = (code_ref[parties + k, 0] + group - 1) // group
        own, rim = lax.fori_loop(0, steps, body, (jnp.int32(0), jnp.int32(0)))
        total_ref[2 * k] = own
        total_ref[2 * k + 1] = rim


def build_lists(ks, codes, follow):
    parties, slots = codes.shape[0] // 2, codes.shape[1]
    return pl.pallas_call(
        functools.partial(list_kernel, ks),
        out_shape=(
            jax.ShapeDtypeStruct((2 * parties, slots + 16), jnp.int32),
            jax.ShapeDtypeStruct((2 * parties,), jnp.int32),
        ),
        in_specs=[SMEM] + [ANY] * len(follow),
        out_specs=(SMEM, SMEM),
        compiler_params=SMALL,
        name="tile_lists",
    )(codes, *follow)


def dense_tile(tiles_ref, slot, keep):
    column = lax.broadcasted_iota(jnp.int32, (SIDE, SIDE), 0).astype(F32)
    edges = tiles_ref.shape[0] // 2
    entries = edges // SIDE
    total = None
    for e in range(entries):
        at = slot * entries + e
        weight = tiles_ref[pl.ds(at, 1), :] * keep
        term = jnp.where(column == tiles_ref[pl.ds(edges + at, 1), :], weight, 0.0)
        total = term if total is None else total + term
    return total.astype(BF16)


def walk_list(list_ref, total_ref, which, tiles_ref, product, acc):
    count = total_ref[which]

    def body(step, carry):
        found = []
        for u in range(UNROLL):
            index = step * UNROLL + u
            used = index < count
            entry = jnp.where(used, list_ref[which, index], 0)
            dense = dense_tile(tiles_ref, entry & 127, jnp.where(used, 1.0, 0.0))
            found.append(product(dense, (entry >> 7) & 63, (entry >> 13) & 31))
        for target, value in found:
            acc[target] += value
        return carry

    lax.fori_loop(0, (count + UNROLL - 1) // UNROLL, body, 0)


def forward_kernel(ks, list_ref, total_ref, own_ref, lower_ref, upper_ref, *rest):
    slot_refs, rest = rest[: len(ks)], rest[len(ks) :]
    outs, (token_ref, acc, rims, tiles) = rest[:-4], rest[-4:]
    token_ref[...] = jnp.zeros_like(token_ref)
    half = lower_ref.shape[0]
    rims[pl.ds(0, half)] = lower_ref[...]
    rims[pl.ds(half, half)] = upper_ref[...]
    for at, (k, slot_ref) in enumerate(zip(ks, slot_refs)):
        acc[...] = jnp.zeros_like(acc)
        tiles[...] = slot_ref[...].astype(F32)
        for part, ref in enumerate((own_ref, rims)):

            def product(dense, block, target, ref=ref):
                return (target, contract_rows(dense, ref[block]))

            walk_list(list_ref, total_ref, 2 * k + part, tiles, product, acc)
        for h in range(2):
            out_ref = outs[2 * at + h]
            span = out_ref.shape[0]
            out_ref[...] = acc[pl.ds(h * span, span)].astype(out_ref.dtype)


def forward_tiles(ks, lists, totals, own, lower, upper, tiles, kind):
    blocks = own.shape[0]
    half = jax.ShapeDtypeStruct((blocks // 2,) + own.shape[1:], kind)
    return pl.pallas_call(
        functools.partial(forward_kernel, ks),
        out_shape=(half,) * (2 * len(ks)) + (jax.ShapeDtypeStruct((8, SIDE), F32),),
        in_specs=[SMEM, SMEM] + [VMEM] * (3 + len(ks)),
        out_specs=(VMEM,) * (2 * len(ks) + 1),
        scratch_shapes=[
            pltpu.VMEM(own.shape, F32),
            pltpu.VMEM((2 * lower.shape[0],) + lower.shape[1:], BF16),
            pltpu.VMEM(tiles[0].shape, F32),
        ],
        compiler_params=PARAMS,
        cost_estimate=cost(1_000_000_000 * len(ks), 4_000_000 * len(ks)),
        name="forward_tiles",
    )(lists, totals, own, lower, upper, *[tiles[k] for k in ks])


def join_kernel(after_ref, left_ref, prior_ref, right_ref, *outs):
    for mine, theirs, out_ref in ((after_ref, left_ref, outs[0]), (prior_ref, right_ref, outs[1])):
        out_ref[...] = (mine[...].astype(F32) + theirs[...].astype(F32)).astype(BF16)


def join(after, from_left, prior, from_right):
    kind = jax.ShapeDtypeStruct(after.shape, BF16)
    return pl.pallas_call(
        join_kernel,
        out_shape=(kind, kind),
        in_specs=[VMEM] * 4,
        out_specs=(VMEM, VMEM),
        compiler_params=PARAMS,
        name="join",
    )(after, from_left, prior, from_right)


def node_kernel(
    continued, feat_ref, cot_ref, own_ref, left_ref, right_ref, in_ref, out_w_ref, gain_ref, *rest,
):
    node_ref, dhid_ref, dagg_ref, dwin_ref, dwout_ref, dgain_ref = rest[-6:]
    step = pl.program_id(0)

    @pl.when(step == 0)
    def _():
        for at, ref in enumerate((dwin_ref, dwout_ref, dgain_ref)):
            ref[...] = rest[2 + at][...] if continued else jnp.zeros_like(ref)

    feat = feat_ref[...]
    agg = (own_ref[...] + (left_ref[...].astype(F32) + right_ref[...].astype(F32))).astype(BF16)
    w_feat, w_agg, w_out = in_ref[:SIDE, :], in_ref[SIDE:, :], out_w_ref[...]
    gain = gain_ref[...]
    pre = rows_by_cols(feat, w_feat) + rows_by_cols(agg, w_agg)
    logistic = sigmoid(pre)
    hidden = (pre * logistic).astype(BF16)
    slope = logistic * (1.0 + pre * (1.0 - logistic))
    update = rows_by_cols(hidden, w_out)
    centre = update - jnp.mean(update, axis=-1, keepdims=True)
    inverse = lax.rsqrt(jnp.mean(centre * centre, axis=-1, keepdims=True) + 1e-05)
    normed = centre * inverse
    node_ref[...] = (feat.astype(F32) + gain * normed).astype(BF16)
    upstream = cot_ref[...].astype(F32)
    d_normed = upstream * gain
    dgain_ref[...] += jnp.sum(upstream * normed, axis=0, keepdims=True)
    d_update = (
        d_normed
        - jnp.mean(d_normed, axis=-1, keepdims=True)
        - normed * jnp.mean(d_normed * normed, axis=-1, keepdims=True)
    ) * inverse
    d_update = d_update.astype(BF16)
    d_hidden = (contract_cols(d_update, w_out) * slope).astype(BF16)
    dhid_ref[...] = d_hidden
    dagg_ref[...] = contract_cols(d_hidden, w_agg).astype(BF16)
    dwout_ref[...] += contract_rows(hidden, d_update)
    dwin_ref[:SIDE, :] += contract_rows(feat, d_hidden)
    dwin_ref[SIDE:, :] += contract_rows(agg, d_hidden)


def node_update(h, node_feat, cotangent, parts, w_in, w_out, gain, before, follow):
    rows = node_feat.shape[0]
    chunk = 512
    steps = rows // 2 // chunk

    def whole(shape):
        return pl.BlockSpec(shape, lambda i: (0, 0))

    tall = pl.BlockSpec((chunk, SIDE), lambda i: (h * steps + i, 0))
    part = pl.BlockSpec((chunk, SIDE), lambda i: (i, 0))
    wide = jax.ShapeDtypeStruct((rows, SIDE), BF16)
    half = jax.ShapeDtypeStruct((rows // 2, SIDE), BF16)
    sums = [(2 * SIDE, SIDE), (SIDE, SIDE), (1, SIDE)]
    return pl.pallas_call(
        functools.partial(node_kernel, bool(before)),
        grid=(steps,),
        out_shape=(wide, wide, half) + tuple(jax.ShapeDtypeStruct(shape, F32) for shape in sums),
        in_specs=[tall, tall, part, part, part]
        + [whole((2 * SIDE, SIDE)), whole((SIDE, SIDE)), whole((1, SIDE))]
        + ([ANY, ANY] + [whole(shape) for shape in sums] if before else [])
        + [ANY] * len(follow),
        out_specs=(tall, tall, part) + tuple(whole(shape) for shape in sums),
        input_output_aliases={8: 0, 9: 1} if before else {},
        compiler_params=PARAMS,
        cost_estimate=cost(5_000_000_000, 10_000_000),
        name="node_update",
    )(node_feat, cotangent, *parts, w_in, w_out, gain, *before, *follow)


def ahead_kernel(feat_ref, cot_ref, dhid_ref, picked_ref, msg_ref, in_ref, slope_ref, base_ref, far_ref):
    w_msg = msg_ref[...]
    slope_ref[...] = silu_slope(rows_by_cols(feat_ref[...], w_msg))
    far_ref[...] = silu_slope(rows_by_cols(picked_ref[...], w_msg))
    base_ref[...] = cot_ref[...].astype(F32) + contract_cols(dhid_ref[...], in_ref[:SIDE, :])


def ahead(feat, cot, dhid, picked, w_msg, w_in):
    rows = feat.shape[0]
    steps = 4
    tall = pl.BlockSpec((rows // steps, SIDE), lambda i: (i, 0))
    short = pl.BlockSpec((picked.shape[0] // steps, SIDE), lambda i: (i, 0))
    wide = jax.ShapeDtypeStruct((rows, SIDE), F32)
    return pl.pallas_call(
        ahead_kernel,
        grid=(steps,),
        out_shape=(wide, wide, jax.ShapeDtypeStruct(picked.shape, F32)),
        in_specs=[tall] * 3 + [short] + [pl.BlockSpec(w.shape, lambda i: (0, 0)) for w in (w_msg, w_in)],
        out_specs=(tall, tall, short),
        compiler_params=PARAMS,
        cost_estimate=cost(3_000_000_000, 7_000_000),
        name="ahead",
    )(feat, cot, dhid, picked, w_msg, w_in)


def backward_kernel(ks, cuts, parts, started, list_ref, total_ref, *rest):
    slot_refs, rest = rest[: len(ks)], rest[len(ks) :]
    tiles, grads, accs = rest[-2 - len(parts)], rest[-1 - len(parts)], rest[-len(parts) :]
    arrays, rest = rest[: cuts * len(ks)], rest[cuts * len(ks) : -2 - len(parts)]
    for at, acc in enumerate(accs):
        acc[...] = rest[at][...] if started else jnp.zeros_like(acc)
    for at, (k, slot_ref) in enumerate(zip(ks, slot_refs)):
        tiles[...] = slot_ref[...].astype(F32)
        source = arrays[at]
        if cuts > 1:
            source, span = grads, grads.shape[0] // cuts
            for c in range(cuts):
                grads[pl.ds(c * span, span)] = arrays[cuts * at + c][...]

        def product(dense, block, target, source=source):
            return (block, rows_by_cols(dense, source[target]))

        for part, acc in zip(parts, accs):
            walk_list(list_ref, total_ref, 2 * k + part, tiles, product, acc)
    if parts == (1,):
        half = accs[0].shape[0] // 2
        for at, out_ref in enumerate(rest[-2:]):
            out_ref[...] = accs[0][pl.ds(at * half, half)].astype(out_ref.dtype)
    else:
        for out_ref, acc in zip(rest[-len(parts) :], accs):
            out_ref[...] = acc[...]


def backward_tiles(ks, lists, parts, sizes, kinds, tiles, arrays, started, follow=()):
    cuts = len(arrays[0])
    cubes = [array.reshape(-1, SIDE, SIDE) for group in arrays for array in group]
    accs = [sum(sizes)] if len(sizes) > len(parts) else sizes
    return pl.pallas_call(
        functools.partial(backward_kernel, ks, cuts, parts, bool(started)),
        out_shape=tuple(jax.ShapeDtypeStruct((size, SIDE, SIDE), kind) for size, kind in zip(sizes, kinds)),
        in_specs=[SMEM, SMEM] + [VMEM] * (len(ks) + len(cubes) + len(started)) + [ANY] * len(follow),
        out_specs=(VMEM,) * len(sizes),
        scratch_shapes=[pltpu.VMEM(tiles[0].shape, F32), pltpu.VMEM((cuts * cubes[0].shape[0], SIDE, SIDE), BF16)]
        + [pltpu.VMEM((size, SIDE, SIDE), F32) for size in accs],
        compiler_params=PARAMS,
        cost_estimate=cost(2_000_000_000 * len(ks), 4_000_000),
        name="backward_tiles",
    )(*lists, *[tiles[k] for k in ks], *cubes, *started, *follow)


def own_kernel(feat_ref, slope_ref, base_ref, own_ref, msg_ref, sum_ref, dw_ref):
    @pl.when(pl.program_id(0) == 0)
    def _():
        dw_ref[...] = jnp.zeros_like(dw_ref)

    d_pre = (own_ref[...] * slope_ref[...]).astype(BF16)
    dw_ref[...] += contract_rows(feat_ref[...], d_pre)
    sum_ref[...] = base_ref[...] + contract_cols(d_pre, msg_ref[...])


def own_products(feat, slope, base, own, w_msg):
    rows = feat.shape[0]
    steps = 4
    tall = pl.BlockSpec((rows // steps, SIDE), lambda i: (i, 0))
    square = pl.BlockSpec((SIDE, SIDE), lambda i: (0, 0))
    return pl.pallas_call(
        own_kernel,
        grid=(steps,),
        out_shape=(jax.ShapeDtypeStruct((rows, SIDE), F32), jax.ShapeDtypeStruct((SIDE, SIDE), F32)),
        in_specs=[tall] * 4 + [square],
        out_specs=(tall, square),
        compiler_params=PARAMS,
        cost_estimate=cost(3_000_000_000, 7_000_000),
        name="own_products",
    )(feat, slope, base, own, w_msg)


def rim_kernel(
    pos_ref, count_ref, lower_ref, upper_ref, picked_ref, far_ref, dw_ref, dwin_ref, dwout_ref, dgain_ref,
    dpre_ref, r0_ref, r1_ref, r2_ref, r3_ref, dw,
):
    halo = lower_ref.shape[0]
    dw[...] = dw_ref[...]
    for k, ref in enumerate((lower_ref, upper_ref)):
        at = pl.ds(k * halo, halo)
        slots = lax.broadcasted_iota(jnp.int32, (halo, SIDE), 0)
        d_pre = jnp.where(slots < count_ref[k], ref[...].astype(F32) * far_ref[at, :], 0.0).astype(BF16)
        dpre_ref[at, :] = d_pre
        dw[...] += contract_rows(picked_ref[at, :], d_pre)
    outs = (r0_ref, r1_ref, r2_ref, r3_ref)
    share = SIDE // len(outs)
    for k, out in enumerate(outs):
        device = lax.rem(pos_ref[0] + k, len(outs))
        start = pl.multiple_of(device * share, share)
        gain = jnp.zeros((16, SIDE), F32)
        for j in range(len(outs)):
            wide = jnp.broadcast_to(dgain_ref[...], (16, SIDE))
            gain = jnp.where(device == j, pltpu.roll(wide, (SIDE - j * share) % SIDE, 1), gain)
        out[pl.ds(0, share), :] = dw[pl.ds(start, share), :].astype(out.dtype)
        at = pl.ds(pl.multiple_of(2 * start, 2 * share), 2 * share)
        out[pl.ds(share, 2 * share), :] = dwin_ref[at, :].astype(out.dtype)
        out[pl.ds(3 * share, share), :] = dwout_ref[pl.ds(start, share), :].astype(out.dtype)
        out[pl.ds(4 * share, 16), :] = gain.astype(out.dtype)


def rim_products(position, halo_count, lower, upper, picked, far, dw, sums):
    piece = jax.ShapeDtypeStruct((SIDE + 16, SIDE), BF16)
    return pl.pallas_call(
        rim_kernel,
        out_shape=(jax.ShapeDtypeStruct(picked.shape, BF16), piece, piece, piece, piece),
        in_specs=[SMEM] * 2 + [VMEM] * 8,
        out_specs=(VMEM,) * 5,
        scratch_shapes=[pltpu.VMEM((SIDE, SIDE), F32)],
        compiler_params=PARAMS,
        name="rim_products",
    )(position, halo_count, lower, upper, picked, far, dw, *sums)


def place_kernel(k, rows_ref, count_ref, sum_ref, dpre_ref, msg_ref, *rest):
    out_ref, token_ref, acc, added = rest[-4:]
    token_ref[...] = jnp.zeros_like(token_ref)
    halo = rows_ref.shape[1]
    acc[...] = sum_ref[...]
    added[...] = contract_cols(dpre_ref[pl.ds(k * halo, halo), :], msg_ref[...])
    group = 16

    def body(step, carry):
        rows = [rows_ref[k, step * group + u] for u in range(group)]
        values = [acc[pl.ds(row, 1), :] + added[pl.ds(step * group + u, 1), :] for u, row in enumerate(rows)]
        for row, value in zip(rows, values):
            acc[pl.ds(row, 1), :] = value
        return carry

    lax.fori_loop(0, (count_ref[k] + group - 1) // group, body, 0)
    out_ref[...] = acc[...].astype(out_ref.dtype)


def place_rows(k, kind, halo_rows, halo_count, total, d_pre, w_msg, follow):
    return pl.pallas_call(
        functools.partial(place_kernel, k),
        out_shape=(jax.ShapeDtypeStruct(total.shape, kind), jax.ShapeDtypeStruct((8, SIDE), F32)),
        in_specs=[SMEM] * 2 + [VMEM] * 3 + [ANY] * len(follow),
        out_specs=(VMEM, VMEM),
        scratch_shapes=[pltpu.VMEM(total.shape, F32), pltpu.VMEM((halo_rows.shape[1], SIDE), F32)],
        compiler_params=PARAMS,
        cost_estimate=cost(4_000_000_000, 7_000_000),
        name="place_rows",
    )(halo_rows, halo_count, total, d_pre, w_msg, *follow)


def shift_wsh(value, step):
    parties = lax.axis_size("wsh")
    return lax.ppermute(value, "wsh", [(i, (i + step) % parties) for i in range(parties)])


def shift_slab(value, step):
    count = lax.axis_size("slab")
    pairs = [(i, i + step) for i in range(count) if 0 <= i + step < count]
    return lax.ppermute(value, "slab", pairs)


def sum_kernel(count, *refs):
    total = refs[0][...].astype(F32)
    for ref in refs[1:count]:
        total = total + ref[...].astype(F32)
    refs[-1][...] = total.astype(BF16)


def sum_group(terms, follow=()):
    return pl.pallas_call(
        functools.partial(sum_kernel, len(terms)),
        out_shape=jax.ShapeDtypeStruct(terms[0].shape, BF16),
        in_specs=[VMEM] * len(terms) + [ANY] * len(follow),
        out_specs=VMEM,
        compiler_params=SMALL,
        name="sum_group",
    )(*terms, *follow)


def sum_wsh(pieces, follow):
    return sum_group([pieces[0]] + [shift_wsh(pieces[k], k) for k in range(1, len(pieces))], follow)


def sum_slab(value, stride, size, follow=()):
    count = lax.axis_size("slab")
    span = stride * size
    turns = [[(i, (i // span) * span + (i + stride * k) % span) for i in range(count)] for k in range(1, size)]
    return sum_group([value] + [lax.ppermute(value, "slab", pairs) for pairs in turns], follow)


def other_core(value):
    return lax.ppermute(value, "slab", [(i, i ^ 1) for i in range(lax.axis_size("slab"))])


def finish_kernel(one_ref, two_ref, msg_ref, in_ref, out_w_ref, gain_ref):
    share = msg_ref.shape[0]
    total = one_ref[...].astype(F32) + two_ref[...].astype(F32)
    msg_ref[...] = total[:share]
    in_ref[...] = total[share : 3 * share]
    out_w_ref[...] = total[3 * share : 4 * share]
    gain_ref[...] = total[4 * share : 4 * share + 1, :share]


def finish(one, two):
    share = SIDE // 4
    shapes = [(share, SIDE), (2 * share, SIDE), (share, SIDE), (1, share)]
    return pl.pallas_call(
        finish_kernel,
        out_shape=tuple(jax.ShapeDtypeStruct(shape, F32) for shape in shapes),
        in_specs=[VMEM, VMEM],
        out_specs=(VMEM,) * 4,
        compiler_params=SMALL,
        name="finish",
    )(one, two)


def on_device(
    node_feat, cotangent, w_msg, w_in, w_out, ln_gain,
    tile_values, tile_cols, tile_dst, tile_src, tile_count, halo_rows, halo_count,
):
    node_rows = node_feat.shape[0]
    slots, entries, side = tile_values.shape
    halo = halo_rows.shape[2]
    parties = lax.axis_size("wsh")
    me = lax.axis_index("wsh").astype(jnp.int32)
    position = me.reshape(1)
    share = w_msg.shape[0]
    own_blocks = node_rows // side
    rim_blocks = 2 * halo // side

    tile, small = pack_shares(tile_count, tile_values, tile_cols, w_msg, w_in, w_out, ln_gain, tile_dst, tile_src)
    smalls = [small] + [shift_wsh(small, -k) for k in range(1, parties)]
    tiles = [tile] + [shift_wsh(tile, -k) for k in range(1, parties)]

    rows = halo_rows.reshape(2, halo)
    counts = halo_count.reshape(2)
    picked = pick_rows(rows, counts, node_feat)
    low, high, full_msg, full_in, full_out, gain, codes = prepare(
        position, smalls, picked, own_blocks, own_blocks + rim_blocks
    )
    lower = shift_slab(high, 1).reshape(rim_blocks // 2, side, side)
    upper = shift_slab(low, -1).reshape(rim_blocks // 2, side, side)
    message = messages(node_feat, full_msg, tiles[1:])
    far_lists = build_lists((2,), codes, ())
    forward = functools.partial(
        forward_tiles, own=message.reshape(own_blocks, side, side), lower=lower,
        upper=upper, tiles=tiles,
    )

    far_first, far_second, token = forward((2,), *far_lists, kind=BF16)
    lists = build_lists((0, 1, 3), codes, (token,))
    from_right = shift_wsh(far_first, -1)
    from_left = shift_wsh(far_second, 1)
    after_first, after_second, prior_first, prior_second, _ = forward((1, 3), *lists, kind=BF16)
    left_first = shift_wsh(after_first, 1)
    right_second = shift_wsh(prior_second, -1)
    mine_first, mine_second, _ = forward((0,), *lists, kind=F32)
    to_after, to_prior = join(after_second, from_left, prior_first, from_right)
    left_second = shift_wsh(to_after, 1)
    right_first = shift_wsh(to_prior, -1)
    parts = ((mine_first, left_first, right_first), (mine_second, left_second, right_second))
    before, d_agg, from_prior, from_after = (), [], [], []
    for h in (0, 1):
        pieces = [part.reshape(-1, side) for part in parts[h]]
        node_out, d_hidden, half, *sums = node_update(
            h, node_feat, cotangent, pieces, full_in, full_out, gain, before, from_prior
        )
        before = (node_out, d_hidden, *sums)
        d_agg.append(half)
        from_prior.append(shift_wsh(half, 1))
        from_after.append(shift_wsh(half, -1))
    quarter = node_rows // 4
    far = []
    for h in (0, 1):
        far.append(shift_wsh(from_prior[h][:quarter], 1))
        far.append(shift_wsh(from_after[h][quarter:], -1))
    slope, base, far_slope = ahead(node_feat, cotangent, d_hidden, picked, full_msg, full_in)

    backward = functools.partial(backward_tiles, tiles=tiles)
    own_part, rim_part = backward(
        (0, 1, 3), lists, (0, 1), (own_blocks, rim_blocks), (F32, F32), arrays=(d_agg, from_after, from_prior),
        started=(),
    )
    back_low, back_high = backward(
        (2,), far_lists, (1,), (rim_blocks // 2,) * 2, (BF16,) * 2, arrays=(far,), started=(rim_part,), follow=(slope,)
    )
    back_upper = shift_slab(back_low.reshape(halo, side), -1)
    back_lower = shift_slab(back_high.reshape(halo, side), 1)
    (d_own,) = backward((2,), far_lists, (0,), (own_blocks,), (F32,), arrays=(far,), started=(own_part,))
    total, d_w_own = own_products(node_feat, slope, base, d_own.reshape(node_rows, side), full_msg)
    d_pre, *pieces = rim_products(
        position, counts, back_lower, back_upper, picked, far_slope, d_w_own, sums
    )
    place = functools.partial(place_rows, halo_rows=rows, halo_count=counts, d_pre=d_pre, w_msg=full_msg)
    total, token = place(0, F32, total=total, follow=())
    value = sum_wsh(pieces, (token,))
    d_node, token = place(1, BF16, total=total, follow=(value,))
    value = sum_slab(value, 8, 4, (token,))
    value = sum_slab(value, 2, 4)
    d_w_msg, d_w_in, d_w_out, d_gain = finish(value, other_core(value))
    return (node_out, d_node, d_w_msg, d_w_in, d_w_out, d_gain.reshape(share))


def solution(mesh):
    both = ("slab", "wsh")
    tall, split, line = P(both, None), P("wsh", None), P(both)
    cube = P(both, None, None)
    return jax.shard_map(
        on_device,
        mesh=mesh,
        in_specs=(
            tall, tall, split, split, split, P("wsh"), cube, cube, line, line, line, cube, tall,
        ),
        out_specs=(tall, tall, split, split, split, P("wsh")),
        check_vma=False,
    )
```

```python
import functools

import jax
import jax.numpy as jnp
from jax import lax
from jax.experimental import pallas as pl
from jax.experimental.pallas import tpu as pltpu
from jax.sharding import PartitionSpec as P

F32 = jnp.float32
BF16 = jnp.bfloat16
SIDE = 128
UNROLL = 8
PARAMS = pltpu.CompilerParams(vmem_limit_bytes=16 * 2**20)
SMALL = pltpu.CompilerParams(vmem_limit_bytes=4 * 2**20)
ROOMY = pltpu.CompilerParams(vmem_limit_bytes=60 * 2**20)
VMEM = pl.BlockSpec(memory_space=pltpu.VMEM)
SMEM = pl.BlockSpec(memory_space=pltpu.SMEM)
ANY = pl.BlockSpec(memory_space=pl.ANY)


def cost(flops, size):
    return pl.CostEstimate(flops=flops, bytes_accessed=size, transcendentals=0)


def dot(left, right, dims):
    return lax.dot_general(left, right, (dims, ((), ())), preferred_element_type=F32)


def rows_by_cols(left, right):
    return dot(left, right, ((1,), (0,)))


def contract_rows(left, right):
    return dot(left, right, ((0,), (0,)))


def contract_cols(left, right):
    return dot(left, right, ((1,), (1,)))


def sigmoid(v):
    return 1.0 / (1.0 + jnp.exp(-v))


def silu_slope(v):
    g = sigmoid(v)
    return g * (1.0 + v * (1.0 - g))


def pick_kernel(rows_ref, count_ref, feat_ref, out_ref, wide, picked):
    halo = rows_ref.shape[1]
    wide[...] = feat_ref[...].astype(F32)
    group = 16
    for k in range(2):
        count = count_ref[k]

        def body(step, carry):
            for u in range(group):
                slot = step * group + u
                row = rows_ref[k, slot]
                picked[pl.ds(slot, 1), :] = wide[pl.ds(row, 1), :]
            return carry

        lax.fori_loop(0, (count + group - 1) // group, body, 0)
        slots = lax.broadcasted_iota(jnp.int32, (halo, SIDE), 0)
        kept = jnp.where(slots < count, picked[...], 0.0)
        out_ref[pl.ds(k * halo, halo), :] = kept.astype(BF16)


def pick_rows(halo_rows, halo_count, node_feat):
    halo = halo_rows.shape[1]
    return pl.pallas_call(
        pick_kernel,
        out_shape=jax.ShapeDtypeStruct((2 * halo, SIDE), BF16),
        in_specs=[SMEM, SMEM, VMEM],
        out_specs=VMEM,
        scratch_shapes=[pltpu.VMEM(node_feat.shape, F32), pltpu.VMEM((halo, SIDE), F32)],
        compiler_params=ROOMY,
        name="pick_rows",
    )(halo_rows, halo_count, node_feat)


def pack_kernel(
    count_ref, values_ref, cols_ref, msg_ref, in_ref, out_w_ref, gain_ref, dst_ref, src_ref, tiles_ref, pack_ref, lines
):
    share, edges = msg_ref.shape[0], values_ref.shape[0]
    tiles_ref[pl.ds(0, edges), :] = values_ref[...]
    tiles_ref[pl.ds(edges, edges), :] = cols_ref[...].astype(F32).astype(BF16)
    pack_ref[pl.ds(0, share), :] = msg_ref[...]
    pack_ref[pl.ds(share, 2 * share), :] = in_ref[...]
    pack_ref[pl.ds(3 * share, share), :] = out_w_ref[...]
    lines[...] = jnp.zeros_like(lines)
    gain = gain_ref[...].astype(F32)
    for j in range(SIDE // share):
        lines[0:1, j * share : (j + 1) * share] = gain
    lines[1:2, :] = dst_ref[...].astype(F32)
    lines[2:3, :] = src_ref[...].astype(F32)
    lines[3:4, :] = jnp.full((1, SIDE), count_ref[0]).astype(F32)
    pack_ref[pl.ds(4 * share, 16), :] = lines[...].astype(BF16)


def pack_shares(tile_count, tile_values, tile_cols, w_msg, w_in, w_out, ln_gain, tile_dst, tile_src):
    share = w_msg.shape[0]
    values, cols = (array.reshape(-1, SIDE) for array in (tile_values, tile_cols))
    return pl.pallas_call(
        pack_kernel,
        out_shape=(
            jax.ShapeDtypeStruct((2 * values.shape[0], SIDE), BF16),
            jax.ShapeDtypeStruct((4 * share + 16, SIDE), BF16),
        ),
        in_specs=[SMEM] + [VMEM] * 8,
        out_specs=(VMEM, VMEM),
        scratch_shapes=[pltpu.VMEM((16, SIDE), F32)],
        compiler_params=ROOMY,
        name="pack_shares",
    )(
        tile_count, values, cols, w_msg, w_in, w_out, ln_gain.reshape(1, share), tile_dst.reshape(1, SIDE),
        tile_src.reshape(1, SIDE),
    )


def prepare_kernel(
    own_blocks, here_blocks, pos_ref, s0_ref, s1_ref, s2_ref, s3_ref, picked_ref,
    low_ref, high_ref, msg_ref, in_ref, out_w_ref, gain_ref, code_ref,
):
    me = pos_ref[0]
    smalls = (s0_ref, s1_ref, s2_ref, s3_ref)
    parties = len(smalls)
    share = SIDE // parties
    lane = lax.broadcasted_iota(jnp.int32, (1, SIDE), 1)
    gain = jnp.zeros((1, SIDE), F32)
    for k, ref in enumerate(smalls):
        device = lax.rem(me + k, parties)
        at = pl.multiple_of(device * share, share)
        msg_ref[pl.ds(at, share), :] = ref[pl.ds(0, share), :]
        in_ref[pl.ds(pl.multiple_of(2 * at, 2 * share), 2 * share), :] = ref[pl.ds(share, 2 * share), :]
        out_w_ref[pl.ds(at, share), :] = ref[pl.ds(3 * share, share), :]
        lines = ref[pl.ds(4 * share, 16), :].astype(F32)
        gain = jnp.where((lane >= at) & (lane < at + share), lines[0:1, :], gain)
        dst, src, count = (lines[i : i + 1, :].astype(jnp.int32) for i in (1, 2, 3))
        block = src - me * here_blocks
        used = (lane < count) & (block >= 0) & (block < here_blocks)
        is_rim = block >= own_blocks
        place = jnp.where(is_rim, block - own_blocks, block)
        code = lane + (place << 7) + (dst << 13) + jnp.where(is_rim, 2 << 20, 1 << 20)
        code_ref[k : k + 1, :] = jnp.where(used, code, 0)
        code_ref[parties + k : parties + k + 1, :] = count
    gain_ref[...] = gain
    half = low_ref.shape[0]
    w_msg = msg_ref[...]
    for k, ref in enumerate((low_ref, high_ref)):
        pre = rows_by_cols(picked_ref[pl.ds(k * half, half), :], w_msg)
        ref[...] = (pre * sigmoid(pre)).astype(BF16)


def prepare(position, smalls, picked, own_blocks, here_blocks):
    half = picked.shape[0] // 2
    return pl.pallas_call(
        functools.partial(prepare_kernel, own_blocks, here_blocks),
        out_shape=(
            jax.ShapeDtypeStruct((half, SIDE), BF16),
            jax.ShapeDtypeStruct((half, SIDE), BF16),
            jax.ShapeDtypeStruct((SIDE, SIDE), BF16),
            jax.ShapeDtypeStruct((2 * SIDE, SIDE), BF16),
            jax.ShapeDtypeStruct((SIDE, SIDE), BF16),
            jax.ShapeDtypeStruct((1, SIDE), F32),
            jax.ShapeDtypeStruct((8, SIDE), jnp.int32),
        ),
        in_specs=[SMEM] + [VMEM] * 5,
        out_specs=(VMEM,) * 7,
        compiler_params=PARAMS,
        name="prepare",
    )(position, *smalls, picked)


def message_kernel(feat_ref, msg_ref, *rest):
    out_ref = rest[-1]
    pre = rows_by_cols(feat_ref[...], msg_ref[...])
    out_ref[...] = (pre * sigmoid(pre)).astype(BF16)


def messages(feat, w_msg, follow):
    rows = feat.shape[0]
    steps = 2
    tall = pl.BlockSpec((rows // steps, SIDE), lambda i: (i, 0))
    return pl.pallas_call(
        message_kernel,
        grid=(steps,),
        out_shape=jax.ShapeDtypeStruct((rows, SIDE), BF16),
        in_specs=[tall, pl.BlockSpec(w_msg.shape, lambda i: (0, 0))] + [ANY] * len(follow),
        out_specs=tall,
        compiler_params=PARAMS,
        name="messages",
    )(feat, w_msg, *follow)


def list_kernel(ks, code_ref, *rest):
    list_ref, total_ref = rest[-2:]
    parties = code_ref.shape[0] // 2
    group = 8
    for k in ks:

        def body(step, carry):
            own, rim = carry
            codes = [code_ref[k, step * group + u] for u in range(group)]
            for code in codes:
                list_ref[2 * k, own] = code
                list_ref[2 * k + 1, rim] = code
                own = own + ((code >> 20) & 1)
                rim = rim + (code >> 21)
            return (own, rim)

        steps = (code_ref[parties + k, 0] + group - 1) // group
        own, rim = lax.fori_loop(0, steps, body, (jnp.int32(0), jnp.int32(0)))
        total_ref[2 * k] = own
        total_ref[2 * k + 1] = rim


def build_lists(ks, codes, follow):
    parties, slots = codes.shape[0] // 2, codes.shape[1]
    return pl.pallas_call(
        functools.partial(list_kernel, ks),
        out_shape=(
            jax.ShapeDtypeStruct((2 * parties, slots + 16), jnp.int32),
            jax.ShapeDtypeStruct((2 * parties,), jnp.int32),
        ),
        in_specs=[SMEM] + [ANY] * len(follow),
        out_specs=(SMEM, SMEM),
        compiler_params=SMALL,
        name="tile_lists",
    )(codes, *follow)


def dense_tile(tiles_ref, slot, keep):
    column = lax.broadcasted_iota(jnp.int32, (SIDE, SIDE), 0).astype(F32)
    edges = tiles_ref.shape[0] // 2
    entries = edges // SIDE
    total = None
    for e in range(entries):
        at = slot * entries + e
        weight = tiles_ref[pl.ds(at, 1), :] * keep
        term = jnp.where(column == tiles_ref[pl.ds(edges + at, 1), :], weight, 0.0)
        total = term if total is None else total + term
    return total.astype(BF16)


def walk_list(list_ref, total_ref, which, tiles_ref, product, acc):
    count = total_ref[which]

    def body(step, carry):
        found = []
        for u in range(UNROLL):
            index = step * UNROLL + u
            used = index < count
            entry = jnp.where(used, list_ref[which, index], 0)
            dense = dense_tile(tiles_ref, entry & 127, jnp.where(used, 1.0, 0.0))
            found.append(product(dense, (entry >> 7) & 63, (entry >> 13) & 31))
        for target, value in found:
            acc[target] += value
        return carry

    lax.fori_loop(0, (count + UNROLL - 1) // UNROLL, body, 0)


def forward_kernel(ks, list_ref, total_ref, own_ref, lower_ref, upper_ref, *rest):
    slot_refs, rest = rest[: len(ks)], rest[len(ks) :]
    outs, (token_ref, acc, rims, tiles) = rest[:-4], rest[-4:]
    token_ref[...] = jnp.zeros_like(token_ref)
    half = lower_ref.shape[0]
    rims[pl.ds(0, half)] = lower_ref[...]
    rims[pl.ds(half, half)] = upper_ref[...]
    for at, (k, slot_ref) in enumerate(zip(ks, slot_refs)):
        acc[...] = jnp.zeros_like(acc)
        tiles[...] = slot_ref[...].astype(F32)
        for part, ref in enumerate((own_ref, rims)):

            def product(dense, block, target, ref=ref):
                return (target, contract_rows(dense, ref[block]))

            walk_list(list_ref, total_ref, 2 * k + part, tiles, product, acc)
        for h in range(2):
            out_ref = outs[2 * at + h]
            span = out_ref.shape[0]
            out_ref[...] = acc[pl.ds(h * span, span)].astype(out_ref.dtype)


def forward_tiles(ks, lists, totals, own, lower, upper, tiles, kind):
    blocks = own.shape[0]
    half = jax.ShapeDtypeStruct((blocks // 2,) + own.shape[1:], kind)
    return pl.pallas_call(
        functools.partial(forward_kernel, ks),
        out_shape=(half,) * (2 * len(ks)) + (jax.ShapeDtypeStruct((8, SIDE), F32),),
        in_specs=[SMEM, SMEM] + [VMEM] * (3 + len(ks)),
        out_specs=(VMEM,) * (2 * len(ks) + 1),
        scratch_shapes=[
            pltpu.VMEM(own.shape, F32),
            pltpu.VMEM((2 * lower.shape[0],) + lower.shape[1:], BF16),
            pltpu.VMEM(tiles[0].shape, F32),
        ],
        compiler_params=PARAMS,
        cost_estimate=cost(1_000_000_000 * len(ks), 4_000_000 * len(ks)),
        name="forward_tiles",
    )(lists, totals, own, lower, upper, *[tiles[k] for k in ks])


def join_kernel(after_ref, left_ref, prior_ref, right_ref, *outs):
    for mine, theirs, out_ref in ((after_ref, left_ref, outs[0]), (prior_ref, right_ref, outs[1])):
        out_ref[...] = (mine[...].astype(F32) + theirs[...].astype(F32)).astype(BF16)


def join(after, from_left, prior, from_right):
    kind = jax.ShapeDtypeStruct(after.shape, BF16)
    return pl.pallas_call(
        join_kernel,
        out_shape=(kind, kind),
        in_specs=[VMEM] * 4,
        out_specs=(VMEM, VMEM),
        compiler_params=PARAMS,
        name="join",
    )(after, from_left, prior, from_right)


def node_kernel(
    continued, feat_ref, cot_ref, own_ref, left_ref, right_ref, in_ref, out_w_ref, gain_ref, *rest,
):
    node_ref, dhid_ref, dagg_ref, dwin_ref, dwout_ref, dgain_ref = rest[-6:]
    step = pl.program_id(0)

    @pl.when(step == 0)
    def _():
        for at, ref in enumerate((dwin_ref, dwout_ref, dgain_ref)):
            ref[...] = rest[2 + at][...] if continued else jnp.zeros_like(ref)

    feat = feat_ref[...]
    agg = (own_ref[...] + (left_ref[...].astype(F32) + right_ref[...].astype(F32))).astype(BF16)
    w_feat, w_agg, w_out = in_ref[:SIDE, :], in_ref[SIDE:, :], out_w_ref[...]
    gain = gain_ref[...]
    pre = rows_by_cols(feat, w_feat) + rows_by_cols(agg, w_agg)
    logistic = sigmoid(pre)
    hidden = (pre * logistic).astype(BF16)
    slope = logistic * (1.0 + pre * (1.0 - logistic))
    update = rows_by_cols(hidden, w_out)
    centre = update - jnp.mean(update, axis=-1, keepdims=True)
    inverse = lax.rsqrt(jnp.mean(centre * centre, axis=-1, keepdims=True) + 1e-05)
    normed = centre * inverse
    node_ref[...] = (feat.astype(F32) + gain * normed).astype(BF16)
    upstream = cot_ref[...].astype(F32)
    d_normed = upstream * gain
    dgain_ref[...] += jnp.sum(upstream * normed, axis=0, keepdims=True)
    d_update = (
        d_normed
        - jnp.mean(d_normed, axis=-1, keepdims=True)
        - normed * jnp.mean(d_normed * normed, axis=-1, keepdims=True)
    ) * inverse
    d_update = d_update.astype(BF16)
    d_hidden = (contract_cols(d_update, w_out) * slope).astype(BF16)
    dhid_ref[...] = d_hidden
    dagg_ref[...] = contract_cols(d_hidden, w_agg).astype(BF16)
    dwout_ref[...] += contract_rows(hidden, d_update)
    dwin_ref[:SIDE, :] += contract_rows(feat, d_hidden)
    dwin_ref[SIDE:, :] += contract_rows(agg, d_hidden)


def node_update(h, node_feat, cotangent, parts, w_in, w_out, gain, before, follow):
    rows = node_feat.shape[0]
    chunk = 512
    steps = rows // 2 // chunk

    def whole(shape):
        return pl.BlockSpec(shape, lambda i: (0, 0))

    tall = pl.BlockSpec((chunk, SIDE), lambda i: (h * steps + i, 0))
    part = pl.BlockSpec((chunk, SIDE), lambda i: (i, 0))
    wide = jax.ShapeDtypeStruct((rows, SIDE), BF16)
    half = jax.ShapeDtypeStruct((rows // 2, SIDE), BF16)
    sums = [(2 * SIDE, SIDE), (SIDE, SIDE), (1, SIDE)]
    return pl.pallas_call(
        functools.partial(node_kernel, bool(before)),
        grid=(steps,),
        out_shape=(wide, wide, half) + tuple(jax.ShapeDtypeStruct(shape, F32) for shape in sums),
        in_specs=[tall, tall, part, part, part]
        + [whole((2 * SIDE, SIDE)), whole((SIDE, SIDE)), whole((1, SIDE))]
        + ([ANY, ANY] + [whole(shape) for shape in sums] if before else [])
        + [ANY] * len(follow),
        out_specs=(tall, tall, part) + tuple(whole(shape) for shape in sums),
        input_output_aliases={8: 0, 9: 1} if before else {},
        compiler_params=PARAMS,
        cost_estimate=cost(5_000_000_000, 10_000_000),
        name="node_update",
    )(node_feat, cotangent, *parts, w_in, w_out, gain, *before, *follow)


def ahead_kernel(feat_ref, cot_ref, dhid_ref, picked_ref, msg_ref, in_ref, slope_ref, base_ref, far_ref):
    w_msg = msg_ref[...]
    slope_ref[...] = silu_slope(rows_by_cols(feat_ref[...], w_msg))
    far_ref[...] = silu_slope(rows_by_cols(picked_ref[...], w_msg))
    base_ref[...] = cot_ref[...].astype(F32) + contract_cols(dhid_ref[...], in_ref[:SIDE, :])


def ahead(feat, cot, dhid, picked, w_msg, w_in):
    rows = feat.shape[0]
    steps = 4
    tall = pl.BlockSpec((rows // steps, SIDE), lambda i: (i, 0))
    short = pl.BlockSpec((picked.shape[0] // steps, SIDE), lambda i: (i, 0))
    wide = jax.ShapeDtypeStruct((rows, SIDE), F32)
    return pl.pallas_call(
        ahead_kernel,
        grid=(steps,),
        out_shape=(wide, wide, jax.ShapeDtypeStruct(picked.shape, F32)),
        in_specs=[tall] * 3 + [short] + [pl.BlockSpec(w.shape, lambda i: (0, 0)) for w in (w_msg, w_in)],
        out_specs=(tall, tall, short),
        compiler_params=PARAMS,
        cost_estimate=cost(3_000_000_000, 7_000_000),
        name="ahead",
    )(feat, cot, dhid, picked, w_msg, w_in)


def backward_kernel(ks, cuts, parts, started, list_ref, total_ref, *rest):
    slot_refs, rest = rest[: len(ks)], rest[len(ks) :]
    tiles, grads, accs = rest[-2 - len(parts)], rest[-1 - len(parts)], rest[-len(parts) :]
    arrays, rest = rest[: cuts * len(ks)], rest[cuts * len(ks) : -2 - len(parts)]
    for at, acc in enumerate(accs):
        acc[...] = rest[at][...] if started else jnp.zeros_like(acc)
    for at, (k, slot_ref) in enumerate(zip(ks, slot_refs)):
        tiles[...] = slot_ref[...].astype(F32)
        source = arrays[at]
        if cuts > 1:
            source, span = grads, grads.shape[0] // cuts
            for c in range(cuts):
                grads[pl.ds(c * span, span)] = arrays[cuts * at + c][...]

        def product(dense, block, target, source=source):
            return (block, rows_by_cols(dense, source[target]))

        for part, acc in zip(parts, accs):
            walk_list(list_ref, total_ref, 2 * k + part, tiles, product, acc)
    if parts == (1,):
        half = accs[0].shape[0] // 2
        for at, out_ref in enumerate(rest[-2:]):
            out_ref[...] = accs[0][pl.ds(at * half, half)].astype(out_ref.dtype)
    else:
        for out_ref, acc in zip(rest[-len(parts) :], accs):
            out_ref[...] = acc[...]


def backward_tiles(ks, lists, parts, sizes, kinds, tiles, arrays, started, follow=()):
    cuts = len(arrays[0])
    cubes = [array.reshape(-1, SIDE, SIDE) for group in arrays for array in group]
    accs = [sum(sizes)] if len(sizes) > len(parts) else sizes
    return pl.pallas_call(
        functools.partial(backward_kernel, ks, cuts, parts, bool(started)),
        out_shape=tuple(jax.ShapeDtypeStruct((size, SIDE, SIDE), kind) for size, kind in zip(sizes, kinds)),
        in_specs=[SMEM, SMEM] + [VMEM] * (len(ks) + len(cubes) + len(started)) + [ANY] * len(follow),
        out_specs=(VMEM,) * len(sizes),
        scratch_shapes=[pltpu.VMEM(tiles[0].shape, F32), pltpu.VMEM((cuts * cubes[0].shape[0], SIDE, SIDE), BF16)]
        + [pltpu.VMEM((size, SIDE, SIDE), F32) for size in accs],
        compiler_params=PARAMS,
        cost_estimate=cost(2_000_000_000 * len(ks), 4_000_000),
        name="backward_tiles",
    )(*lists, *[tiles[k] for k in ks], *cubes, *started, *follow)


def own_kernel(feat_ref, slope_ref, base_ref, own_ref, msg_ref, sum_ref, dw_ref):
    @pl.when(pl.program_id(0) == 0)
    def _():
        dw_ref[...] = jnp.zeros_like(dw_ref)

    d_pre = (own_ref[...] * slope_ref[...]).astype(BF16)
    dw_ref[...] += contract_rows(feat_ref[...], d_pre)
    sum_ref[...] = base_ref[...] + contract_cols(d_pre, msg_ref[...])


def own_products(feat, slope, base, own, w_msg):
    rows = feat.shape[0]
    steps = 4
    tall = pl.BlockSpec((rows // steps, SIDE), lambda i: (i, 0))
    square = pl.BlockSpec((SIDE, SIDE), lambda i: (0, 0))
    return pl.pallas_call(
        own_kernel,
        grid=(steps,),
        out_shape=(jax.ShapeDtypeStruct((rows, SIDE), F32), jax.ShapeDtypeStruct((SIDE, SIDE), F32)),
        in_specs=[tall] * 4 + [square],
        out_specs=(tall, square),
        compiler_params=PARAMS,
        cost_estimate=cost(3_000_000_000, 7_000_000),
        name="own_products",
    )(feat, slope, base, own, w_msg)


def rim_kernel(
    pos_ref, count_ref, lower_ref, upper_ref, picked_ref, far_ref, dw_ref, dwin_ref, dwout_ref, dgain_ref,
    dpre_ref, r0_ref, r1_ref, r2_ref, r3_ref, dw,
):
    halo = lower_ref.shape[0]
    dw[...] = dw_ref[...]
    for k, ref in enumerate((lower_ref, upper_ref)):
        at = pl.ds(k * halo, halo)
        slots = lax.broadcasted_iota(jnp.int32, (halo, SIDE), 0)
        d_pre = jnp.where(slots < count_ref[k], ref[...].astype(F32) * far_ref[at, :], 0.0).astype(BF16)
        dpre_ref[at, :] = d_pre
        dw[...] += contract_rows(picked_ref[at, :], d_pre)
    outs = (r0_ref, r1_ref, r2_ref, r3_ref)
    share = SIDE // len(outs)
    for k, out in enumerate(outs):
        device = lax.rem(pos_ref[0] + k, len(outs))
        start = pl.multiple_of(device * share, share)
        gain = jnp.zeros((16, SIDE), F32)
        for j in range(len(outs)):
            wide = jnp.broadcast_to(dgain_ref[...], (16, SIDE))
            gain = jnp.where(device == j, pltpu.roll(wide, (SIDE - j * share) % SIDE, 1), gain)
        out[pl.ds(0, share), :] = dw[pl.ds(start, share), :].astype(out.dtype)
        at = pl.ds(pl.multiple_of(2 * start, 2 * share), 2 * share)
        out[pl.ds(share, 2 * share), :] = dwin_ref[at, :].astype(out.dtype)
        out[pl.ds(3 * share, share), :] = dwout_ref[pl.ds(start, share), :].astype(out.dtype)
        out[pl.ds(4 * share, 16), :] = gain.astype(out.dtype)


def rim_products(position, halo_count, lower, upper, picked, far, dw, sums):
    piece = jax.ShapeDtypeStruct((SIDE + 16, SIDE), BF16)
    return pl.pallas_call(
        rim_kernel,
        out_shape=(jax.ShapeDtypeStruct(picked.shape, BF16), piece, piece, piece, piece),
        in_specs=[SMEM] * 2 + [VMEM] * 8,
        out_specs=(VMEM,) * 5,
        scratch_shapes=[pltpu.VMEM((SIDE, SIDE), F32)],
        compiler_params=PARAMS,
        name="rim_products",
    )(position, halo_count, lower, upper, picked, far, dw, *sums)


def place_kernel(k, rows_ref, count_ref, sum_ref, dpre_ref, msg_ref, *rest):
    out_ref, token_ref, acc, added = rest[-4:]
    token_ref[...] = jnp.zeros_like(token_ref)
    halo = rows_ref.shape[1]
    acc[...] = sum_ref[...]
    added[...] = contract_cols(dpre_ref[pl.ds(k * halo, halo), :], msg_ref[...])
    group = 16

    def body(step, carry):
        rows = [rows_ref[k, step * group + u] for u in range(group)]
        values = [acc[pl.ds(row, 1), :] + added[pl.ds(step * group + u, 1), :] for u, row in enumerate(rows)]
        for row, value in zip(rows, values):
            acc[pl.ds(row, 1), :] = value
        return carry

    lax.fori_loop(0, (count_ref[k] + group - 1) // group, body, 0)
    out_ref[...] = acc[...].astype(out_ref.dtype)


def place_rows(k, kind, halo_rows, halo_count, total, d_pre, w_msg, follow):
    return pl.pallas_call(
        functools.partial(place_kernel, k),
        out_shape=(jax.ShapeDtypeStruct(total.shape, kind), jax.ShapeDtypeStruct((8, SIDE), F32)),
        in_specs=[SMEM] * 2 + [VMEM] * 3 + [ANY] * len(follow),
        out_specs=(VMEM, VMEM),
        scratch_shapes=[pltpu.VMEM(total.shape, F32), pltpu.VMEM((halo_rows.shape[1], SIDE), F32)],
        compiler_params=PARAMS,
        cost_estimate=cost(4_000_000_000, 7_000_000),
        name="place_rows",
    )(halo_rows, halo_count, total, d_pre, w_msg, *follow)


def shift_wsh(value, step):
    parties = lax.axis_size("wsh")
    return lax.ppermute(value, "wsh", [(i, (i + step) % parties) for i in range(parties)])


def shift_slab(value, step):
    count = lax.axis_size("slab")
    pairs = [(i, i + step) for i in range(count) if 0 <= i + step < count]
    return lax.ppermute(value, "slab", pairs)


def sum_kernel(count, *refs):
    total = refs[0][...].astype(F32)
    for ref in refs[1:count]:
        total = total + ref[...].astype(F32)
    refs[-1][...] = total.astype(BF16)


def sum_group(terms, follow=()):
    return pl.pallas_call(
        functools.partial(sum_kernel, len(terms)),
        out_shape=jax.ShapeDtypeStruct(terms[0].shape, BF16),
        in_specs=[VMEM] * len(terms) + [ANY] * len(follow),
        out_specs=VMEM,
        compiler_params=SMALL,
        name="sum_group",
    )(*terms, *follow)


def sum_wsh(pieces, follow):
    return sum_group([pieces[0]] + [shift_wsh(pieces[k], k) for k in range(1, len(pieces))], follow)


def sum_slab(value, stride, size, follow=()):
    count = lax.axis_size("slab")
    span = stride * size
    turns = [[(i, (i // span) * span + (i + stride * k) % span) for i in range(count)] for k in range(1, size)]
    return sum_group([value] + [lax.ppermute(value, "slab", pairs) for pairs in turns], follow)


def other_core(value):
    return lax.ppermute(value, "slab", [(i, i ^ 1) for i in range(lax.axis_size("slab"))])


def finish_kernel(one_ref, two_ref, msg_ref, in_ref, out_w_ref, gain_ref):
    share = msg_ref.shape[0]
    total = one_ref[...].astype(F32) + two_ref[...].astype(F32)
    msg_ref[...] = total[:share]
    in_ref[...] = total[share : 3 * share]
    out_w_ref[...] = total[3 * share : 4 * share]
    gain_ref[...] = total[4 * share : 4 * share + 1, :share]


def finish(one, two):
    share = SIDE // 4
    shapes = [(share, SIDE), (2 * share, SIDE), (share, SIDE), (1, share)]
    return pl.pallas_call(
        finish_kernel,
        out_shape=tuple(jax.ShapeDtypeStruct(shape, F32) for shape in shapes),
        in_specs=[VMEM, VMEM],
        out_specs=(VMEM,) * 4,
        compiler_params=SMALL,
        name="finish",
    )(one, two)


def on_device(
    node_feat, cotangent, w_msg, w_in, w_out, ln_gain,
    tile_values, tile_cols, tile_dst, tile_src, tile_count, halo_rows, halo_count,
):
    node_rows = node_feat.shape[0]
    slots, entries, side = tile_values.shape
    halo = halo_rows.shape[2]
    parties = lax.axis_size("wsh")
    me = lax.axis_index("wsh").astype(jnp.int32)
    position = me.reshape(1)
    share = w_msg.shape[0]
    own_blocks = node_rows // side
    rim_blocks = 2 * halo // side

    tile, small = pack_shares(tile_count, tile_values, tile_cols, w_msg, w_in, w_out, ln_gain, tile_dst, tile_src)
    smalls = [small] + [shift_wsh(small, -k) for k in range(1, parties)]
    tiles = [tile] + [shift_wsh(tile, -k) for k in range(1, parties)]

    rows = halo_rows.reshape(2, halo)
    counts = halo_count.reshape(2)
    picked = pick_rows(rows, counts, node_feat)
    low, high, full_msg, full_in, full_out, gain, codes = prepare(
        position, smalls, picked, own_blocks, own_blocks + rim_blocks
    )
    lower = shift_slab(high, 1).reshape(rim_blocks // 2, side, side)
    upper = shift_slab(low, -1).reshape(rim_blocks // 2, side, side)
    message = messages(node_feat, full_msg, tiles[1:])
    far_lists = build_lists((2,), codes, ())
    forward = functools.partial(
        forward_tiles, own=message.reshape(own_blocks, side, side), lower=lower,
        upper=upper, tiles=tiles,
    )

    far_first, far_second, token = forward((2,), *far_lists, kind=BF16)
    lists = build_lists((0, 1, 3), codes, (token,))
    from_right = shift_wsh(far_first, -1)
    from_left = shift_wsh(far_second, 1)
    after_first, after_second, prior_first, prior_second, _ = forward((1, 3), *lists, kind=BF16)
    left_first = shift_wsh(after_first, 1)
    right_second = shift_wsh(prior_second, -1)
    mine_first, mine_second, _ = forward((0,), *lists, kind=F32)
    to_after, to_prior = join(after_second, from_left, prior_first, from_right)
    left_second = shift_wsh(to_after, 1)
    right_first = shift_wsh(to_prior, -1)
    parts = ((mine_first, left_first, right_first), (mine_second, left_second, right_second))
    before, d_agg, from_prior, from_after = (), [], [], []
    for h in (0, 1):
        pieces = [part.reshape(-1, side) for part in parts[h]]
        node_out, d_hidden, half, *sums = node_update(
            h, node_feat, cotangent, pieces, full_in, full_out, gain, before, from_prior
        )
        before = (node_out, d_hidden, *sums)
        d_agg.append(half)
        from_prior.append(shift_wsh(half, 1))
        from_after.append(shift_wsh(half, -1))
    quarter = node_rows // 4
    far = []
    for h in (0, 1):
        far.append(shift_wsh(from_prior[h][:quarter], 1))
        far.append(shift_wsh(from_after[h][quarter:], -1))
    slope, base, far_slope = ahead(node_feat, cotangent, d_hidden, picked, full_msg, full_in)

    backward = functools.partial(backward_tiles, tiles=tiles)
    own_part, rim_part = backward(
        (0, 1, 3), lists, (0, 1), (own_blocks, rim_blocks), (F32, F32), arrays=(d_agg, from_after, from_prior),
        started=(),
    )
    back_low, back_high = backward(
        (2,), far_lists, (1,), (rim_blocks // 2,) * 2, (BF16,) * 2, arrays=(far,), started=(rim_part,), follow=(slope,)
    )
    back_upper = shift_slab(back_low.reshape(halo, side), -1)
    back_lower = shift_slab(back_high.reshape(halo, side), 1)
    (d_own,) = backward((2,), far_lists, (0,), (own_blocks,), (F32,), arrays=(far,), started=(own_part,))
    total, d_w_own = own_products(node_feat, slope, base, d_own.reshape(node_rows, side), full_msg)
    d_pre, *pieces = rim_products(
        position, counts, back_lower, back_upper, picked, far_slope, d_w_own, sums
    )
    place = functools.partial(place_rows, halo_rows=rows, halo_count=counts, d_pre=d_pre, w_msg=full_msg)
    total, token = place(0, F32, total=total, follow=())
    value = sum_wsh(pieces, (token,))
    d_node, token = place(1, BF16, total=total, follow=(value,))
    value = sum_slab(value, 8, 4, (token,))
    value = sum_slab(value, 2, 4)
    d_w_msg, d_w_in, d_w_out, d_gain = finish(value, other_core(value))
    return (node_out, d_node, d_w_msg, d_w_in, d_w_out, d_gain.reshape(share))


def solution(mesh):
    both = ("slab", "wsh")
    tall, split, line = P(both, None), P("wsh", None), P(both)
    cube = P(both, None, None)
    return jax.shard_map(
        on_device,
        mesh=mesh,
        in_specs=(
            tall, tall, split, split, split, P("wsh"), cube, cube, line, line, line, cube, tall,
        ),
        out_specs=(tall, tall, split, split, split, P("wsh")),
        check_vma=False,
    )
```

```python
import functools

import jax
import jax.numpy as jnp
from jax import lax
from jax.experimental import pallas as pl
from jax.experimental.pallas import tpu as pltpu
from jax.sharding import PartitionSpec as P

F32 = jnp.float32
BF16 = jnp.bfloat16
SIDE = 128
UNROLL = 8
PARAMS = pltpu.CompilerParams(vmem_limit_bytes=16 * 2**20)
SMALL = pltpu.CompilerParams(vmem_limit_bytes=4 * 2**20)
ROOMY = pltpu.CompilerParams(vmem_limit_bytes=60 * 2**20)
VMEM = pl.BlockSpec(memory_space=pltpu.VMEM)
SMEM = pl.BlockSpec(memory_space=pltpu.SMEM)
ANY = pl.BlockSpec(memory_space=pl.ANY)


def cost(flops, size):
    return pl.CostEstimate(flops=flops, bytes_accessed=size, transcendentals=0)


def dot(left, right, dims):
    return lax.dot_general(left, right, (dims, ((), ())), preferred_element_type=F32)


def rows_by_cols(left, right):
    return dot(left, right, ((1,), (0,)))


def contract_rows(left, right):
    return dot(left, right, ((0,), (0,)))


def contract_cols(left, right):
    return dot(left, right, ((1,), (1,)))


def sigmoid(v):
    return 1.0 / (1.0 + jnp.exp(-v))


def silu_slope(v):
    g = sigmoid(v)
    return g * (1.0 + v * (1.0 - g))


def pick_kernel(rows_ref, count_ref, feat_ref, out_ref, wide, picked):
    halo = rows_ref.shape[1]
    wide[...] = feat_ref[...].astype(F32)
    group = 32
    for k in range(2):
        count = count_ref[k]

        def body(step, carry):
            for u in range(group):
                slot = step * group + u
                row = rows_ref[k, slot]
                picked[pl.ds(slot, 1), :] = wide[pl.ds(row, 1), :]
            return carry

        lax.fori_loop(0, (count + group - 1) // group, body, 0)
        slots = lax.broadcasted_iota(jnp.int32, (halo, SIDE), 0)
        kept = jnp.where(slots < count, picked[...], 0.0)
        out_ref[pl.ds(k * halo, halo), :] = kept.astype(BF16)


def pick_rows(halo_rows, halo_count, node_feat):
    halo = halo_rows.shape[1]
    return pl.pallas_call(
        pick_kernel,
        out_shape=jax.ShapeDtypeStruct((2 * halo, SIDE), BF16),
        in_specs=[SMEM, SMEM, VMEM],
        out_specs=VMEM,
        scratch_shapes=[pltpu.VMEM(node_feat.shape, F32), pltpu.VMEM((halo, SIDE), F32)],
        compiler_params=ROOMY,
        name="pick_rows",
    )(halo_rows, halo_count, node_feat)


def pack_kernel(
    count_ref, values_ref, cols_ref, msg_ref, in_ref, out_w_ref, gain_ref, dst_ref, src_ref, tiles_ref, pack_ref, lines
):
    share, edges = msg_ref.shape[0], values_ref.shape[0]
    tiles_ref[pl.ds(0, edges), :] = values_ref[...]
    tiles_ref[pl.ds(edges, edges), :] = cols_ref[...].astype(F32).astype(BF16)
    pack_ref[pl.ds(0, share), :] = msg_ref[...]
    pack_ref[pl.ds(share, 2 * share), :] = in_ref[...]
    pack_ref[pl.ds(3 * share, share), :] = out_w_ref[...]
    lines[...] = jnp.zeros_like(lines)
    gain = gain_ref[...].astype(F32)
    for j in range(SIDE // share):
        lines[0:1, j * share : (j + 1) * share] = gain
    lines[1:2, :] = dst_ref[...].astype(F32)
    lines[2:3, :] = src_ref[...].astype(F32)
    lines[3:4, :] = jnp.full((1, SIDE), count_ref[0]).astype(F32)
    pack_ref[pl.ds(4 * share, 16), :] = lines[...].astype(BF16)


def pack_shares(tile_count, tile_values, tile_cols, w_msg, w_in, w_out, ln_gain, tile_dst, tile_src):
    share = w_msg.shape[0]
    values, cols = (array.reshape(-1, SIDE) for array in (tile_values, tile_cols))
    return pl.pallas_call(
        pack_kernel,
        out_shape=(
            jax.ShapeDtypeStruct((2 * values.shape[0], SIDE), BF16),
            jax.ShapeDtypeStruct((4 * share + 16, SIDE), BF16),
        ),
        in_specs=[SMEM] + [VMEM] * 8,
        out_specs=(VMEM, VMEM),
        scratch_shapes=[pltpu.VMEM((16, SIDE), F32)],
        compiler_params=ROOMY,
        name="pack_shares",
    )(
        tile_count, values, cols, w_msg, w_in, w_out, ln_gain.reshape(1, share), tile_dst.reshape(1, SIDE),
        tile_src.reshape(1, SIDE),
    )


def prepare_kernel(
    own_blocks, here_blocks, pos_ref, s0_ref, s1_ref, s2_ref, s3_ref, picked_ref,
    low_ref, high_ref, msg_ref, in_ref, out_w_ref, gain_ref, code_ref,
):
    me = pos_ref[0]
    smalls = (s0_ref, s1_ref, s2_ref, s3_ref)
    parties = len(smalls)
    share = SIDE // parties
    lane = lax.broadcasted_iota(jnp.int32, (1, SIDE), 1)
    gain = jnp.zeros((1, SIDE), F32)
    for k, ref in enumerate(smalls):
        device = lax.rem(me + k, parties)
        at = pl.multiple_of(device * share, share)
        msg_ref[pl.ds(at, share), :] = ref[pl.ds(0, share), :]
        in_ref[pl.ds(pl.multiple_of(2 * at, 2 * share), 2 * share), :] = ref[pl.ds(share, 2 * share), :]
        out_w_ref[pl.ds(at, share), :] = ref[pl.ds(3 * share, share), :]
        lines = ref[pl.ds(4 * share, 16), :].astype(F32)
        gain = jnp.where((lane >= at) & (lane < at + share), lines[0:1, :], gain)
        dst, src, count = (lines[i : i + 1, :].astype(jnp.int32) for i in (1, 2, 3))
        block = src - me * here_blocks
        used = (lane < count) & (block >= 0) & (block < here_blocks)
        is_rim = block >= own_blocks
        place = jnp.where(is_rim, block - own_blocks, block)
        code = lane + (place << 7) + (dst << 13) + jnp.where(is_rim, 2 << 20, 1 << 20)
        code_ref[k : k + 1, :] = jnp.where(used, code, 0)
        code_ref[parties + k : parties + k + 1, :] = count
    gain_ref[...] = gain
    half = low_ref.shape[0]
    w_msg = msg_ref[...]
    for k, ref in enumerate((low_ref, high_ref)):
        pre = rows_by_cols(picked_ref[pl.ds(k * half, half), :], w_msg)
        ref[...] = (pre * sigmoid(pre)).astype(BF16)


def prepare(position, smalls, picked, own_blocks, here_blocks):
    half = picked.shape[0] // 2
    return pl.pallas_call(
        functools.partial(prepare_kernel, own_blocks, here_blocks),
        out_shape=(
            jax.ShapeDtypeStruct((half, SIDE), BF16),
            jax.ShapeDtypeStruct((half, SIDE), BF16),
            jax.ShapeDtypeStruct((SIDE, SIDE), BF16),
            jax.ShapeDtypeStruct((2 * SIDE, SIDE), BF16),
            jax.ShapeDtypeStruct((SIDE, SIDE), BF16),
            jax.ShapeDtypeStruct((1, SIDE), F32),
            jax.ShapeDtypeStruct((8, SIDE), jnp.int32),
        ),
        in_specs=[SMEM] + [VMEM] * 5,
        out_specs=(VMEM,) * 7,
        compiler_params=PARAMS,
        name="prepare",
    )(position, *smalls, picked)


def message_kernel(feat_ref, msg_ref, *rest):
    out_ref = rest[-1]
    pre = rows_by_cols(feat_ref[...], msg_ref[...])
    out_ref[...] = (pre * sigmoid(pre)).astype(BF16)


def messages(feat, w_msg, follow):
    rows = feat.shape[0]
    steps = 2
    tall = pl.BlockSpec((rows // steps, SIDE), lambda i: (i, 0))
    return pl.pallas_call(
        message_kernel,
        grid=(steps,),
        out_shape=jax.ShapeDtypeStruct((rows, SIDE), BF16),
        in_specs=[tall, pl.BlockSpec(w_msg.shape, lambda i: (0, 0))] + [ANY] * len(follow),
        out_specs=tall,
        compiler_params=PARAMS,
        name="messages",
    )(feat, w_msg, *follow)


def list_kernel(ks, code_ref, *rest):
    list_ref, total_ref = rest[-2:]
    parties = code_ref.shape[0] // 2
    group = 8
    for k in ks:

        def body(step, carry):
            own, rim = carry
            codes = [code_ref[k, step * group + u] for u in range(group)]
            for code in codes:
                list_ref[2 * k, own] = code
                list_ref[2 * k + 1, rim] = code
                own = own + ((code >> 20) & 1)
                rim = rim + (code >> 21)
            return (own, rim)

        steps = (code_ref[parties + k, 0] + group - 1) // group
        own, rim = lax.fori_loop(0, steps, body, (jnp.int32(0), jnp.int32(0)))
        total_ref[2 * k] = own
        total_ref[2 * k + 1] = rim


def build_lists(ks, codes, follow):
    parties, slots = codes.shape[0] // 2, codes.shape[1]
    return pl.pallas_call(
        functools.partial(list_kernel, ks),
        out_shape=(
            jax.ShapeDtypeStruct((2 * parties, slots + 16), jnp.int32),
            jax.ShapeDtypeStruct((2 * parties,), jnp.int32),
        ),
        in_specs=[SMEM] + [ANY] * len(follow),
        out_specs=(SMEM, SMEM),
        compiler_params=SMALL,
        name="tile_lists",
    )(codes, *follow)


def dense_tile(tiles_ref, slot, keep):
    column = lax.broadcasted_iota(jnp.int32, (SIDE, SIDE), 0).astype(F32)
    edges = tiles_ref.shape[0] // 2
    entries = edges // SIDE
    total = None
    for e in range(entries):
        at = slot * entries + e
        weight = tiles_ref[pl.ds(at, 1), :] * keep
        term = jnp.where(column == tiles_ref[pl.ds(edges + at, 1), :], weight, 0.0)
        total = term if total is None else total + term
    return total.astype(BF16)


def walk_list(list_ref, total_ref, which, tiles_ref, product, acc):
    count = total_ref[which]

    def body(step, carry):
        found = []
        for u in range(UNROLL):
            index = step * UNROLL + u
            used = index < count
            entry = jnp.where(used, list_ref[which, index], 0)
            dense = dense_tile(tiles_ref, entry & 127, jnp.where(used, 1.0, 0.0))
            found.append(product(dense, (entry >> 7) & 63, (entry >> 13) & 31))
        for target, value in found:
            acc[target] += value
        return carry

    lax.fori_loop(0, (count + UNROLL - 1) // UNROLL, body, 0)


def forward_kernel(ks, list_ref, total_ref, own_ref, lower_ref, upper_ref, *rest):
    slot_refs, rest = rest[: len(ks)], rest[len(ks) :]
    outs, (token_ref, acc, rims, tiles) = rest[:-4], rest[-4:]
    token_ref[...] = jnp.zeros_like(token_ref)
    half = lower_ref.shape[0]
    rims[pl.ds(0, half)] = lower_ref[...]
    rims[pl.ds(half, half)] = upper_ref[...]
    for at, (k, slot_ref) in enumerate(zip(ks, slot_refs)):
        acc[...] = jnp.zeros_like(acc)
        tiles[...] = slot_ref[...].astype(F32)
        for part, ref in enumerate((own_ref, rims)):

            def product(dense, block, target, ref=ref):
                return (target, contract_rows(dense, ref[block]))

            walk_list(list_ref, total_ref, 2 * k + part, tiles, product, acc)
        for h in range(2):
            out_ref = outs[2 * at + h]
            span = out_ref.shape[0]
            out_ref[...] = acc[pl.ds(h * span, span)].astype(out_ref.dtype)


def forward_tiles(ks, lists, totals, own, lower, upper, tiles, kind):
    blocks = own.shape[0]
    half = jax.ShapeDtypeStruct((blocks // 2,) + own.shape[1:], kind)
    return pl.pallas_call(
        functools.partial(forward_kernel, ks),
        out_shape=(half,) * (2 * len(ks)) + (jax.ShapeDtypeStruct((8, SIDE), F32),),
        in_specs=[SMEM, SMEM] + [VMEM] * (3 + len(ks)),
        out_specs=(VMEM,) * (2 * len(ks) + 1),
        scratch_shapes=[
            pltpu.VMEM(own.shape, F32),
            pltpu.VMEM((2 * lower.shape[0],) + lower.shape[1:], BF16),
            pltpu.VMEM(tiles[0].shape, F32),
        ],
        compiler_params=PARAMS,
        cost_estimate=cost(1_000_000_000 * len(ks), 4_000_000 * len(ks)),
        name="forward_tiles",
    )(lists, totals, own, lower, upper, *[tiles[k] for k in ks])


def join_kernel(after_ref, left_ref, prior_ref, right_ref, *outs):
    for mine, theirs, out_ref in ((after_ref, left_ref, outs[0]), (prior_ref, right_ref, outs[1])):
        out_ref[...] = (mine[...].astype(F32) + theirs[...].astype(F32)).astype(BF16)


def join(after, from_left, prior, from_right):
    kind = jax.ShapeDtypeStruct(after.shape, BF16)
    return pl.pallas_call(
        join_kernel,
        out_shape=(kind, kind),
        in_specs=[VMEM] * 4,
        out_specs=(VMEM, VMEM),
        compiler_params=PARAMS,
        name="join",
    )(after, from_left, prior, from_right)


def node_kernel(
    continued, feat_ref, cot_ref, own_ref, left_ref, right_ref, in_ref, out_w_ref, gain_ref, *rest,
):
    node_ref, dhid_ref, dagg_ref, dwin_ref, dwout_ref, dgain_ref = rest[-6:]
    step = pl.program_id(0)

    @pl.when(step == 0)
    def _():
        for at, ref in enumerate((dwin_ref, dwout_ref, dgain_ref)):
            ref[...] = rest[2 + at][...] if continued else jnp.zeros_like(ref)

    feat = feat_ref[...]
    agg = (own_ref[...] + (left_ref[...].astype(F32) + right_ref[...].astype(F32))).astype(BF16)
    w_feat, w_agg, w_out = in_ref[:SIDE, :], in_ref[SIDE:, :], out_w_ref[...]
    gain = gain_ref[...]
    pre = rows_by_cols(feat, w_feat) + rows_by_cols(agg, w_agg)
    logistic = sigmoid(pre)
    hidden = (pre * logistic).astype(BF16)
    slope = logistic * (1.0 + pre * (1.0 - logistic))
    update = rows_by_cols(hidden, w_out)
    centre = update - jnp.mean(update, axis=-1, keepdims=True)
    inverse = lax.rsqrt(jnp.mean(centre * centre, axis=-1, keepdims=True) + 1e-05)
    normed = centre * inverse
    node_ref[...] = (feat.astype(F32) + gain * normed).astype(BF16)
    upstream = cot_ref[...].astype(F32)
    d_normed = upstream * gain
    dgain_ref[...] += jnp.sum(upstream * normed, axis=0, keepdims=True)
    d_update = (
        d_normed
        - jnp.mean(d_normed, axis=-1, keepdims=True)
        - normed * jnp.mean(d_normed * normed, axis=-1, keepdims=True)
    ) * inverse
    d_update = d_update.astype(BF16)
    d_hidden = (contract_cols(d_update, w_out) * slope).astype(BF16)
    dhid_ref[...] = d_hidden
    dagg_ref[...] = contract_cols(d_hidden, w_agg).astype(BF16)
    dwout_ref[...] += contract_rows(hidden, d_update)
    dwin_ref[:SIDE, :] += contract_rows(feat, d_hidden)
    dwin_ref[SIDE:, :] += contract_rows(agg, d_hidden)


def node_update(h, node_feat, cotangent, parts, w_in, w_out, gain, before, follow):
    rows = node_feat.shape[0]
    chunk = 512
    steps = rows // 2 // chunk

    def whole(shape):
        return pl.BlockSpec(shape, lambda i: (0, 0))

    tall = pl.BlockSpec((chunk, SIDE), lambda i: (h * steps + i, 0))
    part = pl.BlockSpec((chunk, SIDE), lambda i: (i, 0))
    wide = jax.ShapeDtypeStruct((rows, SIDE), BF16)
    half = jax.ShapeDtypeStruct((rows // 2, SIDE), BF16)
    sums = [(2 * SIDE, SIDE), (SIDE, SIDE), (1, SIDE)]
    return pl.pallas_call(
        functools.partial(node_kernel, bool(before)),
        grid=(steps,),
        out_shape=(wide, wide, half) + tuple(jax.ShapeDtypeStruct(shape, F32) for shape in sums),
        in_specs=[tall, tall, part, part, part]
        + [whole((2 * SIDE, SIDE)), whole((SIDE, SIDE)), whole((1, SIDE))]
        + ([ANY, ANY] + [whole(shape) for shape in sums] if before else [])
        + [ANY] * len(follow),
        out_specs=(tall, tall, part) + tuple(whole(shape) for shape in sums),
        input_output_aliases={8: 0, 9: 1} if before else {},
        compiler_params=PARAMS,
        cost_estimate=cost(5_000_000_000, 10_000_000),
        name="node_update",
    )(node_feat, cotangent, *parts, w_in, w_out, gain, *before, *follow)


def ahead_kernel(feat_ref, cot_ref, dhid_ref, picked_ref, msg_ref, in_ref, slope_ref, base_ref, far_ref):
    w_msg = msg_ref[...]
    slope_ref[...] = silu_slope(rows_by_cols(feat_ref[...], w_msg))
    far_ref[...] = silu_slope(rows_by_cols(picked_ref[...], w_msg))
    base_ref[...] = cot_ref[...].astype(F32) + contract_cols(dhid_ref[...], in_ref[:SIDE, :])


def ahead(feat, cot, dhid, picked, w_msg, w_in):
    rows = feat.shape[0]
    steps = 4
    tall = pl.BlockSpec((rows // steps, SIDE), lambda i: (i, 0))
    short = pl.BlockSpec((picked.shape[0] // steps, SIDE), lambda i: (i, 0))
    wide = jax.ShapeDtypeStruct((rows, SIDE), F32)
    return pl.pallas_call(
        ahead_kernel,
        grid=(steps,),
        out_shape=(wide, wide, jax.ShapeDtypeStruct(picked.shape, F32)),
        in_specs=[tall] * 3 + [short] + [pl.BlockSpec(w.shape, lambda i: (0, 0)) for w in (w_msg, w_in)],
        out_specs=(tall, tall, short),
        compiler_params=PARAMS,
        cost_estimate=cost(3_000_000_000, 7_000_000),
        name="ahead",
    )(feat, cot, dhid, picked, w_msg, w_in)


def backward_kernel(ks, cuts, parts, started, list_ref, total_ref, *rest):
    slot_refs, rest = rest[: len(ks)], rest[len(ks) :]
    tiles, grads, accs = rest[-2 - len(parts)], rest[-1 - len(parts)], rest[-len(parts) :]
    arrays, rest = rest[: cuts * len(ks)], rest[cuts * len(ks) : -2 - len(parts)]
    for at, acc in enumerate(accs):
        acc[...] = rest[at][...] if started else jnp.zeros_like(acc)
    for at, (k, slot_ref) in enumerate(zip(ks, slot_refs)):
        tiles[...] = slot_ref[...].astype(F32)
        source = arrays[at]
        if cuts > 1:
            source, span = grads, grads.shape[0] // cuts
            for c in range(cuts):
                grads[pl.ds(c * span, span)] = arrays[cuts * at + c][...]

        def product(dense, block, target, source=source):
            return (block, rows_by_cols(dense, source[target]))

        for part, acc in zip(parts, accs):
            walk_list(list_ref, total_ref, 2 * k + part, tiles, product, acc)
    if parts == (1,):
        half = accs[0].shape[0] // 2
        for at, out_ref in enumerate(rest[-2:]):
            out_ref[...] = accs[0][pl.ds(at * half, half)].astype(out_ref.dtype)
    else:
        for out_ref, acc in zip(rest[-len(parts) :], accs):
            out_ref[...] = acc[...]


def backward_tiles(ks, lists, parts, sizes, kinds, tiles, arrays, started, follow=()):
    cuts = len(arrays[0])
    cubes = [array.reshape(-1, SIDE, SIDE) for group in arrays for array in group]
    accs = [sum(sizes)] if len(sizes) > len(parts) else sizes
    return pl.pallas_call(
        functools.partial(backward_kernel, ks, cuts, parts, bool(started)),
        out_shape=tuple(jax.ShapeDtypeStruct((size, SIDE, SIDE), kind) for size, kind in zip(sizes, kinds)),
        in_specs=[SMEM, SMEM] + [VMEM] * (len(ks) + len(cubes) + len(started)) + [ANY] * len(follow),
        out_specs=(VMEM,) * len(sizes),
        scratch_shapes=[pltpu.VMEM(tiles[0].shape, F32), pltpu.VMEM((cuts * cubes[0].shape[0], SIDE, SIDE), BF16)]
        + [pltpu.VMEM((size, SIDE, SIDE), F32) for size in accs],
        compiler_params=PARAMS,
        cost_estimate=cost(2_000_000_000 * len(ks), 4_000_000),
        name="backward_tiles",
    )(*lists, *[tiles[k] for k in ks], *cubes, *started, *follow)


def own_kernel(feat_ref, slope_ref, base_ref, own_ref, msg_ref, sum_ref, dw_ref):
    @pl.when(pl.program_id(0) == 0)
    def _():
        dw_ref[...] = jnp.zeros_like(dw_ref)

    d_pre = (own_ref[...] * slope_ref[...]).astype(BF16)
    dw_ref[...] += contract_rows(feat_ref[...], d_pre)
    sum_ref[...] = base_ref[...] + contract_cols(d_pre, msg_ref[...])


def own_products(feat, slope, base, own, w_msg):
    rows = feat.shape[0]
    steps = 4
    tall = pl.BlockSpec((rows // steps, SIDE), lambda i: (i, 0))
    square = pl.BlockSpec((SIDE, SIDE), lambda i: (0, 0))
    return pl.pallas_call(
        own_kernel,
        grid=(steps,),
        out_shape=(jax.ShapeDtypeStruct((rows, SIDE), F32), jax.ShapeDtypeStruct((SIDE, SIDE), F32)),
        in_specs=[tall] * 4 + [square],
        out_specs=(tall, square),
        compiler_params=PARAMS,
        cost_estimate=cost(3_000_000_000, 7_000_000),
        name="own_products",
    )(feat, slope, base, own, w_msg)


def rim_kernel(
    pos_ref, count_ref, lower_ref, upper_ref, picked_ref, far_ref, dw_ref, dwin_ref, dwout_ref, dgain_ref,
    dpre_ref, r0_ref, r1_ref, r2_ref, r3_ref, dw,
):
    halo = lower_ref.shape[0]
    dw[...] = dw_ref[...]
    for k, ref in enumerate((lower_ref, upper_ref)):
        at = pl.ds(k * halo, halo)
        slots = lax.broadcasted_iota(jnp.int32, (halo, SIDE), 0)
        d_pre = jnp.where(slots < count_ref[k], ref[...].astype(F32) * far_ref[at, :], 0.0).astype(BF16)
        dpre_ref[at, :] = d_pre
        dw[...] += contract_rows(picked_ref[at, :], d_pre)
    outs = (r0_ref, r1_ref, r2_ref, r3_ref)
    share = SIDE // len(outs)
    for k, out in enumerate(outs):
        device = lax.rem(pos_ref[0] + k, len(outs))
        start = pl.multiple_of(device * share, share)
        gain = jnp.zeros((16, SIDE), F32)
        for j in range(len(outs)):
            wide = jnp.broadcast_to(dgain_ref[...], (16, SIDE))
            gain = jnp.where(device == j, pltpu.roll(wide, (SIDE - j * share) % SIDE, 1), gain)
        out[pl.ds(0, share), :] = dw[pl.ds(start, share), :].astype(out.dtype)
        at = pl.ds(pl.multiple_of(2 * start, 2 * share), 2 * share)
        out[pl.ds(share, 2 * share), :] = dwin_ref[at, :].astype(out.dtype)
        out[pl.ds(3 * share, share), :] = dwout_ref[pl.ds(start, share), :].astype(out.dtype)
        out[pl.ds(4 * share, 16), :] = gain.astype(out.dtype)


def rim_products(position, halo_count, lower, upper, picked, far, dw, sums):
    piece = jax.ShapeDtypeStruct((SIDE + 16, SIDE), BF16)
    return pl.pallas_call(
        rim_kernel,
        out_shape=(jax.ShapeDtypeStruct(picked.shape, BF16), piece, piece, piece, piece),
        in_specs=[SMEM] * 2 + [VMEM] * 8,
        out_specs=(VMEM,) * 5,
        scratch_shapes=[pltpu.VMEM((SIDE, SIDE), F32)],
        compiler_params=PARAMS,
        name="rim_products",
    )(position, halo_count, lower, upper, picked, far, dw, *sums)


def place_kernel(k, rows_ref, count_ref, sum_ref, dpre_ref, msg_ref, *rest):
    out_ref, token_ref, acc, added = rest[-4:]
    token_ref[...] = jnp.zeros_like(token_ref)
    halo = rows_ref.shape[1]
    acc[...] = sum_ref[...]
    added[...] = contract_cols(dpre_ref[pl.ds(k * halo, halo), :], msg_ref[...])
    group = 32

    def body(step, carry):
        rows = [rows_ref[k, step * group + u] for u in range(group)]
        values = [acc[pl.ds(row, 1), :] + added[pl.ds(step * group + u, 1), :] for u, row in enumerate(rows)]
        for row, value in zip(rows, values):
            acc[pl.ds(row, 1), :] = value
        return carry

    lax.fori_loop(0, (count_ref[k] + group - 1) // group, body, 0)
    out_ref[...] = acc[...].astype(out_ref.dtype)


def place_rows(k, kind, halo_rows, halo_count, total, d_pre, w_msg, follow):
    return pl.pallas_call(
        functools.partial(place_kernel, k),
        out_shape=(jax.ShapeDtypeStruct(total.shape, kind), jax.ShapeDtypeStruct((8, SIDE), F32)),
        in_specs=[SMEM] * 2 + [VMEM] * 3 + [ANY] * len(follow),
        out_specs=(VMEM, VMEM),
        scratch_shapes=[pltpu.VMEM(total.shape, F32), pltpu.VMEM((halo_rows.shape[1], SIDE), F32)],
        compiler_params=PARAMS,
        cost_estimate=cost(4_000_000_000, 7_000_000),
        name="place_rows",
    )(halo_rows, halo_count, total, d_pre, w_msg, *follow)


def shift_wsh(value, step):
    parties = lax.axis_size("wsh")
    return lax.ppermute(value, "wsh", [(i, (i + step) % parties) for i in range(parties)])


def shift_slab(value, step):
    count = lax.axis_size("slab")
    pairs = [(i, i + step) for i in range(count) if 0 <= i + step < count]
    return lax.ppermute(value, "slab", pairs)


def sum_kernel(count, *refs):
    total = refs[0][...].astype(F32)
    for ref in refs[1:count]:
        total = total + ref[...].astype(F32)
    refs[-1][...] = total.astype(BF16)


def sum_group(terms, follow=()):
    return pl.pallas_call(
        functools.partial(sum_kernel, len(terms)),
        out_shape=jax.ShapeDtypeStruct(terms[0].shape, BF16),
        in_specs=[VMEM] * len(terms) + [ANY] * len(follow),
        out_specs=VMEM,
        compiler_params=SMALL,
        name="sum_group",
    )(*terms, *follow)


def sum_wsh(pieces, follow):
    return sum_group([pieces[0]] + [shift_wsh(pieces[k], k) for k in range(1, len(pieces))], follow)


def sum_slab(value, stride, size, follow=()):
    count = lax.axis_size("slab")
    span = stride * size
    turns = [[(i, (i // span) * span + (i + stride * k) % span) for i in range(count)] for k in range(1, size)]
    return sum_group([value] + [lax.ppermute(value, "slab", pairs) for pairs in turns], follow)


def other_core(value):
    return lax.ppermute(value, "slab", [(i, i ^ 1) for i in range(lax.axis_size("slab"))])


def finish_kernel(one_ref, two_ref, msg_ref, in_ref, out_w_ref, gain_ref):
    share = msg_ref.shape[0]
    total = one_ref[...].astype(F32) + two_ref[...].astype(F32)
    msg_ref[...] = total[:share]
    in_ref[...] = total[share : 3 * share]
    out_w_ref[...] = total[3 * share : 4 * share]
    gain_ref[...] = total[4 * share : 4 * share + 1, :share]


def finish(one, two):
    share = SIDE // 4
    shapes = [(share, SIDE), (2 * share, SIDE), (share, SIDE), (1, share)]
    return pl.pallas_call(
        finish_kernel,
        out_shape=tuple(jax.ShapeDtypeStruct(shape, F32) for shape in shapes),
        in_specs=[VMEM, VMEM],
        out_specs=(VMEM,) * 4,
        compiler_params=SMALL,
        name="finish",
    )(one, two)


def on_device(
    node_feat, cotangent, w_msg, w_in, w_out, ln_gain,
    tile_values, tile_cols, tile_dst, tile_src, tile_count, halo_rows, halo_count,
):
    node_rows = node_feat.shape[0]
    slots, entries, side = tile_values.shape
    halo = halo_rows.shape[2]
    parties = lax.axis_size("wsh")
    me = lax.axis_index("wsh").astype(jnp.int32)
    position = me.reshape(1)
    share = w_msg.shape[0]
    own_blocks = node_rows // side
    rim_blocks = 2 * halo // side

    tile, small = pack_shares(tile_count, tile_values, tile_cols, w_msg, w_in, w_out, ln_gain, tile_dst, tile_src)
    smalls = [small] + [shift_wsh(small, -k) for k in range(1, parties)]
    tiles = [tile] + [shift_wsh(tile, -k) for k in range(1, parties)]

    rows = halo_rows.reshape(2, halo)
    counts = halo_count.reshape(2)
    picked = pick_rows(rows, counts, node_feat)
    low, high, full_msg, full_in, full_out, gain, codes = prepare(
        position, smalls, picked, own_blocks, own_blocks + rim_blocks
    )
    lower = shift_slab(high, 1).reshape(rim_blocks // 2, side, side)
    upper = shift_slab(low, -1).reshape(rim_blocks // 2, side, side)
    message = messages(node_feat, full_msg, tiles[1:])
    far_lists = build_lists((2,), codes, ())
    forward = functools.partial(
        forward_tiles, own=message.reshape(own_blocks, side, side), lower=lower,
        upper=upper, tiles=tiles,
    )

    far_first, far_second, token = forward((2,), *far_lists, kind=BF16)
    lists = build_lists((0, 1, 3), codes, (token,))
    from_right = shift_wsh(far_first, -1)
    from_left = shift_wsh(far_second, 1)
    after_first, after_second, prior_first, prior_second, _ = forward((1, 3), *lists, kind=BF16)
    left_first = shift_wsh(after_first, 1)
    right_second = shift_wsh(prior_second, -1)
    mine_first, mine_second, _ = forward((0,), *lists, kind=F32)
    to_after, to_prior = join(after_second, from_left, prior_first, from_right)
    left_second = shift_wsh(to_after, 1)
    right_first = shift_wsh(to_prior, -1)
    parts = ((mine_first, left_first, right_first), (mine_second, left_second, right_second))
    before, d_agg, from_prior, from_after = (), [], [], []
    for h in (0, 1):
        pieces = [part.reshape(-1, side) for part in parts[h]]
        node_out, d_hidden, half, *sums = node_update(
            h, node_feat, cotangent, pieces, full_in, full_out, gain, before, from_prior
        )
        before = (node_out, d_hidden, *sums)
        d_agg.append(half)
        from_prior.append(shift_wsh(half, 1))
        from_after.append(shift_wsh(half, -1))
    quarter = node_rows // 4
    far = []
    for h in (0, 1):
        far.append(shift_wsh(from_prior[h][:quarter], 1))
        far.append(shift_wsh(from_after[h][quarter:], -1))
    slope, base, far_slope = ahead(node_feat, cotangent, d_hidden, picked, full_msg, full_in)

    backward = functools.partial(backward_tiles, tiles=tiles)
    own_part, rim_part = backward(
        (0, 1, 3), lists, (0, 1), (own_blocks, rim_blocks), (F32, F32), arrays=(d_agg, from_after, from_prior),
        started=(),
    )
    back_low, back_high = backward(
        (2,), far_lists, (1,), (rim_blocks // 2,) * 2, (BF16,) * 2, arrays=(far,), started=(rim_part,), follow=(slope,)
    )
    back_upper = shift_slab(back_low.reshape(halo, side), -1)
    back_lower = shift_slab(back_high.reshape(halo, side), 1)
    (d_own,) = backward((2,), far_lists, (0,), (own_blocks,), (F32,), arrays=(far,), started=(own_part,))
    total, d_w_own = own_products(node_feat, slope, base, d_own.reshape(node_rows, side), full_msg)
    d_pre, *pieces = rim_products(
        position, counts, back_lower, back_upper, picked, far_slope, d_w_own, sums
    )
    place = functools.partial(place_rows, halo_rows=rows, halo_count=counts, d_pre=d_pre, w_msg=full_msg)
    total, token = place(0, F32, total=total, follow=())
    value = sum_wsh(pieces, (token,))
    d_node, token = place(1, BF16, total=total, follow=(value,))
    value = sum_slab(value, 8, 4, (token,))
    value = sum_slab(value, 2, 4)
    d_w_msg, d_w_in, d_w_out, d_gain = finish(value, other_core(value))
    return (node_out, d_node, d_w_msg, d_w_in, d_w_out, d_gain.reshape(share))


def solution(mesh):
    both = ("slab", "wsh")
    tall, split, line = P(both, None), P("wsh", None), P(both)
    cube = P(both, None, None)
    return jax.shard_map(
        on_device,
        mesh=mesh,
        in_specs=(
            tall, tall, split, split, split, P("wsh"), cube, cube, line, line, line, cube, tall,
        ),
        out_specs=(tall, tall, split, split, split, P("wsh")),
        check_vma=False,
    )
```
